32 devices in a mesh: rows: 8 (over z, y), head: 4 (over x, core).
Axes of the slice: x: 2, y: 2, z: 4, core: 2. Of those that a mesh axis runs over, the one named last changes fastest.
Arguments:
- tokens: bfloat16 [2, 4096, 512], P(None, 'rows'), may hold values from -6 to 6
- cotangent: bfloat16 [2, 4096, 512], P(None, 'rows'), may hold values from -6 to 6
- dataset_ids: int32 [2, 4096], P(None, 'rows'), may hold values from 0 to 15, never falling along the last dimension, each value on 1 to 2048 neighbouring positions
- prompt_map: int32 [2, 16], replicated, may hold values from 0 to 7
- attn_in: bfloat16 [3, 512, 512], P(None, None, 'head'), may hold values from -0.25 to 0.25
- attn_out: bfloat16 [512, 512], P('head'), may hold values from -6 to 6
- up_weight: bfloat16 [512, 1024], P(None, 'head'), may hold values from -0.25 to 0.25
- up_bias: float32 [1024], P('head'), may hold values from -4 to 4
- down_weight: bfloat16 [1024, 512], P('head'), may hold values from -0.1875 to 0.1875
- down_bias: float32 [512], replicated, may hold values from -4 to 4
- norm_gains: float32 [2, 512], replicated, may hold values from 0.5 to 1.5
- norm_shifts: float32 [2, 512], replicated, may hold values from -4 to 4
- prompts: float32 [8000, 512], P('rows'), may hold values from -6 to 6
- moment_one: float32 [8000, 512], P('rows'), may hold values from -0.0008544922 to 0.0008544922
- moment_two: float32 [8000, 512], P('rows'), may hold values from 1.2207031e-10 to 1.953125e-09
- step_count: int32 [], replicated, may hold values from 1 to 20
Outputs:
- layer_out: float32 [2, 4096, 512], P(None, 'rows')
- input_grad: float32 [2, 4096, 512], P(None, 'rows')
- clipped_grad: float32 [8000, 512], P('rows')
- grad_norm: float32 [], replicated
- new_moment_one: float32 [8000, 512], P('rows')
- new_moment_two: float32 [8000, 512], P('rows')
- new_prompts: float32 [8000, 512], P('rows')
The draws below stay inside these ranges and needn't reach their ends.
Inputs may be any that keep to these rules, and one draw needn't show every extreme that they name: `dataset_ids`: within a micro-batch dataset numbers never fall along the tokens; each dataset holds 1 to 2048 tokens, one exactly 2048.
All inputs are finite; a program needn't handle non-finite values.
Results may differ from the reference program's by a relative error of at most 0.023.
Values may be sent and summed in bfloat16 or wider, within the bound.
No kernel may reach another device: no remote copies, remote signals or barrier semaphores. Data moves between devices by JAX's collectives and lax.ppermute only.
A program may use at most 320 MiB of HBM per device.

```python
import math
import jax
import jax.numpy as jnp
import numpy as np
from jax import lax

D = 512
HEADS = 4
HEAD_DIM = 128
FF = 1024
PLEN = 1000
NPROMPT = 8
NDATA = 16
MICRO = 2
TOKENS = 4096
MOSTLEN = 2048


def draw_cotangent(key, part):
    shape = (MICRO, TOKENS, D)
    values = jax.random.truncated_normal(key, -6.0, 6.0, shape, jnp.float32)
    return values.astype(jnp.bfloat16)


def set_ends(result, key, smallest, largest):
    longest = result.shape.index(max(result.shape))
    spots = []
    for shift in (0, 1):
        where = [jax.random.randint(jax.random.fold_in(key, axis), (), 0, length) for axis, length in enumerate(result.shape)]
        where[longest] = (where[longest] + shift) % result.shape[longest]
        spots.append(tuple(where))
    return result.at[spots[0]].set(smallest).at[spots[1]].set(largest)


def block_levels(own_key, shape, split, least, top_value):
    def one(dim, parts):
        draws = jax.random.uniform(jax.random.fold_in(jax.random.fold_in(own_key, 6), dim), (parts,), jnp.float32, least / len(split), top_value / len(split))
        return jnp.repeat(jnp.exp(draws), shape[dim] // parts).reshape((-1,) + (1,) * (len(shape) - dim - 1))

    level = one(*split[0])
    for cut in split[1:]:
        level = level * one(*cut)
    return level


def profile(count, total, most, slope):
    portions = [(1 << 20) // math.isqrt(rank ** slope) + 1 for rank in range(2, count + 1)]
    spare, holding = total - most - (count - 1), [1] * (count - 1)
    while spare > 0:
        candidates = [i for i in range(count - 1) if holding[i] < most]
        mass, budget = sum([portions[i] for i in candidates]), spare
        for i in candidates:
            extra = min(most - holding[i], max(1, budget * portions[i] // mass), spare)
            holding[i] = holding[i] + extra
            spare = spare - extra
    return np.array([most] + holding)


def uneven_parts(own_key, number_of, total, most, lean):
    if number_of == 2:
        one = jax.random.randint(own_key, (), max(1, total - most), min(most, total - 1) + 1)
        return jnp.stack([one, total - one])
    sizes = jnp.asarray(profile(number_of, total, most, lean), jnp.int32)
    couples = (number_of - 1) // 2
    source_of, receiver = sizes[1:1 + 2 * couples:2], sizes[2:2 + 2 * couples:2]
    margin = jnp.minimum(source_of - 1, most - receiver)
    moved = jax.random.randint(jax.random.fold_in(own_key, 1), (couples,), 0, 1 << 20) % (margin + 1)
    sizes = sizes.at[1:1 + 2 * couples:2].set(source_of - moved).at[2:2 + 2 * couples:2].set(receiver + moved)
    return sizes[jax.random.permutation(jax.random.fold_in(own_key, 2), number_of)]


def scatter_about(own_key, shape, scale, limit, shards=(), kind=jnp.bfloat16):
    drawn = scale * jax.random.normal(own_key, shape, jnp.float32)
    if shards:
        drawn = drawn * block_levels(own_key, shape, shards, -0.22, 0.18)
    return jnp.clip(drawn, -limit, limit).astype(kind)


def setup_inputs(seed: int = 0) -> dict:
    splits = jax.random.split(jax.random.key(seed), 17)
    return {
        "tokens": scatter_about(splits[0], (MICRO, TOKENS, D), 1.0, 6.0, ((1, 8),)),
        "cotangent": draw_cotangent(jax.random.fold_in(splits[16], 71), 0),
        "dataset_ids": jax.vmap(lambda own: jnp.searchsorted(jnp.cumsum(uneven_parts(own, NDATA, TOKENS, MOSTLEN, 2)), jnp.arange(TOKENS), side="right"))(jax.random.split(splits[2], MICRO)).reshape((MICRO, TOKENS)).astype(jnp.int32),
        "prompt_map": set_ends(jax.random.randint(splits[3], (MICRO, NDATA), 0, NPROMPT), jax.random.fold_in(splits[3], 1), 0, NPROMPT - 1).astype(jnp.int32),
        "attn_in": scatter_about(splits[4], (3, D, D), D ** -0.5, 0.25, ((2, 4),)),
        "attn_out": scatter_about(splits[5], (D, D), ((2 * PLEN) ** 0.5 * D ** -0.5), 6.0, ((0, 4),)),
        "up_weight": scatter_about(splits[6], (D, FF), D ** -0.5, 0.25, ((1, 4),)),
        "up_bias": scatter_about(splits[7], (FF,), 0.3, 4.0, ((0, 4),), jnp.float32),
        "down_weight": scatter_about(splits[8], (FF, D), FF ** -0.5, 0.1875, ((0, 4),)),
        "down_bias": scatter_about(splits[9], (D,), 0.3, 4.0, (), jnp.float32),
        "norm_gains": jnp.clip(1.0 + 0.1 * jax.random.normal(splits[10], (2, D), jnp.float32), 0.5, 1.5),
        "norm_shifts": scatter_about(splits[11], (2, D), 0.3, 4.0, (), jnp.float32),
        "prompts": scatter_about(splits[12], (NPROMPT * PLEN, D), 1.0, 6.0, ((0, 8),), jnp.float32),
        "moment_one": scatter_about(splits[13], (NPROMPT * PLEN, D), (0.111 * (NPROMPT * PLEN * D) ** -0.5), 0.0008544922, ((0, 8),), jnp.float32),
        "moment_two": jnp.clip(jnp.exp(math.log(1.9531249950688334e-09) - 2.7725887 * jax.random.uniform(splits[14], (NPROMPT * PLEN, D), jnp.float32) ** block_levels(splits[14], (NPROMPT * PLEN, D), ((0, 8),), -0.2, 0.2)), 1.220703121918021e-10, 1.9531249950688334e-09),
        "step_count": jax.random.randint(splits[15], (), 1, 21).astype(jnp.int32),
    }


HIGHEST = lax.Precision.HIGHEST
NEGATIVE = -1e+30
BETA_ONE = 0.9
BETA_TWO = 0.999
LEARNING_RATE = 0.5
DECAY_RATE = 0.01
EPSILON = 1e-08
CLIP_NORM = 1.0

@jax.custom_vjp
def low(v):
    return lax.optimization_barrier(v.astype(jnp.bfloat16)).astype(jnp.float32)

@jax.custom_vjp
def low_back(v):
    return v

def low_keep(v):
    return (low(v), None)

def low_pass(kept, grad):
    return (grad,)

def back_keep(v):
    return (v, None)

def back_low(kept, grad):
    return (low(grad),)
low.defvjp(low_keep, low_pass)
low_back.defvjp(back_keep, back_low)

def rounded(value):
    return low(low_back(value))

def norm_rows(value, gain, shift):
    center = value - lax.optimization_barrier(jnp.mean(value, axis=-1, keepdims=True))
    spread = lax.optimization_barrier(jnp.mean(center * center, axis=-1, keepdims=True))
    return center * lax.rsqrt(spread + 1e-05) * gain + shift

def reference(tokens, cotangent, dataset_ids, prompt_map, attn_in, attn_out, up_weight, up_bias, down_weight, down_bias, norm_gains, norm_shifts, prompts, moment_one, moment_two, step_count):
    weights_in = attn_in.astype(jnp.float32)
    weight_out = attn_out.astype(jnp.float32)
    weight_up = up_weight.astype(jnp.float32)
    weight_down = down_weight.astype(jnp.float32)
    key_prompt = jnp.arange(NPROMPT * PLEN, dtype=jnp.int32) // PLEN
    query_block = math.gcd(TOKENS, 512)
    block_count = TOKENS // query_block
    score_scale = HEAD_DIM ** (-0.5)

    def layer(inputs, prompt_weights):
        prompt_proj = rounded(jnp.einsum('pd,cde->cpe', low(prompt_weights), weights_in[1:], precision=HIGHEST))
        prompt_keys = prompt_proj[0].reshape(NPROMPT * PLEN, HEADS, HEAD_DIM)
        prompt_vals = prompt_proj[1].reshape(NPROMPT * PLEN, HEADS, HEAD_DIM)
        results = []
        for micro_index in range(MICRO):
            rows_in = inputs[micro_index]
            tok_ids = dataset_ids[micro_index]
            query_prompt = prompt_map[micro_index][tok_ids]
            projected = rounded(jnp.einsum('td,cde->cte', rows_in, weights_in, precision=HIGHEST))
            projected = projected.reshape(3, TOKENS, HEADS, HEAD_DIM)
            queries, keys, values = (projected[0], projected[1], projected[2])

            def attend(block):
                query_rows, query_ids, query_prompts = block
                token_scores = low_back(jnp.einsum('qhe,khe->hqk', query_rows, keys, precision=HIGHEST) * score_scale)
                prompt_scores = low_back(jnp.einsum('qhe,khe->hqk', query_rows, prompt_keys, precision=HIGHEST) * score_scale)
                token_scores = jnp.where((query_ids[:, None] == tok_ids[None, :])[None], token_scores, NEGATIVE)
                prompt_scores = jnp.where((query_prompts[:, None] == key_prompt[None, :])[None], prompt_scores, NEGATIVE)
                log_total = jax.nn.logsumexp(jnp.concatenate([token_scores, prompt_scores], axis=-1), axis=-1, keepdims=True)
                token_probs = low(jnp.exp(token_scores - log_total))
                prompt_probs = low(jnp.exp(prompt_scores - log_total))
                mixed = jnp.einsum('hqk,khe->qhe', token_probs, values, precision=HIGHEST)
                mixed = mixed + jnp.einsum('hqk,khe->qhe', prompt_probs, prompt_vals, precision=HIGHEST)
                return rounded(mixed.reshape(query_block, HEADS * HEAD_DIM))
            attended = lax.map(jax.checkpoint(attend), (queries.reshape(block_count, query_block, HEADS, HEAD_DIM), tok_ids.reshape(block_count, query_block), query_prompt.reshape(block_count, query_block)))
            attended = attended.reshape(TOKENS, D)
            attn = low_back(jnp.dot(attended, weight_out, precision=HIGHEST))
            normed = norm_rows(rows_in + attn, norm_gains[0], norm_shifts[0])
            hidden_pre = low_back(jnp.dot(low(normed), weight_up, precision=HIGHEST) + up_bias)
            hidden = low(jax.nn.gelu(hidden_pre, approximate=False))
            branch = low_back(jnp.dot(hidden, weight_down, precision=HIGHEST) + down_bias)
            results.append(norm_rows(normed + branch, norm_gains[1], norm_shifts[1]))
        return jnp.stack(results)
    outputs, pullback = jax.vjp(layer, tokens.astype(jnp.float32), prompts)
    input_grad, prompt_grad = pullback(cotangent.astype(jnp.float32))
    grad_norm = jnp.sqrt(jnp.sum(prompt_grad * prompt_grad))
    factor = jnp.minimum(1.0, CLIP_NORM / (grad_norm + 1e-06))
    clipped = prompt_grad * factor
    step_value = step_count.astype(jnp.float32)
    new_one = BETA_ONE * moment_one + (1.0 - BETA_ONE) * clipped
    new_two = BETA_TWO * moment_two + (1.0 - BETA_TWO) * clipped * clipped
    first_hat = new_one / (1.0 - jnp.power(BETA_ONE, step_value))
    second_hat = new_two / (1.0 - jnp.power(BETA_TWO, step_value))
    new_prompts = prompts * (1.0 - LEARNING_RATE * DECAY_RATE) - LEARNING_RATE * first_hat / (jnp.sqrt(second_hat) + EPSILON)
    return (outputs, input_grad, clipped, grad_norm, new_one, new_two, new_prompts)
```

```python
import functools

import jax
import jax.numpy as jnp
from jax import lax
from jax.experimental import pallas as pl
from jax.experimental.pallas import tpu as pltpu
from jax.sharding import PartitionSpec as P

PLEN = 1000
NEGATIVE = -1e30
BETA_ONE = 0.9
BETA_TWO = 0.999
LEARNING_RATE = 0.5
DECAY_RATE = 0.01
EPSILON = 1e-08
CLIP_NORM = 1.0
LOG2E = 1.4426950408889634
PACK = 16
STATS = 32
VMEM_LIMIT = 60 * 1024 * 1024
BF = jnp.bfloat16
F32 = jnp.float32
BOTH = ("rows", "head")


def params():
    return pltpu.CompilerParams(vmem_limit_bytes=VMEM_LIMIT)


def cost(flops, bytes_accessed, transcendentals=0):
    return pl.CostEstimate(
        flops=int(flops), bytes_accessed=int(bytes_accessed), transcendentals=int(transcendentals)
    )


def mm(a, b):
    return lax.dot_general(a, b, (((1,), (0,)), ((), ())), preferred_element_type=F32)


def mm_nt(a, b):
    return lax.dot_general(a, b, (((1,), (1,)), ((), ())), preferred_element_type=F32)


def split3(value):
    high = value.astype(BF)
    rest = value - high.astype(F32)
    mid = rest.astype(BF)
    low = (rest - mid.astype(F32)).astype(BF)
    return high, mid, low


def bit_orders(row_count):
    bits = row_count.bit_length() - 1
    return ([0] + list(range(bits - 1, 0, -1)), list(range(bits - 1, 0, -1)) + [0])


def slot_of(offset, parity, row_count):
    order_even, order_odd = bit_orders(row_count)

    def mapped(order):
        total = 0
        for place, bit in enumerate(order):
            total = total + (((offset >> bit) & 1) << place)
        return total

    return jnp.where(parity == 0, mapped(order_even), mapped(order_odd))


def gather_rows(block, row_count, head_count):
    order_even, order_odd = bit_orders(row_count)
    held = block[None]
    for even_bit, odd_bit in zip(order_even, order_odd):
        pairs = []
        for row in range(row_count):
            for head in range(head_count):
                bit = even_bit if head % 2 == 0 else odd_bit
                pairs.append((row * head_count + head, (row ^ (1 << bit)) * head_count + head))
        held = jnp.concatenate([held, lax.ppermute(held, BOTH, pairs)], axis=0)
    return held


def swap_head(value, mask, head_count):
    return lax.ppermute(value, "head", [(i, i ^ mask) for i in range(head_count)])


def project_kernel(meta, mine, theirs, weights, q_out, kv_out, ids_out):
    half = mine.shape[1] - PACK
    head_width = q_out.shape[1]
    parity = meta[2]
    w = weights[...]
    for part, ref in ((parity, mine), (1 - parity, theirs)):
        rows = pl.ds(pl.multiple_of(part * half, half), half)
        result = mm(ref[0, :half], w).astype(BF)
        q_out[rows, :] = result[:, :head_width]
        kv_out[rows, :] = result[:, head_width:]
    ids_out[0] = mine[0, half : half + 1].astype(F32)


def project_tokens(meta, mine, theirs, weights, row_count):
    half = mine.shape[1] - PACK
    width = mine.shape[2]
    total = row_count * 2 * half
    third = weights.shape[1] // 3

    def slot_mine(g, meta):
        return (slot_of(g ^ meta[0], meta[2], row_count), 0, 0)

    def slot_theirs(g, meta):
        return (slot_of(g ^ meta[0], 1 - meta[2], row_count), 0, 0)

    return pl.pallas_call(
        project_kernel,
        out_shape=(
            jax.ShapeDtypeStruct((total, third), BF),
            jax.ShapeDtypeStruct((total, 2 * third), BF),
            jax.ShapeDtypeStruct((row_count, 1, width), F32),
        ),
        grid_spec=pltpu.PrefetchScalarGridSpec(
            num_scalar_prefetch=1,
            grid=(row_count,),
            in_specs=[
                pl.BlockSpec((1, half + PACK, width), slot_mine),
                pl.BlockSpec((1, half + PACK, width), slot_theirs),
                pl.BlockSpec(weights.shape, lambda g, meta: (0, 0)),
            ],
            out_specs=[
                pl.BlockSpec((2 * half, third), lambda g, meta: (g, 0)),
                pl.BlockSpec((2 * half, 2 * third), lambda g, meta: (g, 0)),
                pl.BlockSpec((1, 1, width), lambda g, meta: (g, 0, 0)),
            ],
        ),
        compiler_params=params(),
        cost_estimate=cost(2 * total * width * 3 * third, total * 2 * (width + 3 * third)),
        name="project_tokens",
    )(meta, mine, theirs, weights)


def key_range(starts, low, high, data_count):
    first = jnp.int32(1 << 30)
    last = jnp.int32(0)
    for data in range(data_count):
        begin, end = starts[data], starts[data + 1]
        hit = (begin < high) & (end > low) & (begin < end)
        first = jnp.where(hit, jnp.minimum(first, begin), first)
        last = jnp.where(hit, jnp.maximum(last, end), last)
    return first, last


def online(scores, value, m_ref, l_ref, acc_ref, head, rows):
    old_max = m_ref[head, rows, :]
    new_max = jnp.maximum(old_max, jnp.max(scores, axis=1, keepdims=True))
    probs = jnp.exp2(scores - new_max)
    alpha = jnp.exp2(old_max - new_max)
    l_ref[head, rows, :] = l_ref[head, rows, :] * alpha + jnp.sum(probs, axis=1, keepdims=True)
    acc_ref[head, rows, :] = acc_ref[head, rows, :] * alpha + mm(probs.astype(BF), value)
    m_ref[head, rows, :] = new_max


def token_forward_kernel(
    data_count, factor, meta, starts, q_ref, kv_ref, idr_ref, idc_ref, m_ref, l_ref, acc_ref
):
    size = idc_ref.shape[0]
    dim = acc_ref.shape[2]
    sub = size // 2
    base = meta[0] * size
    first, last = key_range(starts, base, base + size, data_count)
    m_ref[...] = jnp.full(m_ref.shape, NEGATIVE, F32)
    l_ref[...] = jnp.zeros(l_ref.shape, F32)
    acc_ref[...] = jnp.zeros(acc_ref.shape, F32)

    def step(block, carry):
        keys = pl.ds(pl.multiple_of(block * size, size), size)
        key_ids = idr_ref[block]
        for part in range(2):
            rows = pl.ds(part * sub, sub)
            mask = idc_ref[rows, :] == key_ids
            for head in range(2):
                query = q_ref[rows, pl.ds(head * dim, dim)]
                raw = mm_nt(query, kv_ref[keys, pl.ds(head * dim, dim)]) * factor
                scores = jnp.where(mask, raw, NEGATIVE)
                online(
                    scores, kv_ref[keys, pl.ds((2 + head) * dim, dim)], m_ref, l_ref, acc_ref, head, rows
                )
        return carry

    lax.fori_loop(first // size, (last + size - 1) // size, step, 0)


def smem():
    return pl.BlockSpec(memory_space=pltpu.SMEM)


def vmem():
    return pl.BlockSpec(memory_space=pltpu.VMEM)


def token_forward(meta, starts, q_all, kv_all, ids_row, ids_col, factor, data_count):
    size = ids_col.shape[0]
    dim = q_all.shape[1] // 2
    return pl.pallas_call(
        functools.partial(token_forward_kernel, data_count, factor),
        out_shape=(
            jax.ShapeDtypeStruct((2, size, 1), F32),
            jax.ShapeDtypeStruct((2, size, 1), F32),
            jax.ShapeDtypeStruct((2, size, dim), F32),
        ),
        in_specs=[smem(), smem(), vmem(), vmem(), vmem(), vmem()],
        out_specs=[vmem(), vmem(), vmem()],
        compiler_params=params(),
        cost_estimate=cost(4e9, 8e6, 2e6),
        name="token_forward",
    )(meta, starts, q_all, kv_all, ids_row, ids_col)


def prompt_forward_kernel(
    data_count,
    factor,
    meta,
    starts,
    table,
    q_ref,
    idc_ref,
    m_in,
    l_in,
    acc_in,
    prompt_hbm,
    weights,
    o_ref,
    wide_ref,
    lse_ref,
    kv_hbm,
    m_ref,
    l_ref,
    acc_ref,
    raw_ref,
    kv_ref,
    done,
    in_sem,
    out_sem,
):
    size = idc_ref.shape[0]
    dim = acc_ref.shape[2]
    sub = size // 2
    base = meta[0] * size
    head_count, block = raw_ref.shape[1], raw_ref.shape[2]
    pieces = PLEN // block
    prompt_count = done.shape[0]
    m_ref[...] = m_in[...]
    l_ref[...] = l_in[...]
    acc_ref[...] = acc_in[...]
    for number in range(prompt_count):
        done[number] = 0

    def load(number):
        @pl.when(done[number] == 0)
        def _():
            copy = pltpu.make_async_copy(
                prompt_hbm.at[pl.ds(number * pieces, pieces)], raw_ref, in_sem
            )
            copy.start()
            copy.wait()
            for piece in range(pieces):
                rows = jnp.concatenate([raw_ref[piece, h] for h in range(head_count)], axis=1)
                kv_ref[number * pieces + piece] = mm(rows, weights[...]).astype(BF)
            done[number] = 1
            pltpu.make_async_copy(
                kv_ref.at[pl.ds(number * pieces, pieces)],
                kv_hbm.at[pl.ds(number * pieces, pieces)],
                out_sem.at[number],
            ).start()

    for part in range(2):
        low = base + part * sub
        rows = pl.ds(part * sub, sub)

        def visit(data, carry):
            begin, end = starts[data], starts[data + 1]

            @pl.when((begin < low + sub) & (end > low) & (begin < end))
            def _():
                number = table[data]
                load(number)
                mask = idc_ref[rows, :] == data.astype(F32)
                for piece in range(pieces):
                    for head in range(2):
                        query = q_ref[rows, pl.ds(head * dim, dim)]
                        key = kv_ref[number * pieces + piece, :, pl.ds(head * dim, dim)]
                        value = kv_ref[number * pieces + piece, :, pl.ds((2 + head) * dim, dim)]
                        scores = jnp.where(mask, mm_nt(query, key) * factor, NEGATIVE)
                        online(scores, value, m_ref, l_ref, acc_ref, head, rows)

            return carry

        lax.fori_loop(0, data_count, visit, 0)
    for head in range(2):
        total = l_ref[head]
        wide = acc_ref[head] / total
        wide_ref[:, pl.ds(head * dim, dim)] = wide
        o_ref[:, pl.ds(head * dim, dim)] = wide.astype(BF)
        lse_ref[head] = m_ref[head] + jnp.log2(total)
    for number in range(prompt_count):

        @pl.when(done[number] == 1)
        def _():
            pltpu.make_async_copy(
                kv_ref.at[pl.ds(number * pieces, pieces)],
                kv_hbm.at[pl.ds(number * pieces, pieces)],
                out_sem.at[number],
            ).wait()


def prompt_forward(
    meta, starts, table, q_all, ids_col, state, prompt_all, weights, factor, data_count
):
    size = ids_col.shape[0]
    dim = q_all.shape[1] // 2
    shards, head_count, block, _ = prompt_all.shape
    pieces = PLEN // block
    prompt_count = shards // pieces
    width = weights.shape[1]
    anywhere = pl.BlockSpec(memory_space=pl.ANY)
    return pl.pallas_call(
        functools.partial(prompt_forward_kernel, data_count, factor),
        out_shape=(
            jax.ShapeDtypeStruct((size, 2 * dim), BF),
            jax.ShapeDtypeStruct((size, 2 * dim), F32),
            jax.ShapeDtypeStruct((2, size, 1), F32),
            jax.ShapeDtypeStruct((shards, block, width), BF),
        ),
        in_specs=[smem(), smem(), smem(), vmem(), vmem(), vmem(), vmem(), vmem(), anywhere, vmem()],
        out_specs=[vmem(), vmem(), vmem(), anywhere],
        scratch_shapes=[
            pltpu.VMEM((2, size, 1), F32),
            pltpu.VMEM((2, size, 1), F32),
            pltpu.VMEM((2, size, dim), F32),
            pltpu.VMEM((pieces, head_count, block, prompt_all.shape[3]), BF),
            pltpu.VMEM((shards, block, width), BF),
            pltpu.SMEM((prompt_count,), jnp.int32),
            pltpu.SemaphoreType.DMA,
            pltpu.SemaphoreType.DMA((prompt_count,)),
        ],
        compiler_params=params(),
        cost_estimate=cost(4e9, 8e6, 2e6),
        name="prompt_forward",
    )(meta, starts, table, q_all, ids_col, *state, prompt_all, weights)


def norm_parts(value):
    center = value - jnp.mean(value, axis=-1, keepdims=True)
    scale = lax.rsqrt(jnp.mean(center * center, axis=-1, keepdims=True) + 1e-05)
    return center * scale, scale


def norm_back(grad, unit, scale, gain):
    part = grad * gain
    return scale * (
        part
        - jnp.mean(part, axis=-1, keepdims=True)
        - unit * jnp.mean(part * unit, axis=-1, keepdims=True)
    )


def feed_kernel(
    meta,
    mine,
    theirs,
    wide_ref,
    lse_ref,
    tok_ref,
    cot_ref,
    w_ref,
    down_bias,
    gains,
    shifts,
    out_ref,
    da_ref,
    pack_ref,
    delta_ref,
):
    size, width = tok_ref.shape
    dim = mine.shape[1] // 2
    heads = w_ref.shape[0]
    hid = (w_ref.shape[1] - PACK - dim) // 2
    even = meta[2] == 0
    place_out = slice(hid, hid + dim)
    place_up = slice(hid + dim, 2 * hid + dim)
    place_bias = 2 * hid + dim
    sub = min(256, size)
    g0, g1 = gains[0:1, :], gains[1:2, :]
    for part in range(size // sub):
        rows = pl.ds(part * sub, sub)
        a, b = mine[rows, :], theirs[rows, :]
        first = jnp.where(even, a, b)
        second = jnp.where(even, b, a)
        attn = mm(first[:, :dim], w_ref[0, place_out, :])
        attn += mm(second[:, :dim], w_ref[1, place_out, :])
        attn += mm(first[:, dim:], w_ref[2, place_out, :])
        attn += mm(second[:, dim:], w_ref[3, place_out, :])
        unit_one, scale_one = norm_parts(tok_ref[rows, :].astype(F32) + attn)
        normed = unit_one * g0 + shifts[0:1, :]
        normed_low = normed.astype(BF)
        branch = down_bias[...]
        slopes = []
        for q in range(heads):
            bias = (
                w_ref[q, place_bias : place_bias + 1, :hid].astype(F32)
                + w_ref[q, place_bias : place_bias + 1, hid : 2 * hid].astype(F32)
                + w_ref[q, place_bias + 1 : place_bias + 2, :hid].astype(F32)
            )
            pre = mm_nt(normed_low, w_ref[q, place_up, :]) + bias
            cdf = 0.5 * (1.0 + lax.erf(pre * 0.7071067811865476))
            slopes.append(cdf + pre * (jnp.exp(-0.5 * pre * pre) * 0.3989422804014327))
            branch = branch + mm((pre * cdf).astype(BF), w_ref[q, :hid, :])
        unit_two, scale_two = norm_parts(normed + branch)
        out_ref[rows, :] = unit_two * g1 + shifts[1:2, :]
        grad_mixed = norm_back(cot_ref[rows, :].astype(F32), unit_two, scale_two, g1)
        mixed_low = grad_mixed.astype(BF)
        grad_normed = grad_mixed
        for q in range(heads):
            grad_pre = mm_nt(mixed_low, w_ref[q, :hid, :]) * slopes[q]
            grad_normed = grad_normed + mm(grad_pre.astype(BF), w_ref[q, place_up, :])
        grad_sum = norm_back(grad_normed, unit_one, scale_one, g0)
        da_ref[rows, :] = grad_sum
        sum_low = grad_sum.astype(BF)
        for head in range(2):
            cols = pl.ds(head * dim, dim)
            weight = w_ref[2 * head + meta[2], place_out, :]
            grad_out = mm_nt(sum_low, weight).astype(BF)
            pack_ref[rows, cols] = grad_out
            delta = jnp.sum(grad_out.astype(F32) * wide_ref[rows, cols], axis=1, keepdims=True)
            delta_ref[head, rows, :] = delta
    rows_per = size // (2 * dim)
    pack_ref[pl.ds(size, STATS), :] = jnp.zeros((STATS, 2 * dim), BF)
    for head in range(2):
        for kind, ref in enumerate((lse_ref, delta_ref)):
            line = jnp.transpose(jnp.broadcast_to(ref[head], (size, 128)))[0:1, :]
            for place, term in enumerate(split3(line)):
                for i in range(rows_per):
                    row = size + ((head * 2 + kind) * 3 + place) * rows_per + i
                    pack_ref[row : row + 1, :] = term[:, i * 2 * dim : (i + 1) * 2 * dim]


def feed(meta, mine, theirs, wide, lse, tok, cot, w, down_bias, gains, shifts):
    size, width = tok.shape
    dim = mine.shape[1] // 2
    return pl.pallas_call(
        feed_kernel,
        out_shape=(
            jax.ShapeDtypeStruct((size, width), F32),
            jax.ShapeDtypeStruct((size, width), F32),
            jax.ShapeDtypeStruct((size + STATS, 2 * dim), BF),
            jax.ShapeDtypeStruct((2, size, 1), F32),
        ),
        in_specs=[smem()] + [vmem()] * 10,
        out_specs=[vmem()] * 4,
        compiler_params=params(),
        cost_estimate=cost(3e9, 8e6, 1e6),
        name="feed",
    )(meta, mine, theirs, wide, lse, tok, cot, w, down_bias, gains, shifts)


def query_grad_kernel(
    data_count,
    factor,
    meta,
    starts,
    table,
    q_ref,
    kv_ref,
    idr_ref,
    idc_ref,
    lse_ref,
    delta_ref,
    do_ref,
    prompt_hbm,
    dq_ref,
    acc_ref,
    pkv_ref,
    done,
    in_sem,
):
    size = idc_ref.shape[0]
    dim = acc_ref.shape[2]
    sub = size // 2
    base = meta[0] * size
    block = pkv_ref.shape[1]
    pieces = PLEN // block
    prompt_count = done.shape[0]
    first, last = key_range(starts, base, base + size, data_count)
    acc_ref[...] = jnp.zeros(acc_ref.shape, F32)
    for number in range(prompt_count):
        done[number] = 0

    def update(part, head, mask, key, value):
        rows = pl.ds(part * sub, sub)
        cols = pl.ds(head * dim, dim)
        query = q_ref[rows, cols]
        scores = jnp.where(mask, mm_nt(query, key) * factor, NEGATIVE)
        probs = jnp.exp2(scores - lse_ref[head, rows, :])
        grad = mm_nt(do_ref[rows, cols], value)
        low = (probs * (grad - delta_ref[head, rows, :])).astype(BF)
        acc_ref[head, rows, :] += mm(low, key)

    def step(index, carry):
        keys = pl.ds(pl.multiple_of(index * size, size), size)
        key_ids = idr_ref[index]
        for part in range(2):
            mask = idc_ref[pl.ds(part * sub, sub), :] == key_ids
            for head in range(2):
                update(
                    part,
                    head,
                    mask,
                    kv_ref[keys, pl.ds(head * dim, dim)],
                    kv_ref[keys, pl.ds((2 + head) * dim, dim)],
                )
        return carry

    lax.fori_loop(first // size, (last + size - 1) // size, step, 0)

    def load(number):
        @pl.when(done[number] == 0)
        def _():
            rows = pl.ds(number * pieces, pieces)
            copy = pltpu.make_async_copy(prompt_hbm.at[rows], pkv_ref.at[rows], in_sem)
            copy.start()
            copy.wait()
            done[number] = 1

    for part in range(2):
        low = base + part * sub

        def visit(data, carry):
            begin, end = starts[data], starts[data + 1]

            @pl.when((begin < low + sub) & (end > low) & (begin < end))
            def _():
                number = table[data]
                load(number)
                mask = idc_ref[pl.ds(part * sub, sub), :] == data.astype(F32)
                for piece in range(pieces):
                    for head in range(2):
                        update(
                            part,
                            head,
                            mask,
                            pkv_ref[number * pieces + piece, :, pl.ds(head * dim, dim)],
                            pkv_ref[number * pieces + piece, :, pl.ds((2 + head) * dim, dim)],
                        )

            return carry

        lax.fori_loop(0, data_count, visit, 0)
    for head in range(2):
        dq_ref[:, pl.ds(head * dim, dim)] = (acc_ref[head] * dim ** (-0.5)).astype(BF)


def query_grad(
    meta, starts, table, q_all, kv_all, ids_row, ids_col, lse, delta, do, prompt_kv, factor, data_count
):
    size = ids_col.shape[0]
    dim = q_all.shape[1] // 2
    shards, block, width = prompt_kv.shape
    prompt_count = shards * block // PLEN
    return pl.pallas_call(
        functools.partial(query_grad_kernel, data_count, factor),
        out_shape=jax.ShapeDtypeStruct((size, 2 * dim), BF),
        in_specs=[smem()] * 3 + [vmem()] * 7 + [pl.BlockSpec(memory_space=pl.ANY)],
        out_specs=vmem(),
        scratch_shapes=[
            pltpu.VMEM((2, size, dim), F32),
            pltpu.VMEM((shards, block, width), BF),
            pltpu.SMEM((prompt_count,), jnp.int32),
            pltpu.SemaphoreType.DMA,
        ],
        compiler_params=params(),
        cost_estimate=cost(6e9, 16e6, 4e6),
        name="query_grad",
    )(meta, starts, table, q_all, kv_all, ids_row, ids_col, lse, delta, do, prompt_kv)


def stat_line(pack_ref, slot, size, dim, head, kind, part):
    rows_per = size // (2 * dim)
    total = 0.0
    for place in range(3):
        row = size + ((head * 2 + kind) * 3 + place) * rows_per + part
        total = total + pack_ref[slot, row : row + 1, :].astype(F32)
    return total


def key_update(query, grad, key, value, mask, lse, delta, factor):
    scores = jnp.where(mask, mm_nt(key, query) * factor, NEGATIVE)
    probs = jnp.exp2(scores - lse)
    grad_value = mm(probs.astype(BF), grad)
    low = (probs * (mm_nt(value, grad) - delta)).astype(BF)
    return mm(low, query), grad_value


def prompt_grad_kernel(
    data_count, factor, meta, starts, table, q_ref, idr_ref, pack_ref, own_ref, weights, out_ref, dk_ref, dv_ref, kv_ref
):
    row_count = pack_ref.shape[0]
    size = pack_ref.shape[1] - STATS
    block = own_ref.shape[0]
    dim = q_ref.shape[1] // 2
    sub = 2 * dim
    number = meta[0] * block // PLEN
    dk_ref[...] = jnp.zeros(dk_ref.shape, F32)
    dv_ref[...] = jnp.zeros(dv_ref.shape, F32)
    kv_ref[...] = mm(own_ref[...], weights[...]).astype(BF)
    parts = size // sub

    def visit(data, carry):
        begin, end = starts[data], starts[data + 1]

        @pl.when((table[data] == number) & (begin < end))
        def _():
            def step(index, inner):
                shard = index // parts
                slot = slot_of(shard ^ meta[0], meta[2], row_count)
                for part in range(parts):

                    @pl.when(index % parts == part)
                    def _():
                        low = pl.multiple_of(index * sub, sub)
                        mask = idr_ref[shard, :, part * sub : (part + 1) * sub] == data.astype(F32)
                        for head in range(2):
                            cols = pl.ds(head * dim, dim)
                            dk, dv = key_update(
                                q_ref[pl.ds(low, sub), cols],
                                pack_ref[slot, part * sub : (part + 1) * sub, cols],
                                kv_ref[:, cols],
                                kv_ref[:, pl.ds((2 + head) * dim, dim)],
                                mask,
                                stat_line(pack_ref, slot, size, dim, head, 0, part),
                                stat_line(pack_ref, slot, size, dim, head, 1, part),
                                factor,
                            )
                            dk_ref[:, cols] += dk
                            dv_ref[:, cols] += dv

                return inner

            lax.fori_loop(begin // sub, (end + sub - 1) // sub, step, 0)

        return carry

    lax.fori_loop(0, data_count, visit, 0)
    grads = jnp.concatenate(
        [(dk_ref[...] * dim ** (-0.5)).astype(BF), dv_ref[...].astype(BF)], axis=1
    )
    out_ref[...] = mm_nt(grads, weights[...]).astype(BF)


def prompt_grad(meta, starts, table, q_all, ids_row, pack_all, own, weights, factor, data_count):
    block, width = own.shape
    dim = q_all.shape[1] // 2
    return pl.pallas_call(
        functools.partial(prompt_grad_kernel, data_count, factor),
        out_shape=jax.ShapeDtypeStruct((block, width), BF),
        in_specs=[smem()] * 3 + [vmem()] * 5,
        out_specs=vmem(),
        scratch_shapes=[
            pltpu.VMEM((block, 2 * dim), F32),
            pltpu.VMEM((block, 2 * dim), F32),
            pltpu.VMEM((block, 4 * dim), BF),
        ],
        compiler_params=params(),
        cost_estimate=cost(6e9, 16e6, 4e6),
        name="prompt_grad",
    )(meta, starts, table, q_all, ids_row, pack_all, own, weights)


def token_grad_kernel(
    data_count, factor, meta, starts, q_ref, kv_ref, idr_ref, idc_ref, pack_ref, dq_ref, weights, out_ref, dk_ref, dv_ref
):
    row_count = pack_ref.shape[0]
    size = idc_ref.shape[0]
    dim = q_ref.shape[1] // 2
    sub = 2 * dim
    base = pl.multiple_of(meta[0] * size, size)
    first, last = key_range(starts, base, base + size, data_count)
    dk_ref[...] = jnp.zeros(dk_ref.shape, F32)
    dv_ref[...] = jnp.zeros(dv_ref.shape, F32)

    def step(shard, carry):
        slot = slot_of(shard ^ meta[0], meta[2], row_count)
        low = pl.multiple_of(shard * size, size)
        for part in range(size // sub):
            mask = idc_ref[...] == idr_ref[shard, :, part * sub : (part + 1) * sub]
            for head in range(2):
                cols = pl.ds(head * dim, dim)
                dk, dv = key_update(
                    q_ref[pl.ds(low + part * sub, sub), cols],
                    pack_ref[slot, part * sub : (part + 1) * sub, cols],
                    kv_ref[:, cols],
                    kv_ref[:, pl.ds((2 + head) * dim, dim)],
                    mask,
                    stat_line(pack_ref, slot, size, dim, head, 0, part),
                    stat_line(pack_ref, slot, size, dim, head, 1, part),
                    factor,
                )
                dk_ref[:, cols] += dk
                dv_ref[:, cols] += dv
        return carry

    lax.fori_loop(first // size, (last + size - 1) // size, step, 0)
    grads = jnp.concatenate(
        [dq_ref[...], (dk_ref[...] * dim ** (-0.5)).astype(BF), dv_ref[...].astype(BF)], axis=1
    )
    out_ref[...] = mm_nt(grads, weights[...]).astype(BF)


def token_grad(meta, starts, q_all, kv_all, ids_row, ids_col, pack_all, dq, weights, factor, data_count):
    size = ids_col.shape[0]
    dim = q_all.shape[1] // 2
    return pl.pallas_call(
        functools.partial(token_grad_kernel, data_count, factor),
        out_shape=jax.ShapeDtypeStruct((size, weights.shape[0]), BF),
        in_specs=[smem()] * 2 + [vmem()] * 7,
        out_specs=vmem(),
        scratch_shapes=[pltpu.VMEM((size, 2 * dim), F32), pltpu.VMEM((size, 2 * dim), F32)],
        compiler_params=params(),
        cost_estimate=cost(4e9, 16e6, 4e6),
        name="token_grad",
    )(meta, starts, q_all, kv_all, ids_row, ids_col, pack_all, dq, weights)


def per_device(
    tokens,
    cotangent,
    dataset_ids,
    prompt_map,
    attn_in,
    attn_out,
    up_weight,
    up_bias,
    down_weight,
    down_bias,
    norm_gains,
    norm_shifts,
    prompts,
    moment_one,
    moment_two,
    step_count,
):
    size, width = tokens.shape[1:]
    dim = attn_in.shape[2]
    hid = up_weight.shape[1]
    data_count = prompt_map.shape[1]
    row_count = lax.axis_size("rows")
    head_count = lax.axis_size("head")
    factor = dim ** (-0.5) * LOG2E
    row = lax.axis_index("rows")
    head = lax.axis_index("head")
    batch, parity = head // 2, head % 2
    half = size // 2
    meta = jnp.stack([row, batch, parity]).astype(jnp.int32)

    tok = lax.dynamic_index_in_dim(tokens, batch, 0, keepdims=False)
    cot = lax.dynamic_index_in_dim(cotangent, batch, 0, keepdims=False)
    ids = lax.dynamic_index_in_dim(dataset_ids, batch, 0, keepdims=False)
    table = lax.dynamic_index_in_dim(prompt_map, batch, 0, keepdims=False)
    tok_half = lax.dynamic_slice_in_dim(tok, parity * half, half, 0)
    id_rows = jnp.zeros((PACK, width), BF).at[0, :size].set(ids.astype(BF))
    mine = gather_rows(jnp.concatenate([tok_half, id_rows], axis=0), row_count, head_count)
    theirs = swap_head(mine, 1, head_count)

    in_other = swap_head(attn_in, 2, head_count)
    in_first = jnp.where(batch == 0, attn_in, in_other)
    in_second = jnp.where(batch == 0, in_other, attn_in)
    weights = jnp.concatenate(
        [w[i] for i in range(3) for w in (in_first, in_second)], axis=1
    )
    weights_kv = weights[:, 2 * dim :]

    prompt_low = prompts.astype(BF)
    column = width // head_count
    prompt_own = lax.dynamic_slice_in_dim(prompt_low, head * column, column, 1)
    prompt_all = lax.all_gather(prompt_own, BOTH, axis=0, tiled=False)
    prompt_all = prompt_all.reshape(row_count, head_count, prompt_own.shape[0], column)

    bias_high = lax.reduce_precision(up_bias, 8, 7)
    bias_rest = up_bias - bias_high
    bias_mid = lax.reduce_precision(bias_rest, 8, 7)
    bias_terms = [t.astype(BF) for t in (bias_high, bias_mid, bias_rest - bias_mid)]
    bias_rows = jnp.zeros((PACK, width), BF)
    for place, term in enumerate(bias_terms):
        line, lane = place // 2, (place % 2) * hid
        bias_rows = bias_rows.at[line, lane : lane + hid].set(term)
    layer_weights = lax.all_gather(
        jnp.concatenate([down_weight, attn_out, up_weight.T, bias_rows], axis=0), "head", axis=0
    )

    q_all, kv_all, ids_row = project_tokens(meta, mine, theirs, weights, row_count)
    numbers = jnp.arange(data_count + 1, dtype=jnp.int32).astype(F32)
    starts = jnp.sum((ids_row.reshape(1, -1) < numbers[:, None]).astype(jnp.int32), axis=1)
    ids_col = ids.astype(F32).reshape(size, 1)
    q_own = lax.dynamic_slice_in_dim(q_all, row * size, size, 0)
    kv_own = lax.dynamic_slice_in_dim(kv_all, row * size, size, 0)
    state = token_forward(meta, starts, q_own, kv_all, ids_row, ids_col, factor, data_count)
    o_mine, wide, lse, prompt_kv = prompt_forward(
        meta, starts, table, q_own, ids_col, state, prompt_all, weights_kv, factor, data_count
    )
    o_theirs = swap_head(o_mine, 1, head_count)
    out, grad_sum, pack, delta = feed(
        meta,
        o_mine,
        o_theirs,
        wide,
        lse,
        tok,
        cot,
        layer_weights,
        down_bias.reshape(1, width),
        norm_gains,
        norm_shifts,
    )
    out_other = swap_head(out, 2, head_count)
    layer_out = jnp.stack(
        [jnp.where(batch == 0, out, out_other), jnp.where(batch == 0, out_other, out)]
    )

    pack_all = gather_rows(pack, row_count, head_count)
    dq = query_grad(
        meta, starts, table, q_own, kv_all, ids_row, ids_col, lse, delta, pack, prompt_kv, factor, data_count
    )
    prompt_part = prompt_grad(
        meta, starts, table, q_all, ids_row, pack_all, prompt_low, weights_kv, factor, data_count
    )
    token_part = token_grad(
        meta, starts, q_all, kv_own, ids_row, ids_col, pack_all, dq, weights, factor, data_count
    )

    split = width // 2
    keep = lax.dynamic_slice_in_dim(prompt_part, parity * split, split, 1)
    send = lax.dynamic_slice_in_dim(prompt_part, (1 - parity) * split, split, 1)
    pair = keep.astype(F32) + swap_head(send, 1, head_count).astype(F32)
    pair_low = lax.reduce_precision(pair, 8, 7).astype(BF)
    full_low = pair_low.astype(F32) + swap_head(pair_low, 2, head_count).astype(F32)
    full_low = lax.reduce_precision(full_low, 8, 7).astype(BF)
    squares = jnp.sum(full_low.astype(F32) ** 2).reshape(1, 1)
    squares = jnp.broadcast_to(squares, (8, 128))
    squares = squares + swap_head(squares, 1, head_count)
    mask = 1
    while mask < row_count:
        squares = squares + lax.ppermute(
            squares, "rows", [(i, i ^ mask) for i in range(row_count)]
        )
        mask = mask * 2
    grad_norm = jnp.sqrt(squares[0, 0])
    full_other = swap_head(full_low, 1, head_count)
    prompt_grads = jnp.concatenate(
        [jnp.where(parity == 0, full_low, full_other), jnp.where(parity == 0, full_other, full_low)],
        axis=1,
    ).astype(F32)
    clipped = prompt_grads * jnp.minimum(1.0, CLIP_NORM / (grad_norm + 1e-06))
    step_value = step_count.astype(F32)
    new_one = BETA_ONE * moment_one + (1.0 - BETA_ONE) * clipped
    new_two = BETA_TWO * moment_two + (1.0 - BETA_TWO) * clipped * clipped
    first_hat = new_one / (1.0 - jnp.power(BETA_ONE, step_value))
    second_hat = new_two / (1.0 - jnp.power(BETA_TWO, step_value))
    new_prompts = prompts * (1.0 - LEARNING_RATE * DECAY_RATE) - LEARNING_RATE * first_hat / (
        jnp.sqrt(second_hat) + EPSILON
    )

    core_sum = token_part.astype(F32) + swap_head(token_part, 1, head_count).astype(F32)
    total = lax.reduce_precision(grad_sum + core_sum, 8, 7).astype(BF)
    mine_half = lax.dynamic_slice_in_dim(total, parity * half, half, 0)
    other_half = swap_head(mine_half, 2, head_count)
    other_rest = swap_head(other_half, 1, head_count)
    other = jnp.concatenate(
        [
            jnp.where(parity == 0, other_half, other_rest),
            jnp.where(parity == 0, other_rest, other_half),
        ],
        axis=0,
    )
    input_grad = jnp.stack(
        [jnp.where(batch == 0, total, other), jnp.where(batch == 0, other, total)]
    ).astype(F32)
    return (layer_out, input_grad, clipped, grad_norm, new_one, new_two, new_prompts)


def solution(mesh):
    in_specs = (
        P(None, "rows", None),
        P(None, "rows", None),
        P(None, "rows"),
        P(),
        P(None, None, "head"),
        P("head", None),
        P(None, "head"),
        P("head"),
        P("head", None),
        P(),
        P(),
        P(),
        P("rows", None),
        P("rows", None),
        P("rows", None),
        P(),
    )
    out_specs = (
        P(None, "rows", None),
        P(None, "rows", None),
        P("rows", None),
        P(),
        P("rows", None),
        P("rows", None),
        P("rows", None),
    )
    return jax.shard_map(
        per_device, mesh=mesh, in_specs=in_specs, out_specs=out_specs, check_vma=False
    )
```

```python
import functools

import jax
import jax.numpy as jnp
from jax import lax
from jax.experimental import pallas as pl
from jax.experimental.pallas import tpu as pltpu
from jax.sharding import PartitionSpec as P

PLEN = 1000
NEGATIVE = -1e30
BETA_ONE = 0.9
BETA_TWO = 0.999
LEARNING_RATE = 0.5
DECAY_RATE = 0.01
EPSILON = 1e-08
CLIP_NORM = 1.0
LOG2E = 1.4426950408889634
PACK = 16
STATS = 32
VMEM_LIMIT = 60 * 1024 * 1024
BF = jnp.bfloat16
F32 = jnp.float32
BOTH = ("rows", "head")


def params(operand_bytes):
    return pltpu.CompilerParams(vmem_limit_bytes=min(VMEM_LIMIT, operand_bytes + (20 << 20)))


def cost(flops, bytes_accessed, transcendentals=0):
    return pl.CostEstimate(
        flops=int(flops), bytes_accessed=int(bytes_accessed), transcendentals=int(transcendentals)
    )


def mm(a, b):
    return lax.dot_general(a, b, (((1,), (0,)), ((), ())), preferred_element_type=F32)


def mm_nt(a, b):
    return lax.dot_general(a, b, (((1,), (1,)), ((), ())), preferred_element_type=F32)


def split3(value):
    high = value.astype(BF)
    rest = value - high.astype(F32)
    mid = rest.astype(BF)
    low = (rest - mid.astype(F32)).astype(BF)
    return high, mid, low


def bit_orders(row_count):
    bits = row_count.bit_length() - 1
    return ([0] + list(range(bits - 1, 0, -1)), list(range(bits - 1, 0, -1)) + [0])


def slot_of(offset, parity, row_count):
    order_even, order_odd = bit_orders(row_count)

    def mapped(order):
        total = 0
        for place, bit in enumerate(order):
            total = total + (((offset >> bit) & 1) << place)
        return total

    return jnp.where(parity == 0, mapped(order_even), mapped(order_odd))


def gather_rows(block, row_count, head_count):
    order_even, order_odd = bit_orders(row_count)
    held = block[None]
    for place, (even_bit, odd_bit) in enumerate(zip(order_even, order_odd)):
        pairs = []
        for row in range(row_count):
            for head in range(head_count):
                bit = even_bit if head % 2 == 0 else odd_bit
                pairs.append((row * head_count + head, (row ^ (1 << bit)) * head_count + head))
        other = lax.ppermute(held, BOTH, pairs)
        if place < len(order_even) - 1:
            held = jnp.concatenate([held, other], axis=0)
    return held, other


def swap_head(value, mask, head_count):
    return lax.ppermute(value, "head", [(i, i ^ mask) for i in range(head_count)])


def smem():
    return pl.BlockSpec(memory_space=pltpu.SMEM)


def vmem():
    return pl.BlockSpec(memory_space=pltpu.VMEM)


def anywhere():
    return pl.BlockSpec(memory_space=pl.ANY)


def join_weights(meta, own, other, target, first):
    dim = own.shape[2]
    for kind in range(first, own.shape[0]):
        for place in range(2):
            column = ((kind - first) * 2 + place) * dim
            target[:, column : column + dim] = jnp.where(meta[1] == place, own[kind], other[kind])


def wide(value, count):
    return jnp.concatenate([value] * count, axis=1)


def column_of(line):
    return jnp.transpose(jnp.broadcast_to(line, (128, line.shape[1])))


def project_query_kernel(meta, a, b, c, d, own, other, q_out):
    half = a.shape[1] - PACK
    dim = own.shape[2]
    weights = jnp.concatenate(
        [jnp.where(meta[1] == place, own[0], other[0]) for place in range(2)], axis=1
    )
    for high, pair in enumerate(((a, b), (c, d))):
        for place, ref in enumerate(pair):
            q_out[high, 0, place] = mm(ref[0, :half], weights).astype(BF)


def project_query(meta, mine, theirs, in_own, in_other):
    slots, rows, width = mine[0].shape
    half = rows - PACK
    dim = in_own.shape[2]
    block = pl.BlockSpec((1, rows, width), lambda g: (g, 0, 0))
    whole = pl.BlockSpec((1,) + in_own.shape[1:], lambda g: (0, 0, 0))
    out = pl.pallas_call(
        project_query_kernel,
        out_shape=jax.ShapeDtypeStruct((2, slots, 2, half, 2 * dim), BF),
        grid=(slots,),
        in_specs=[smem()] + [block] * 4 + [whole] * 2,
        out_specs=pl.BlockSpec((2, 1, 2, half, 2 * dim), lambda g: (0, g, 0, 0, 0)),
        compiler_params=params(8 << 20),
        cost_estimate=cost(8 * slots * half * width * 2 * dim, 8 * slots * half * width),
        name="project_query",
    )(meta, mine[0], theirs[0], mine[1], theirs[1], in_own, in_other)
    return out.reshape(4 * slots, half, 2 * dim)


def key_range(starts, low, high, data_count):
    first = jnp.int32(1 << 30)
    last = jnp.int32(0)
    for data in range(data_count):
        begin, end = starts[data], starts[data + 1]
        hit = (begin < high) & (end > low) & (begin < end)
        first = jnp.where(hit, jnp.minimum(first, begin), first)
        last = jnp.where(hit, jnp.maximum(last, end), last)
    return first, last


def load_shard(meta, shard, gathered, x_ref, line_ref):
    mine_low, theirs_low, mine_high, theirs_high = gathered
    slots, half = mine_low.shape[0], mine_low.shape[1] - PACK
    parity = meta[2]
    for place, (low, high) in enumerate(((mine_low, mine_high), (theirs_low, theirs_high))):
        slot = slot_of(shard ^ meta[0], parity ^ place, 2 * slots)
        for bank, ref in enumerate((low, high)):

            @pl.when((slot < slots) if bank == 0 else (slot >= slots))
            def _():
                x_ref[place * half : (place + 1) * half, :] = ref[slot - bank * slots, :half, :]
                if place == 0:
                    line_ref[...] = ref[slot - bank * slots, half : half + 1, :].astype(F32)

    line = line_ref[...]
    first, second = line[:, :half], line[:, half : 2 * half]
    return jnp.concatenate(
        [jnp.where(parity == 0, first, second), jnp.where(parity == 0, second, first)], axis=1
    )


def online(scores, factor, mask, m_ref, head, rows):
    old_max = m_ref[head, rows, :]
    size = old_max.shape[0]
    top = jnp.broadcast_to(jnp.max(scores, axis=1, keepdims=True) * factor, (size, 128))
    new_max = jnp.maximum(old_max, top)
    shift = new_max
    if mask is not None:
        new_max = jnp.where(mask, new_max, old_max)
        shift = jnp.where(mask, new_max, -NEGATIVE)
    m_ref[head, rows, :] = new_max
    probs = jnp.exp2(scores * factor - wide(shift, scores.shape[1] // 128))
    return probs.astype(BF), jnp.exp2(old_max - new_max)


def accumulate(acc_ref, head, rows, alpha, probs, value):
    with_ones = jnp.concatenate([value, jnp.ones((value.shape[0], 128), BF)], axis=1)
    acc_ref[head, rows, :] = acc_ref[head, rows, :] * wide(
        alpha, with_ones.shape[1] // 128
    ) + mm(probs, with_ones)


def token_forward_kernel(
    data_count,
    factor,
    meta,
    starts,
    tok_ref,
    ids_ref,
    mine_low,
    theirs_low,
    mine_high,
    theirs_high,
    in_own,
    in_other,
    q_ref,
    m_ref,
    acc_ref,
    w_ref,
    x_ref,
    line_ref,
    id_ref,
):
    size, dim = tok_ref.shape[1], in_own.shape[2]
    base = meta[0] * size
    first, last = key_range(starts, base, base + size, data_count)
    join_weights(meta, in_own, in_other, w_ref, 0)
    q_ref[...] = mm(tok_ref[meta[1]], w_ref[:, : 2 * dim]).astype(BF)
    m_ref[...] = jnp.full(m_ref.shape, NEGATIVE, F32)
    acc_ref[...] = jnp.zeros(acc_ref.shape, F32)
    id_ref[...] = column_of(ids_ref[...])
    rows = pl.ds(0, size)

    def step(shard, carry):
        line = load_shard(
            meta, shard, (mine_low, theirs_low, mine_high, theirs_high), x_ref, line_ref
        )
        kv = mm(x_ref[...], w_ref[:, 2 * dim :]).astype(BF)
        mask = wide(id_ref[...], size // 128) == line
        raw = [
            mm_nt(q_ref[:, h * dim : (h + 1) * dim], kv[:, h * dim : (h + 1) * dim])
            for h in range(2)
        ]
        parts = [
            online(jnp.where(mask, raw[h], NEGATIVE), factor, None, m_ref, h, rows)
            for h in range(2)
        ]
        for h in range(2):
            value = kv[:, (2 + h) * dim : (3 + h) * dim]
            accumulate(acc_ref, h, rows, parts[h][1], parts[h][0], value)
        return carry

    lax.fori_loop(first // size, (last + size - 1) // size, step, 0)


def token_forward(meta, starts, tokens, ids_row, mine, theirs, in_own, in_other, factor, data_count):
    size, width = tokens.shape[1:]
    dim = in_own.shape[2]
    return pl.pallas_call(
        functools.partial(token_forward_kernel, data_count, factor),
        out_shape=(
            jax.ShapeDtypeStruct((size, 2 * dim), BF),
            jax.ShapeDtypeStruct((2, size, 128), F32),
            jax.ShapeDtypeStruct((2, size, dim + 128), F32),
        ),
        in_specs=[smem(), smem()] + [vmem()] * 8,
        out_specs=[vmem()] * 3,
        scratch_shapes=[
            pltpu.VMEM((width, 6 * dim), BF),
            pltpu.VMEM((size, width), BF),
            pltpu.VMEM((1, width), F32),
            pltpu.VMEM((size, 128), F32),
        ],
        compiler_params=params(4 * mine[0].size * 2),
        cost_estimate=cost(4e9, 8e6, 2e6),
        name="token_forward",
    )(meta, starts, tokens, ids_row, mine[0], theirs[0], mine[1], theirs[1], in_own, in_other)


def fetch_prompts(data_count, starts, table, base, size, prompt_hbm, raw_ref, state, sem):
    pieces = raw_ref.shape[1]
    for number in range(raw_ref.shape[0]):
        used = jnp.int32(0)
        for data in range(data_count):
            begin, end = starts[data], starts[data + 1]
            hit = (begin < base + size) & (end > base) & (begin < end) & (table[data] == number)
            used = jnp.where(hit, 1, used)
        state[number] = used

        @pl.when(used == 1)
        def _():
            pltpu.make_async_copy(
                prompt_hbm.at[pl.ds(number * pieces, pieces)], raw_ref.at[number], sem.at[number]
            ).start()


def project_prompt(number, prompt_hbm, raw_ref, w_ref, kv_ref, state, sem):
    pieces, head_count, block, _ = raw_ref.shape[1:]

    @pl.when(state[number] == 1)
    def _():
        pltpu.make_async_copy(
            prompt_hbm.at[pl.ds(number * pieces, pieces)], raw_ref.at[number], sem.at[number]
        ).wait()
        for piece in range(pieces):
            rows = jnp.concatenate([raw_ref[number, piece, h] for h in range(head_count)], axis=1)
            kv_ref[number, pl.ds(piece * block, block), :] = mm(rows, w_ref[...]).astype(BF)
        kv_ref[number, PLEN:, :] = jnp.zeros((kv_ref.shape[1] - PLEN, kv_ref.shape[2]), BF)
        state[number] = 2


def prompt_mask(scores):
    lanes = lax.broadcasted_iota(jnp.int32, (scores.shape[0], 128), 1)
    edge = scores.shape[1] - 128
    tail = jnp.where(lanes < PLEN - edge, scores[:, edge:], NEGATIVE)
    return jnp.concatenate([scores[:, :edge], tail], axis=1)


def visit_prompts(data_count, starts, table, base, size, prepare, update):
    def visit(data, carry):
        begin, end = starts[data], starts[data + 1]

        @pl.when((begin < base + size) & (end > base) & (begin < end))
        def _():
            number = table[data]
            prepare(number)
            low = (jnp.maximum(begin, base) - base) // 128
            count = (jnp.minimum(end, base + size) - base + 127) // 128 - low
            for case in range(1, size // 128 + 1):

                @pl.when(count == case)
                def _():
                    update(pl.ds(pl.multiple_of(low * 128, 128), case * 128), data, number)

        return carry

    lax.fori_loop(0, data_count, visit, 0)


def prompt_forward_kernel(
    data_count,
    factor,
    meta,
    starts,
    table,
    q_ref,
    ids_ref,
    m_in,
    acc_in,
    prompt_hbm,
    in_own,
    in_other,
    o_ref,
    wide_ref,
    lse_ref,
    m_ref,
    acc_ref,
    raw_ref,
    w_ref,
    kv_ref,
    id_ref,
    state,
    sem,
):
    size, dim = q_ref.shape[0], q_ref.shape[1] // 2
    base = meta[0] * size
    fetch_prompts(data_count, starts, table, base, size, prompt_hbm, raw_ref, state, sem)
    join_weights(meta, in_own, in_other, w_ref, 1)
    m_ref[...] = m_in[...]
    acc_ref[...] = acc_in[...]
    id_ref[...] = column_of(ids_ref[...])

    def prepare(number):
        project_prompt(number, prompt_hbm, raw_ref, w_ref, kv_ref, state, sem)

    def update(rows, data, number):
        mask = id_ref[rows, :] == data.astype(F32)
        raw = [
            mm_nt(q_ref[rows, pl.ds(h * dim, dim)], kv_ref[number, :, pl.ds(h * dim, dim)])
            for h in range(2)
        ]
        parts = [online(prompt_mask(raw[h]), factor, mask, m_ref, h, rows) for h in range(2)]
        for h in range(2):
            value = kv_ref[number, :, pl.ds((2 + h) * dim, dim)]
            accumulate(acc_ref, h, rows, parts[h][1], parts[h][0], value)

    visit_prompts(data_count, starts, table, base, size, prepare, update)
    for head in range(2):
        cols = pl.ds(head * dim, dim)
        total = acc_ref[head, :, dim:]
        attended = acc_ref[head, :, :dim] / total
        wide_ref[:, cols] = attended
        o_ref[:, cols] = attended.astype(BF)
        lse_ref[head] = m_ref[head] + jnp.log2(total)


def prompt_scratch(prompt_all, width, dim):
    shards, head_count, block, column = prompt_all.shape
    pieces = PLEN // block
    count = shards // pieces
    return [
        pltpu.VMEM((count, pieces, head_count, block, column), BF),
        pltpu.VMEM((width, 4 * dim), BF),
        pltpu.VMEM((count, -(-PLEN // 128) * 128, 4 * dim), BF),
    ], [pltpu.SMEM((count,), jnp.int32), pltpu.SemaphoreType.DMA((count,))]


def prompt_forward(
    meta, starts, table, q_own, ids_row, state, prompt_all, in_own, in_other, factor, data_count
):
    size, dim = q_own.shape[0], q_own.shape[1] // 2
    buffers, flags = prompt_scratch(prompt_all, in_own.shape[1], dim)
    return pl.pallas_call(
        functools.partial(prompt_forward_kernel, data_count, factor),
        out_shape=(
            jax.ShapeDtypeStruct((size, 2 * dim), BF),
            jax.ShapeDtypeStruct((size, 2 * dim), F32),
            jax.ShapeDtypeStruct((2, size, 128), F32),
        ),
        in_specs=[smem()] * 3 + [vmem()] * 4 + [anywhere()] + [vmem()] * 2,
        out_specs=[vmem()] * 3,
        scratch_shapes=[
            pltpu.VMEM(state[0].shape, F32),
            pltpu.VMEM(state[1].shape, F32),
            *buffers,
            pltpu.VMEM((size, 128), F32),
            *flags,
        ],
        compiler_params=params(20 << 20),
        cost_estimate=cost(4e9, 8e6, 2e6),
        name="prompt_forward",
    )(meta, starts, table, q_own, ids_row, *state, prompt_all, in_own, in_other)


def norm_parts(value):
    center = value - jnp.mean(value, axis=-1, keepdims=True)
    scale = lax.rsqrt(jnp.mean(center * center, axis=-1, keepdims=True) + 1e-05)
    return center * scale, scale


def norm_back(grad, unit, scale, gain):
    part = grad * gain
    return scale * (
        part
        - jnp.mean(part, axis=-1, keepdims=True)
        - unit * jnp.mean(part * unit, axis=-1, keepdims=True)
    )


def feed_kernel(
    meta,
    mine,
    theirs,
    wide_ref,
    lse_ref,
    tok_ref,
    cot_ref,
    w_ref,
    down_bias,
    gains,
    shifts,
    out_ref,
    da_ref,
    pack_ref,
    delta_ref,
):
    size, width = tok_ref.shape[1:]
    dim = mine.shape[1] // 2
    heads = w_ref.shape[0]
    hid = (w_ref.shape[1] - PACK - dim) // 2
    batch, parity = meta[1], meta[2]
    even = parity == 0
    spot = [((q % 2) ^ parity) * 2 + ((q // 2) ^ batch) for q in range(heads)]
    place_out = slice(hid, hid + dim)
    place_up = slice(hid + dim, 2 * hid + dim)
    place_bias = 2 * hid + dim
    sub = min(256, size)
    rows_per = size // (2 * dim)
    pack_ref[pl.ds(size, STATS), :] = jnp.zeros((STATS, 2 * dim), BF)
    g0, g1 = gains[0:1, :], gains[1:2, :]
    for part in range(size // sub):
        rows = pl.ds(part * sub, sub)
        a, b = mine[rows, :], theirs[rows, :]
        first = jnp.where(even, a, b)
        second = jnp.where(even, b, a)
        attn = mm(first[:, :dim], w_ref[spot[0], place_out, :])
        attn += mm(second[:, :dim], w_ref[spot[1], place_out, :])
        attn += mm(first[:, dim:], w_ref[spot[2], place_out, :])
        attn += mm(second[:, dim:], w_ref[spot[3], place_out, :])
        unit_one, scale_one = norm_parts(tok_ref[batch, rows, :].astype(F32) + attn)
        normed = unit_one * g0 + shifts[0:1, :]
        normed_low = normed.astype(BF)
        branch = down_bias[...]
        slopes = []
        for q in range(heads):
            bias = (
                w_ref[spot[q], place_bias : place_bias + 1, :hid].astype(F32)
                + w_ref[spot[q], place_bias : place_bias + 1, hid : 2 * hid].astype(F32)
                + w_ref[spot[q], place_bias + 1 : place_bias + 2, :hid].astype(F32)
            )
            pre = mm_nt(normed_low, w_ref[spot[q], place_up, :]) + bias
            cdf = 0.5 * (1.0 + lax.erf(pre * 0.7071067811865476))
            slopes.append(cdf + pre * (jnp.exp(-0.5 * pre * pre) * 0.3989422804014327))
            branch = branch + mm((pre * cdf).astype(BF), w_ref[spot[q], :hid, :])
        unit_two, scale_two = norm_parts(normed + branch)
        out_ref[rows, :] = unit_two * g1 + shifts[1:2, :]
        grad_mixed = norm_back(cot_ref[batch, rows, :].astype(F32), unit_two, scale_two, g1)
        mixed_low = grad_mixed.astype(BF)
        grad_normed = grad_mixed
        for q in range(heads):
            grad_pre = mm_nt(mixed_low, w_ref[spot[q], :hid, :]) * slopes[q]
            grad_normed = grad_normed + mm(grad_pre.astype(BF), w_ref[spot[q], place_up, :])
        grad_sum = norm_back(grad_normed, unit_one, scale_one, g0)
        da_ref[rows, :] = grad_sum
        sum_low = grad_sum.astype(BF)
        for head in range(2):
            cols = pl.ds(head * dim, dim)
            grad_out = mm_nt(sum_low, w_ref[head ^ batch, place_out, :]).astype(BF)
            pack_ref[rows, cols] = grad_out
            delta = jnp.sum(grad_out.astype(F32) * wide_ref[rows, cols], axis=1, keepdims=True)
            delta_ref[head, rows, :] = jnp.broadcast_to(delta, (sub, 128))
    for head in range(2):
        for kind, ref in enumerate((lse_ref, delta_ref)):
            for place, term in enumerate(split3(jnp.transpose(ref[head])[0:1, :])):
                for i in range(rows_per):
                    row = size + ((head * 2 + kind) * 3 + place) * rows_per + i
                    pack_ref[row : row + 1, :] = term[:, i * 2 * dim : (i + 1) * 2 * dim]


def feed(meta, mine, theirs, wide_out, lse, tokens, cotangent, w, down_bias, gains, shifts):
    size, width = tokens.shape[1:]
    dim = mine.shape[1] // 2
    return pl.pallas_call(
        feed_kernel,
        out_shape=(
            jax.ShapeDtypeStruct((size, width), F32),
            jax.ShapeDtypeStruct((size, width), F32),
            jax.ShapeDtypeStruct((size + STATS, 2 * dim), BF),
            jax.ShapeDtypeStruct((2, size, 128), F32),
        ),
        in_specs=[smem()] + [vmem()] * 10,
        out_specs=[vmem()] * 4,
        compiler_params=params(10 << 20),
        cost_estimate=cost(3e9, 8e6, 1e6),
        name="feed",
    )(meta, mine, theirs, wide_out, lse, tokens, cotangent, w, down_bias, gains, shifts)


def query_grad_kernel(
    data_count,
    factor,
    meta,
    starts,
    table,
    q_ref,
    ids_ref,
    lse_ref,
    delta_ref,
    do_ref,
    mine_low,
    theirs_low,
    mine_high,
    theirs_high,
    in_own,
    in_other,
    prompt_hbm,
    dq_ref,
    acc_ref,
    x_ref,
    line_ref,
    raw_ref,
    w_ref,
    kv_ref,
    id_ref,
    state,
    sem,
):
    size, dim = q_ref.shape[0], q_ref.shape[1] // 2
    base = meta[0] * size
    fetch_prompts(data_count, starts, table, base, size, prompt_hbm, raw_ref, state, sem)
    join_weights(meta, in_own, in_other, w_ref, 1)
    first, last = key_range(starts, base, base + size, data_count)
    acc_ref[...] = jnp.zeros(acc_ref.shape, F32)
    id_ref[...] = column_of(ids_ref[...])

    def low_grads(h, rows, scores, shift, grads):
        count = scores.shape[1] // 128
        probs = jnp.exp2(scores * factor - wide(shift, count))
        return (probs * (grads - wide(delta_ref[h, rows, :], count))).astype(BF)

    def step(shard, carry):
        line = load_shard(
            meta, shard, (mine_low, theirs_low, mine_high, theirs_high), x_ref, line_ref
        )
        kv = mm(x_ref[...], w_ref[...]).astype(BF)
        mask = wide(id_ref[...], size // 128) == line
        rows = pl.ds(0, size)
        raw, grads, low = [], [], []
        for h in range(2):
            raw.append(mm_nt(q_ref[:, h * dim : (h + 1) * dim], kv[:, h * dim : (h + 1) * dim]))
            grads.append(
                mm_nt(
                    do_ref[pl.ds(0, size), h * dim : (h + 1) * dim],
                    kv[:, (2 + h) * dim : (3 + h) * dim],
                )
            )
        for h in range(2):
            low.append(
                low_grads(h, rows, jnp.where(mask, raw[h], NEGATIVE), lse_ref[h], grads[h])
            )
        for h in range(2):
            acc_ref[h] += mm(low[h], kv[:, h * dim : (h + 1) * dim])
        return carry

    lax.fori_loop(first // size, (last + size - 1) // size, step, 0)

    def prepare(number):
        project_prompt(number, prompt_hbm, raw_ref, w_ref, kv_ref, state, sem)

    def update(rows, data, number):
        mask = id_ref[rows, :] == data.astype(F32)
        raw, grads, low = [], [], []
        for h in range(2):
            cols = pl.ds(h * dim, dim)
            raw.append(mm_nt(q_ref[rows, cols], kv_ref[number, :, cols]))
            grads.append(mm_nt(do_ref[rows, cols], kv_ref[number, :, pl.ds((2 + h) * dim, dim)]))
        for h in range(2):
            shift = jnp.where(mask, lse_ref[h, rows, :], -NEGATIVE)
            low.append(low_grads(h, rows, prompt_mask(raw[h]), shift, grads[h]))
        for h in range(2):
            acc_ref[h, rows, :] += mm(low[h], kv_ref[number, :, pl.ds(h * dim, dim)])

    visit_prompts(data_count, starts, table, base, size, prepare, update)
    for head in range(2):
        dq_ref[:, pl.ds(head * dim, dim)] = (acc_ref[head] * dim ** (-0.5)).astype(BF)


def query_grad(
    meta,
    starts,
    table,
    q_own,
    ids_row,
    lse,
    delta,
    pack,
    mine,
    theirs,
    in_own,
    in_other,
    prompt_all,
    factor,
    data_count,
):
    size, dim = q_own.shape[0], q_own.shape[1] // 2
    width = in_own.shape[1]
    buffers, flags = prompt_scratch(prompt_all, width, dim)
    return pl.pallas_call(
        functools.partial(query_grad_kernel, data_count, factor),
        out_shape=jax.ShapeDtypeStruct((size, 2 * dim), BF),
        in_specs=[smem()] * 3 + [vmem()] * 11 + [anywhere()],
        out_specs=vmem(),
        scratch_shapes=[
            pltpu.VMEM((2, size, dim), F32),
            pltpu.VMEM((size, width), BF),
            pltpu.VMEM((1, width), F32),
            *buffers,
            pltpu.VMEM((size, 128), F32),
            *flags,
        ],
        compiler_params=params((16 << 20) + 4 * mine[0].size * 2),
        cost_estimate=cost(6e9, 16e6, 4e6),
        name="query_grad",
    )(
        meta,
        starts,
        table,
        q_own,
        ids_row,
        lse,
        delta,
        pack,
        mine[0],
        theirs[0],
        mine[1],
        theirs[1],
        in_own,
        in_other,
        prompt_all,
    )


def half_shard(meta, index, q_ref, ids_ref, low_ref, high_ref):
    slots, rows, double = low_ref.shape
    half = q_ref.shape[1]
    size = rows - STATS
    shard, part = index // 2, index % 2
    slot = slot_of(shard ^ meta[0], meta[2], 2 * slots)
    other = slot_of(shard ^ meta[0], 1 - meta[2], 2 * slots)
    query = q_ref[jnp.where(part == meta[2], slot * 2, other * 2 + 1)]
    in_low = slot < slots
    place_low, place_high = jnp.minimum(slot, slots - 1), jnp.maximum(slot - slots, 0)
    span = pl.ds(pl.multiple_of(part * half, half), half)
    grad = jnp.where(in_low, low_ref[place_low, span, :], high_ref[place_high, span, :])
    line = ids_ref[slot]
    line = jnp.where(part == 0, line[:, :half], line[:, half : 2 * half])
    tail = pl.ds(size, STATS)
    stats = jnp.where(in_low, low_ref[place_low, tail, :], high_ref[place_high, tail, :])
    stats = stats.astype(F32)
    rows_per = size // double

    def stat(head, kind):
        total = 0.0
        for place in range(3):
            row = ((head * 2 + kind) * 3 + place) * rows_per
            term = stats[row : row + 1, :]
            for i in range(1, rows_per):
                term = jnp.where(part == i, stats[row + i : row + i + 1, :], term)
            total = total + term
        return total

    return query, grad, line, stat


def key_update(query, grad, kv_ref, mask, rows_mask, stat, factor, dk_ref, dv_ref):
    dim = query.shape[1] // 2
    cols = [slice(h * dim, (h + 1) * dim) for h in range(2)]
    raw = [mm_nt(kv_ref[:, cols[h]], query[:, cols[h]]) for h in range(2)]
    grads = [mm_nt(kv_ref[:, pl.ds((2 + h) * dim, dim)], grad[:, cols[h]]) for h in range(2)]
    probs, low = [], []
    for h in range(2):
        shift = stat(h, 0)
        scores = raw[h]
        if rows_mask is None:
            shift = jnp.where(mask, shift, -NEGATIVE)
        else:
            scores = jnp.where(rows_mask, scores, NEGATIVE)
        p = jnp.exp2(scores * factor - shift)
        probs.append(p.astype(BF))
        low.append((p * (grads[h] - stat(h, 1))).astype(BF))
    for h in range(2):
        dv_ref[:, cols[h]] += mm(probs[h], grad[:, cols[h]])
        dk_ref[:, cols[h]] += mm(low[h], query[:, cols[h]])


def prompt_grad_kernel(
    data_count,
    factor,
    meta,
    starts,
    table,
    q_ref,
    ids_ref,
    low_ref,
    high_ref,
    own_ref,
    in_own,
    in_other,
    keep_ref,
    send_ref,
    dk_ref,
    dv_ref,
    w_ref,
    kv_ref,
):
    half = q_ref.shape[1]
    block, width = own_ref.shape
    dim = in_own.shape[2]
    number = meta[0] * block // PLEN
    dk_ref[...] = jnp.zeros(dk_ref.shape, F32)
    dv_ref[...] = jnp.zeros(dv_ref.shape, F32)
    join_weights(meta, in_own, in_other, w_ref, 1)
    kv_ref[...] = mm(own_ref[...], w_ref[...]).astype(BF)

    def visit(data, carry):
        begin, end = starts[data], starts[data + 1]

        @pl.when((table[data] == number) & (begin < end))
        def _():
            def step(index, inner):
                query, grad, line, stat = half_shard(meta, index, q_ref, ids_ref, low_ref, high_ref)
                key_update(
                    query, grad, kv_ref, line == data.astype(F32), None, stat, factor, dk_ref, dv_ref
                )
                return inner

            lax.fori_loop(begin // half, (end + half - 1) // half, step, 0)

        return carry

    lax.fori_loop(0, data_count, visit, 0)
    grads = jnp.concatenate(
        [(dk_ref[...] * dim ** (-0.5)).astype(BF), dv_ref[...].astype(BF)], axis=1
    )
    split = width // 2
    parity = meta[2]
    send = w_ref[pl.ds(pl.multiple_of((1 - parity) * split, split), split), :]
    keep = w_ref[pl.ds(pl.multiple_of(parity * split, split), split), :]
    send_ref[...] = mm_nt(grads, send).astype(BF)
    keep_ref[...] = mm_nt(grads, keep)


def prompt_grad(meta, starts, table, q_all, ids_all, packs, own, in_own, in_other, factor, data_count):
    block, width = own.shape
    dim = in_own.shape[2]
    return pl.pallas_call(
        functools.partial(prompt_grad_kernel, data_count, factor),
        out_shape=(
            jax.ShapeDtypeStruct((block, width // 2), F32),
            jax.ShapeDtypeStruct((block, width // 2), BF),
        ),
        in_specs=[smem()] * 3 + [vmem()] * 7,
        out_specs=[vmem(), vmem()],
        scratch_shapes=[
            pltpu.VMEM((block, 2 * dim), F32),
            pltpu.VMEM((block, 2 * dim), F32),
            pltpu.VMEM((width, 4 * dim), BF),
            pltpu.VMEM((block, 4 * dim), BF),
        ],
        compiler_params=params(q_all.size * 2 + packs[0].size * 4),
        cost_estimate=cost(6e9, 16e6, 4e6),
        name="prompt_grad",
    )(meta, starts, table, q_all, ids_all, *packs, own, in_own, in_other)


def token_grad_kernel(
    data_count,
    factor,
    meta,
    starts,
    q_ref,
    ids_ref,
    low_ref,
    high_ref,
    tok_ref,
    own_ids,
    dq_ref,
    in_own,
    in_other,
    out_ref,
    dk_ref,
    dv_ref,
    w_ref,
    kv_ref,
    id_ref,
):
    size = tok_ref.shape[1]
    half = q_ref.shape[1]
    dim = in_own.shape[2]
    base = meta[0] * size
    first, last = key_range(starts, base, base + size, data_count)
    dk_ref[...] = jnp.zeros(dk_ref.shape, F32)
    dv_ref[...] = jnp.zeros(dv_ref.shape, F32)
    join_weights(meta, in_own, in_other, w_ref, 0)
    kv_ref[...] = mm(tok_ref[meta[1]], w_ref[:, 2 * dim :]).astype(BF)
    id_ref[...] = column_of(own_ids[...])

    def step(index, carry):
        query, grad, line, stat = half_shard(meta, index, q_ref, ids_ref, low_ref, high_ref)
        mask = wide(id_ref[...], half // 128) == line
        key_update(query, grad, kv_ref, None, mask, stat, factor, dk_ref, dv_ref)
        return carry

    lax.fori_loop(first // half, (last + half - 1) // half, step, 0)
    grads = jnp.concatenate(
        [dq_ref[...], (dk_ref[...] * dim ** (-0.5)).astype(BF), dv_ref[...].astype(BF)], axis=1
    )
    out_ref[...] = mm_nt(grads, w_ref[...]).astype(BF)


def token_grad(
    meta, starts, q_all, ids_all, packs, tokens, ids_row, dq, in_own, in_other, factor, data_count
):
    size, width = tokens.shape[1:]
    dim = in_own.shape[2]
    return pl.pallas_call(
        functools.partial(token_grad_kernel, data_count, factor),
        out_shape=jax.ShapeDtypeStruct((size, width), BF),
        in_specs=[smem()] * 2 + [vmem()] * 9,
        out_specs=vmem(),
        scratch_shapes=[
            pltpu.VMEM((size, 2 * dim), F32),
            pltpu.VMEM((size, 2 * dim), F32),
            pltpu.VMEM((width, 6 * dim), BF),
            pltpu.VMEM((size, 4 * dim), BF),
            pltpu.VMEM((size, 128), F32),
        ],
        compiler_params=params(q_all.size * 2 + packs[0].size * 4),
        cost_estimate=cost(4e9, 16e6, 4e6),
        name="token_grad",
    )(meta, starts, q_all, ids_all, *packs, tokens, ids_row, dq, in_own, in_other)


def per_device(
    tokens,
    cotangent,
    dataset_ids,
    prompt_map,
    attn_in,
    attn_out,
    up_weight,
    up_bias,
    down_weight,
    down_bias,
    norm_gains,
    norm_shifts,
    prompts,
    moment_one,
    moment_two,
    step_count,
):
    size, width = tokens.shape[1:]
    dim = attn_in.shape[2]
    hid = up_weight.shape[1]
    data_count = prompt_map.shape[1]
    row_count = lax.axis_size("rows")
    head_count = lax.axis_size("head")
    factor = dim ** (-0.5) * LOG2E
    row = lax.axis_index("rows")
    head = lax.axis_index("head")
    batch, parity = head // 2, head % 2
    half = size // 2
    meta = jnp.stack([row, batch, parity]).astype(jnp.int32)

    ids = jnp.where(batch == 0, dataset_ids[0], dataset_ids[1])
    table = jnp.where(batch == 0, prompt_map[0], prompt_map[1])
    ids_row = ids.astype(F32).reshape(1, size)
    tok_half = lax.dynamic_slice(tokens, (batch, parity * half, 0), (1, half, width))[0]
    id_rows = jnp.broadcast_to(ids.astype(BF)[None, :], (PACK, size))
    shard = jnp.concatenate([tok_half, id_rows], axis=0)
    prompt_low = prompts.astype(BF)
    column = width // head_count
    prompt_own = lax.dynamic_slice_in_dim(prompt_low, head * column, column, 1)
    prompt_all = lax.all_gather(prompt_own, BOTH, axis=0, tiled=False)
    prompt_all = prompt_all.reshape(row_count, head_count, prompt_own.shape[0], column)
    mine = gather_rows(shard, row_count, head_count)
    theirs = [swap_head(part, 1, head_count) for part in mine]
    in_other = swap_head(attn_in, 2, head_count)

    bias_high = lax.reduce_precision(up_bias, 8, 7)
    bias_rest = up_bias - bias_high
    bias_mid = lax.reduce_precision(bias_rest, 8, 7)
    bias_low = bias_rest - bias_mid
    bias_rows = jnp.concatenate([bias_high, bias_mid, bias_low, bias_low]).astype(BF)
    bias_rows = jnp.pad(bias_rows.reshape(-1, width), ((0, PACK - 4 * hid // width), (0, 0)))
    w_own = jnp.concatenate([down_weight, attn_out, up_weight.T, bias_rows], axis=0)
    w_pair = jnp.stack([w_own, swap_head(w_own, 2, head_count)])
    layer_weights = jnp.concatenate([w_pair, swap_head(w_pair, 1, head_count)], axis=0)

    ids_all = jnp.concatenate([part[:, half, :size] for part in mine], axis=0).astype(F32)
    numbers = jnp.arange(data_count + 1, dtype=jnp.int32).astype(F32)
    starts = jnp.sum((ids_all.reshape(1, -1) < numbers[:, None]).astype(jnp.int32), axis=1)
    ids_all = ids_all.reshape(row_count, 1, size)
    q_own, *state = token_forward(
        meta, starts, tokens, ids_row, mine, theirs, attn_in, in_other, factor, data_count
    )
    q_all = project_query(meta, mine, theirs, attn_in, in_other)
    o_mine, wide_out, lse = prompt_forward(
        meta, starts, table, q_own, ids_row, state, prompt_all, attn_in, in_other, factor, data_count
    )
    o_theirs = swap_head(o_mine, 1, head_count)
    out, grad_sum, pack, delta = feed(
        meta,
        o_mine,
        o_theirs,
        wide_out,
        lse,
        tokens,
        cotangent,
        layer_weights,
        down_bias.reshape(1, width),
        norm_gains,
        norm_shifts,
    )
    out_other = swap_head(out, 2, head_count)
    layer_out = jnp.stack(
        [jnp.where(batch == 0, out, out_other), jnp.where(batch == 0, out_other, out)]
    )

    packs = gather_rows(pack, row_count, head_count)
    dq = query_grad(
        meta,
        starts,
        table,
        q_own,
        ids_row,
        lse,
        delta,
        pack,
        mine,
        theirs,
        attn_in,
        in_other,
        prompt_all,
        factor,
        data_count,
    )
    packs, layer_out, dq = lax.optimization_barrier((packs, layer_out, dq))
    keep, send = prompt_grad(
        meta, starts, table, q_all, ids_all, packs, prompt_low, attn_in, in_other, factor, data_count
    )

    pair = keep + swap_head(send, 1, head_count).astype(F32)
    pair_low = lax.reduce_precision(pair, 8, 7).astype(BF)
    dq, pair_low = lax.optimization_barrier((dq, pair_low))
    pair_other = swap_head(pair_low, 2, head_count)
    token_part = token_grad(
        meta, starts, q_all, ids_all, packs, tokens, ids_row, dq, attn_in, in_other, factor, data_count
    )
    full_low = pair_low.astype(F32) + pair_other.astype(F32)
    full_low = lax.reduce_precision(full_low, 8, 7).astype(BF)
    squares = jnp.sum(full_low.astype(F32) ** 2).reshape(1, 1)
    squares = jnp.broadcast_to(squares, (8, 128))
    squares = squares + swap_head(squares, 1, head_count)
    mask = 1
    while mask < row_count:
        squares = squares + lax.ppermute(
            squares, "rows", [(i, i ^ mask) for i in range(row_count)]
        )
        mask = mask * 2
    grad_norm = jnp.sqrt(squares[0, 0])
    full_other = swap_head(full_low, 1, head_count)
    prompt_grads = jnp.concatenate(
        [jnp.where(parity == 0, full_low, full_other), jnp.where(parity == 0, full_other, full_low)],
        axis=1,
    ).astype(F32)
    clipped = prompt_grads * jnp.minimum(1.0, CLIP_NORM / (grad_norm + 1e-06))
    step_value = step_count.astype(F32)
    new_one = BETA_ONE * moment_one + (1.0 - BETA_ONE) * clipped
    new_two = BETA_TWO * moment_two + (1.0 - BETA_TWO) * clipped * clipped
    first_hat = new_one / (1.0 - jnp.power(BETA_ONE, step_value))
    second_hat = new_two / (1.0 - jnp.power(BETA_TWO, step_value))
    new_prompts = prompts * (1.0 - LEARNING_RATE * DECAY_RATE) - LEARNING_RATE * first_hat / (
        jnp.sqrt(second_hat) + EPSILON
    )

    core_sum = token_part.astype(F32) + swap_head(token_part, 1, head_count).astype(F32)
    total = lax.reduce_precision(grad_sum + core_sum, 8, 7).astype(BF)
    mine_half = lax.dynamic_slice_in_dim(total, parity * half, half, 0)
    other_half = swap_head(mine_half, 2, head_count)
    other_rest = swap_head(other_half, 1, head_count)
    other = jnp.concatenate(
        [
            jnp.where(parity == 0, other_half, other_rest),
            jnp.where(parity == 0, other_rest, other_half),
        ],
        axis=0,
    )
    input_grad = jnp.stack(
        [jnp.where(batch == 0, total, other), jnp.where(batch == 0, other, total)]
    ).astype(F32)
    return (layer_out, input_grad, clipped, grad_norm, new_one, new_two, new_prompts)


def solution(mesh):
    in_specs = (
        P(None, "rows", None),
        P(None, "rows", None),
        P(None, "rows"),
        P(),
        P(None, None, "head"),
        P("head", None),
        P(None, "head"),
        P("head"),
        P("head", None),
        P(),
        P(),
        P(),
        P("rows", None),
        P("rows", None),
        P("rows", None),
        P(),
    )
    out_specs = (
        P(None, "rows", None),
        P(None, "rows", None),
        P("rows", None),
        P(),
        P("rows", None),
        P("rows", None),
        P("rows", None),
    )
    return jax.shard_map(
        per_device, mesh=mesh, in_specs=in_specs, out_specs=out_specs, check_vma=False
    )
```

```python
import functools

import jax
import jax.numpy as jnp
from jax import lax
from jax.experimental import pallas as pl
from jax.experimental.pallas import tpu as pltpu
from jax.sharding import PartitionSpec as P

PLEN = 1000
NEGATIVE = -1e30
BETA_ONE = 0.9
BETA_TWO = 0.999
LEARNING_RATE = 0.5
DECAY_RATE = 0.01
EPSILON = 1e-08
CLIP_NORM = 1.0
LOG2E = 1.4426950408889634
PACK = 16
STATS = 32
VMEM_LIMIT = 60 * 1024 * 1024
BF = jnp.bfloat16
F32 = jnp.float32
BOTH = ("rows", "head")


def params(*operands, spare=20 << 20):
    held = sum(x.size * x.dtype.itemsize for x in operands)
    return pltpu.CompilerParams(vmem_limit_bytes=min(VMEM_LIMIT, held + spare))


def cost(flops, bytes_accessed, transcendentals=0):
    return pl.CostEstimate(
        flops=int(flops), bytes_accessed=int(bytes_accessed), transcendentals=int(transcendentals)
    )


def mm(a, b):
    return lax.dot_general(a, b, (((1,), (0,)), ((), ())), preferred_element_type=F32)


def mm_nt(a, b):
    return lax.dot_general(a, b, (((1,), (1,)), ((), ())), preferred_element_type=F32)


def split3(value):
    high = value.astype(BF)
    rest = value - high.astype(F32)
    mid = rest.astype(BF)
    low = (rest - mid.astype(F32)).astype(BF)
    return high, mid, low


def bit_orders(row_count):
    bits = row_count.bit_length() - 1
    return ([0] + list(range(bits - 1, 0, -1)), list(range(bits - 1, 0, -1)) + [0])


def prompt_orders(row_count):
    bits = row_count.bit_length() - 1
    if bits < 2:
        return bit_orders(row_count)
    high = list(range(bits - 1, 1, -1))
    return (high + [0, 1], [1] + high + [0])


def slot_of(offset, parity, orders):
    def mapped(order):
        total = 0
        for place, bit in enumerate(order):
            total = total + (((offset >> bit) & 1) << place)
        return total

    return jnp.where(parity == 0, mapped(orders[0]), mapped(orders[1]))


def gather_stage(held, place, orders, row_count, head_count):
    pairs = []
    for row in range(row_count):
        for head in range(head_count):
            bit = orders[head % 2][place]
            pairs.append((row * head_count + head, (row ^ (1 << bit)) * head_count + head))
    return lax.ppermute(held, BOTH, pairs)


def gather_rows(block, row_count, head_count, before_send):
    held = block[None]
    orders = bit_orders(row_count)
    stages = len(orders[0])
    for place in range(stages):
        held = before_send(stages - place, held)
        other = gather_stage(held, place, orders, row_count, head_count)
        if place < stages - 1:
            held = jnp.concatenate([held, other], axis=0)
    return held, other


def xor_sum(value, row_count, head_count, after):
    def moved(mask):
        count = row_count * head_count
        return lax.ppermute(value, BOTH, [(i, i ^ mask) for i in range(count)])

    masks = [1]
    bit = head_count
    while bit < row_count * head_count:
        masks.append(bit)
        bit = bit * 2
    done = 0
    while masks:
        if len(masks) == 1:
            value = value + moved(masks[0])
        else:
            first, second, both = (moved(m) for m in (masks[0], masks[1], masks[0] ^ masks[1]))
            value = (value + first) + (second + both)
        masks = masks[2:]
        done = done + 1
        value = after(done, value)
    return value


def swap_head(value, mask, head_count):
    return lax.ppermute(value, "head", [(i, i ^ mask) for i in range(head_count)])


def smem():
    return pl.BlockSpec(memory_space=pltpu.SMEM)


def vmem():
    return pl.BlockSpec(memory_space=pltpu.VMEM)


def hbm():
    return pl.BlockSpec(memory_space=pltpu.HBM)


def join_weights(meta, own, other, target, first):
    dim = own.shape[2]
    for kind in range(first, own.shape[0]):
        for place in range(2):
            column = ((kind - first) * 2 + place) * dim
            target[:, column : column + dim] = jnp.where(meta[1] == place, own[kind], other[kind])


def wide(value, count):
    return jnp.concatenate([value] * count, axis=1)


def column_of(line):
    return jnp.transpose(jnp.broadcast_to(line, (128, line.shape[1])))


def project_query_kernel(meta, a, b, c, d, own, other, q_out):
    half = a.shape[1] - PACK
    dim = own.shape[2]
    weights = jnp.concatenate(
        [jnp.where(meta[1] == place, own[0], other[0]) for place in range(2)], axis=1
    )
    for high, pair in enumerate(((a, b), (c, d))):
        for place, ref in enumerate(pair):
            q_out[high, 0, place] = mm(ref[0, :half], weights).astype(BF)


def project_query(meta, mine, theirs, in_own, in_other):
    slots, rows, width = mine[0].shape
    half = rows - PACK
    dim = in_own.shape[2]
    block = pl.BlockSpec((1, rows, width), lambda g: (g, 0, 0))
    whole = pl.BlockSpec((1,) + in_own.shape[1:], lambda g: (0, 0, 0))
    out = pl.pallas_call(
        project_query_kernel,
        out_shape=jax.ShapeDtypeStruct((2, slots, 2, half, 2 * dim), BF),
        grid=(slots,),
        in_specs=[smem()] + [block] * 4 + [whole] * 2,
        out_specs=pl.BlockSpec((2, 1, 2, half, 2 * dim), lambda g: (0, g, 0, 0, 0)),
        compiler_params=params(),
        cost_estimate=cost(8 * slots * half * width * 2 * dim, 8 * slots * half * width),
        name="project_query",
    )(meta, mine[0], theirs[0], mine[1], theirs[1], in_own, in_other)
    return out.reshape(4 * slots, half, 2 * dim)


def key_range(starts, low, high, data_count):
    first = jnp.int32(1 << 30)
    last = jnp.int32(0)
    for data in range(data_count):
        begin, end = starts[data], starts[data + 1]
        hit = (begin < high) & (end > low) & (begin < end)
        first = jnp.where(hit, jnp.minimum(first, begin), first)
        last = jnp.where(hit, jnp.maximum(last, end), last)
    return first, last


def shard_copies(meta, shard, gathered, x_ref, sem):
    slots = gathered[0].shape[0]
    copies = []
    for place in range(2):
        slot = slot_of(shard ^ meta[0], meta[2] ^ place, bit_orders(2 * slots))
        for bank in range(2):
            here = (slot < slots) if bank == 0 else (slot >= slots)
            source = gathered[place * 2 + bank]
            copy = pltpu.make_async_copy(
                source.at[jnp.where(here, slot - bank * slots, 0)],
                x_ref.at[shard, place],
                sem.at[shard, place],
            )
            copies.append((here, copy))
    return copies


def fetch_shards(meta, first, last, gathered, x_ref, sem):
    def start(shard, carry):
        for here, copy in shard_copies(meta, shard, gathered, x_ref, sem):

            @pl.when(here)
            def _():
                copy.start()

        return carry

    lax.fori_loop(first, last, start, 0)


def load_shard(meta, shard, gathered, x_ref, sem):
    half = x_ref.shape[2] - PACK
    parity = meta[2]
    for place in range(2):
        pltpu.make_async_copy(gathered[0].at[0], x_ref.at[shard, place], sem.at[shard, place]).wait()
    line = x_ref[shard, 0, half : half + 1, :].astype(F32)
    first, second = line[:, :half], line[:, half : 2 * half]
    line = jnp.concatenate(
        [jnp.where(parity == 0, first, second), jnp.where(parity == 0, second, first)], axis=1
    )
    return jnp.concatenate([x_ref[shard, 0, :half, :], x_ref[shard, 1, :half, :]], axis=0), line


def online(scores, factor, mask, m_ref, place):
    old_max = m_ref[place]
    size = old_max.shape[0]
    top = jnp.broadcast_to(jnp.max(scores, axis=1, keepdims=True) * factor, (size, 128))
    new_max = jnp.maximum(old_max, top)
    shift = new_max
    if mask is not None:
        new_max = jnp.where(mask, new_max, old_max)
        shift = jnp.where(mask, new_max, -NEGATIVE)
    m_ref[place] = new_max
    probs = jnp.exp2(scores * factor - wide(shift, scores.shape[1] // 128))
    return probs.astype(BF), jnp.exp2(old_max - new_max)


def accumulate(acc_ref, place, alpha, probs, value):
    with_ones = jnp.concatenate([value, jnp.ones((value.shape[0], 128), BF)], axis=1)
    acc_ref[place] = acc_ref[place] * wide(alpha, with_ones.shape[1] // 128) + mm(probs, with_ones)


def token_forward_kernel(
    data_count,
    factor,
    meta,
    starts,
    ids_ref,
    in_own,
    in_other,
    tok_hbm,
    mine_low,
    mine_high,
    theirs_low,
    theirs_high,
    q_ref,
    m_ref,
    acc_ref,
    w_ref,
    x_ref,
    id_ref,
    tok_ref,
    sem,
    tok_sem,
):
    size, dim = tok_ref.shape[1], in_own.shape[2]
    tok_copy = pltpu.make_async_copy(tok_hbm, tok_ref, tok_sem)
    tok_copy.start()
    base = meta[0] * size
    first, last = key_range(starts, base, base + size, data_count)
    first, last = first // size, (last + size - 1) // size
    gathered = (mine_low, mine_high, theirs_low, theirs_high)
    fetch_shards(meta, first, last, gathered, x_ref, sem)
    join_weights(meta, in_own, in_other, w_ref, 0)
    tok_copy.wait()
    for slot in range(2):
        q_ref[slot] = mm(tok_ref[meta[1] ^ slot], w_ref[:, : 2 * dim]).astype(BF)
    m_ref[...] = jnp.full(m_ref.shape, NEGATIVE, F32)
    acc_ref[...] = jnp.zeros(acc_ref.shape, F32)
    id_ref[...] = column_of(ids_ref[meta[1]])
    rows = pl.ds(0, size)

    def step(shard, carry):
        raw_rows, line = load_shard(meta, shard, gathered, x_ref, sem)
        kv = mm(raw_rows, w_ref[:, 2 * dim :]).astype(BF)
        mask = wide(id_ref[...], size // 128) == line
        raw = [
            mm_nt(q_ref[0, :, h * dim : (h + 1) * dim], kv[:, h * dim : (h + 1) * dim])
            for h in range(2)
        ]
        parts = [
            online(jnp.where(mask, raw[h], NEGATIVE), factor, None, m_ref, (h, rows))
            for h in range(2)
        ]
        for h in range(2):
            value = kv[:, (2 + h) * dim : (3 + h) * dim]
            accumulate(acc_ref, (h, rows), parts[h][1], parts[h][0], value)
        return carry

    lax.fori_loop(first, last, step, 0)


def shard_scratch(banks):
    slots, rows, width = banks[0].shape
    return pltpu.VMEM((2 * slots, 2, rows, width), BF)


def token_forward(meta, starts, tokens, ids_rows, mine, theirs, in_own, in_other, factor, data_count):
    size, width = tokens.shape[1:]
    dim = in_own.shape[2]
    return pl.pallas_call(
        functools.partial(token_forward_kernel, data_count, factor),
        out_shape=(
            jax.ShapeDtypeStruct((2, size, 2 * dim), BF),
            jax.ShapeDtypeStruct((2, size, 128), F32),
            jax.ShapeDtypeStruct((2, size, dim + 128), F32),
        ),
        in_specs=[smem(), smem()] + [vmem()] * 3 + [hbm()] * 5,
        out_specs=[vmem()] * 3,
        scratch_shapes=[
            pltpu.VMEM((width, 6 * dim), BF),
            shard_scratch(mine),
            pltpu.VMEM((size, 128), F32),
            pltpu.VMEM(tokens.shape, BF),
            pltpu.SemaphoreType.DMA((2 * mine[0].shape[0], 2)),
            pltpu.SemaphoreType.DMA,
        ],
        compiler_params=params(*mine, *theirs),
        cost_estimate=cost(8e9, 8e6, 2e6),
        name="token_forward",
    )(meta, starts, ids_rows, in_own, in_other, tokens, *mine, *theirs)


def half_rows(block):
    return -(-block // 32) * 16


def fetch_prompts(meta, local, table, sources, raws, state, sem):
    pieces = raws.shape[2]
    slots = sources[0].shape[0]
    for number in range(state.shape[0]):
        state[number] = 0
    for batch in range(2):
        for data in range(table.shape[1]):
            number = table[batch, data]
            used = local[batch, data + 1] > local[batch, data]
            state[number] = jnp.where(used, 1, state[number])

    def start(number, carry):
        @pl.when(state[number] == 1)
        def _():
            for piece in range(pieces):
                for place in range(2):
                    shard = number * pieces + piece
                    slot = slot_of(shard ^ meta[0], meta[2] ^ place, prompt_orders(2 * slots))
                    for bank in range(2):

                        @pl.when((slot < slots) if bank == 0 else (slot >= slots))
                        def _():
                            pltpu.make_async_copy(
                                sources[place * 2 + bank].at[slot - bank * slots],
                                raws.at[place, number, piece],
                                sem.at[place, number, piece],
                            ).start()

        return carry

    lax.fori_loop(0, state.shape[0], start, 0)


def project_prompt(meta, number, sources, raws, w_ref, kv_ref, state, sem):
    pieces, block = raws.shape[2:4]

    @pl.when(state[number] == 1)
    def _():
        even = meta[2] == 0
        for piece in range(pieces):
            for place in range(2):
                pltpu.make_async_copy(
                    sources[0].at[0], raws.at[place, number, piece], sem.at[place, number, piece]
                ).wait()
            a, b = raws[0, number, piece], raws[1, number, piece]
            rows = jnp.concatenate([jnp.where(even, a, b), jnp.where(even, b, a)], axis=1)
            kv_ref[number, pl.ds(piece * block, block), :] = mm(rows, w_ref[...]).astype(BF)
        full = pieces * block
        if full < kv_ref.shape[1]:
            kv_ref[number, full:, :] = jnp.zeros((kv_ref.shape[1] - full, kv_ref.shape[2]), BF)
        state[number] = 2


def prompt_mask(meta, scores, block):
    part = half_rows(block)
    pieces = PLEN // block
    doubled = 2 * part - block
    head = min(128, part) if pieces == 1 else scores.shape[1]
    lanes = lax.broadcasted_iota(jnp.int32, (scores.shape[0], head), 1)
    out = (lanes % part < doubled * meta[1]) | (lanes >= pieces * part)
    first = jnp.where(out, NEGATIVE, scores[:, :head])
    if head == scores.shape[1]:
        return first
    return jnp.concatenate([first, scores[:, head:]], axis=1)


def visit_prompts(meta, local, table, size, prepare, update):
    data_count = table.shape[1]

    def visit(index, carry):
        slot, data = index // data_count, index % data_count
        batch = meta[1] ^ slot
        begin, end = local[batch, data], local[batch, data + 1]

        @pl.when(begin < end)
        def _():
            number = table[batch, data]
            prepare(number)
            low = begin // 128
            count = (end + 127) // 128 - low
            for case in range(1, size // 128 + 1):

                @pl.when(count == case)
                def _():
                    rows = pl.ds(pl.multiple_of(low * 128, 128), case * 128)
                    update(slot, rows, data, number)

        return carry

    lax.fori_loop(0, 2 * data_count, visit, 0)


def store_line(ref, row, line):
    width = ref.shape[1]
    for term in split3(line):
        for low in range(0, line.shape[1], width):
            ref[row : row + 1, :] = term[:, low : low + width]
            row = row + 1
    return row


def load_line(ref, row, length):
    width = ref.shape[1]
    rows_per = length // width
    total = 0.0
    for place in range(3):
        first = row + place * rows_per
        pieces = [ref[first + i : first + i + 1, :].astype(F32) for i in range(rows_per)]
        total = total + jnp.concatenate(pieces, axis=1)
    return total


def prompt_forward_kernel(
    block,
    factor,
    meta,
    local,
    table,
    q_ref,
    ids_ref,
    m_in,
    acc_in,
    in_own,
    in_other,
    mine_low,
    mine_high,
    theirs_low,
    theirs_high,
    wide_ref,
    lse_ref,
    send_ref,
    m_ref,
    acc_ref,
    raws,
    w_ref,
    kv_ref,
    id_ref,
    state,
    sem,
):
    size, dim = q_ref.shape[1], q_ref.shape[2] // 2
    sources = (mine_low, mine_high, theirs_low, theirs_high)
    fetch_prompts(meta, local, table, sources, raws, state, sem)
    join_weights(meta, in_own, in_other, w_ref, 1)
    m_ref[0] = m_in[...]
    acc_ref[0] = acc_in[...]
    m_ref[1] = jnp.full(m_in.shape, NEGATIVE, F32)
    acc_ref[1] = jnp.zeros(acc_in.shape, F32)
    for slot in range(2):
        id_ref[slot] = column_of(ids_ref[meta[1] ^ slot])

    def prepare(number):
        project_prompt(meta, number, sources, raws, w_ref, kv_ref, state, sem)

    def update(slot, rows, data, number):
        mask = id_ref[slot, rows, :] == data.astype(F32)
        raw = [
            mm_nt(q_ref[slot, rows, pl.ds(h * dim, dim)], kv_ref[number, :, pl.ds(h * dim, dim)])
            for h in range(2)
        ]
        parts = [
            online(prompt_mask(meta, raw[h], block), factor, mask, m_ref, (slot, h, rows))
            for h in range(2)
        ]
        for h in range(2):
            value = kv_ref[number, :, pl.ds((2 + h) * dim, dim)]
            accumulate(acc_ref, (slot, h, rows), parts[h][1], parts[h][0], value)

    visit_prompts(meta, local, table, size, prepare, update)
    row = size
    send_ref[pl.ds(size, PACK), :] = jnp.zeros((PACK, 2 * dim), BF)
    for h in range(2):
        cols = pl.ds(h * dim, dim)
        total = acc_ref[0, h, :, dim:]
        wide_ref[:, cols] = acc_ref[0, h, :, :dim] / total
        lse_ref[h] = m_ref[0, h] + jnp.log2(total)
        total = acc_ref[1, h, :, dim:]
        send_ref[pl.ds(0, size), cols] = (acc_ref[1, h, :, :dim] / total).astype(BF)
        line = jnp.transpose(m_ref[1, h] + jnp.log2(total))[0:1, :]
        row = store_line(send_ref, row, line)


def prompt_scratch(prompt_banks, width, dim, block):
    slots, part, columns = prompt_banks[0].shape
    pieces = PLEN // block
    count = 2 * slots // pieces
    return [
        pltpu.VMEM((2, count, pieces, part, columns), BF),
        pltpu.VMEM((width, 4 * dim), BF),
        pltpu.VMEM((count, -(-pieces * part // 128) * 128, 4 * dim), BF),
    ], [pltpu.SMEM((count,), jnp.int32), pltpu.SemaphoreType.DMA((2, count, pieces))]


def prompt_forward(
    meta, local, table, q_own, ids_rows, state, prompt_mine, prompt_theirs, in_own, in_other, factor, block
):
    size, dim = q_own.shape[1], q_own.shape[2] // 2
    buffers, flags = prompt_scratch(prompt_mine, in_own.shape[1], dim, block)
    return pl.pallas_call(
        functools.partial(prompt_forward_kernel, block, factor),
        out_shape=(
            jax.ShapeDtypeStruct((size, 2 * dim), F32),
            jax.ShapeDtypeStruct((2, size, 128), F32),
            jax.ShapeDtypeStruct((size + PACK, 2 * dim), BF),
        ),
        in_specs=[smem()] * 3 + [vmem()] * 6 + [hbm()] * 4,
        out_specs=[vmem()] * 3,
        scratch_shapes=[
            pltpu.VMEM((2,) + state[0].shape, F32),
            pltpu.VMEM((2,) + state[1].shape, F32),
            *buffers,
            pltpu.VMEM((2, size, 128), F32),
            *flags,
        ],
        compiler_params=params(*prompt_mine, *prompt_mine, *prompt_mine, *prompt_mine),
        cost_estimate=cost(4e9, 8e6, 2e6),
        name="prompt_forward",
    )(meta, local, table, q_own, ids_rows, *state, in_own, in_other, *prompt_mine, *prompt_theirs)


def join_kernel(wide_in, lse_in, other_ref, o_ref, wide_ref, lse_ref):
    size, dim = wide_in.shape[0], wide_in.shape[1] // 2
    rows_per = size // (2 * dim)
    for h in range(2):
        cols = pl.ds(h * dim, dim)
        first = lse_in[h]
        second = column_of(load_line(other_ref, size + h * 3 * rows_per, size))
        top = jnp.maximum(first, second)
        first, second = jnp.exp2(first - top), jnp.exp2(second - top)
        total = first + second
        other = other_ref[pl.ds(0, size), cols].astype(F32)
        attended = (first * wide_in[:, cols] + second * other) / total
        wide_ref[:, cols] = attended
        o_ref[:, cols] = attended.astype(BF)
        lse_ref[h] = top + jnp.log2(total)


def join_halves(wide_half, lse_half, other):
    return pl.pallas_call(
        join_kernel,
        out_shape=(
            jax.ShapeDtypeStruct(wide_half.shape, BF),
            jax.ShapeDtypeStruct(wide_half.shape, F32),
            jax.ShapeDtypeStruct(lse_half.shape, F32),
        ),
        in_specs=[vmem()] * 3,
        out_specs=[vmem()] * 3,
        compiler_params=params(),
        cost_estimate=cost(4e6, 3e6, 1e6),
        name="join_halves",
    )(wide_half, lse_half, other)


def norm_parts(value):
    center = value - jnp.mean(value, axis=-1, keepdims=True)
    scale = lax.rsqrt(jnp.mean(center * center, axis=-1, keepdims=True) + 1e-05)
    return center * scale, scale


def norm_back(grad, unit, scale, gain):
    part = grad * gain
    return scale * (
        part
        - jnp.mean(part, axis=-1, keepdims=True)
        - unit * jnp.mean(part * unit, axis=-1, keepdims=True)
    )


def feed_kernel(
    meta,
    mine,
    theirs,
    wide_ref,
    lse_ref,
    tok_ref,
    cot_ref,
    down_bias,
    gains,
    shifts,
    w_own,
    w_along,
    w_core,
    w_far,
    out_ref,
    da_ref,
    pack_ref,
    delta_ref,
    w_ref,
    sem,
):
    size, width = tok_ref.shape[1:]
    dim = mine.shape[1] // 2
    heads = w_ref.shape[0]
    hid = (w_ref.shape[1] - PACK - dim) // 2
    batch, parity = meta[1], meta[2]
    even = parity == 0
    for q in range(heads):
        for place, ref in enumerate((w_own, w_along, w_core, w_far)):

            @pl.when((2 * batch + parity) == (q ^ (0, 2, 1, 3)[place]))
            def _():
                pltpu.make_async_copy(ref, w_ref.at[q], sem.at[q]).start()

    place_out = slice(hid, hid + dim)
    place_up = slice(hid + dim, 2 * hid + dim)
    place_bias = 2 * hid + dim
    sub = min(256, size)
    pack_ref[pl.ds(size, STATS), :] = jnp.zeros((STATS, 2 * dim), BF)
    g0, g1 = gains[0:1, :], gains[1:2, :]
    for q in range(heads):
        pltpu.make_async_copy(w_own, w_ref.at[q], sem.at[q]).wait()
    for part in range(size // sub):
        rows = pl.ds(part * sub, sub)
        a, b = mine[rows, :], theirs[rows, :]
        first = jnp.where(even, a, b)
        second = jnp.where(even, b, a)
        attn = mm(first[:, :dim], w_ref[0, place_out, :])
        attn += mm(second[:, :dim], w_ref[1, place_out, :])
        attn += mm(first[:, dim:], w_ref[2, place_out, :])
        attn += mm(second[:, dim:], w_ref[3, place_out, :])
        unit_one, scale_one = norm_parts(tok_ref[batch, rows, :].astype(F32) + attn)
        normed = unit_one * g0 + shifts[0:1, :]
        normed_low = normed.astype(BF)
        branch = down_bias[...]
        slopes = []
        for q in range(heads):
            bias = (
                w_ref[q, place_bias : place_bias + 1, :hid].astype(F32)
                + w_ref[q, place_bias : place_bias + 1, hid : 2 * hid].astype(F32)
                + w_ref[q, place_bias + 1 : place_bias + 2, :hid].astype(F32)
            )
            pre = mm_nt(normed_low, w_ref[q, place_up, :]) + bias
            cdf = 0.5 * (1.0 + lax.erf(pre * 0.7071067811865476))
            slopes.append(cdf + pre * (jnp.exp(-0.5 * pre * pre) * 0.3989422804014327))
            branch = branch + mm((pre * cdf).astype(BF), w_ref[q, :hid, :])
        unit_two, scale_two = norm_parts(normed + branch)
        out_ref[rows, :] = (unit_two * g1 + shifts[1:2, :]).astype(BF)
        grad_mixed = norm_back(cot_ref[batch, rows, :].astype(F32), unit_two, scale_two, g1)
        mixed_low = grad_mixed.astype(BF)
        grad_normed = grad_mixed
        for q in range(heads):
            grad_pre = mm_nt(mixed_low, w_ref[q, :hid, :]) * slopes[q]
            grad_normed = grad_normed + mm(grad_pre.astype(BF), w_ref[q, place_up, :])
        grad_sum = norm_back(grad_normed, unit_one, scale_one, g0)
        da_ref[rows, :] = grad_sum
        sum_low = grad_sum.astype(BF)
        for head in range(2):
            cols = pl.ds(head * dim, dim)
            grad_out = mm_nt(sum_low, w_ref[2 * head + parity, place_out, :]).astype(BF)
            pack_ref[rows, cols] = grad_out
            delta = jnp.sum(grad_out.astype(F32) * wide_ref[rows, cols], axis=1, keepdims=True)
            delta_ref[head, rows, :] = jnp.broadcast_to(delta, (sub, 128))
    row = size
    for head in range(2):
        for ref in (lse_ref, delta_ref):
            row = store_line(pack_ref, row, jnp.transpose(ref[head])[0:1, :])


def feed(meta, mine, theirs, wide_out, lse, tokens, cotangent, w, down_bias, gains, shifts):
    size, width = tokens.shape[1:]
    dim = mine.shape[1] // 2
    return pl.pallas_call(
        feed_kernel,
        out_shape=(
            jax.ShapeDtypeStruct((size, width), BF),
            jax.ShapeDtypeStruct((size, width), F32),
            jax.ShapeDtypeStruct((size + STATS, 2 * dim), BF),
            jax.ShapeDtypeStruct((2, size, 128), F32),
        ),
        in_specs=[smem()] + [vmem()] * 9 + [hbm()] * 4,
        out_specs=[vmem()] * 4,
        scratch_shapes=[pltpu.VMEM((4,) + w[0].shape, BF), pltpu.SemaphoreType.DMA((4,))],
        compiler_params=params(),
        cost_estimate=cost(3e9, 8e6, 1e6),
        name="feed",
    )(meta, mine, theirs, wide_out, lse, tokens, cotangent, down_bias, gains, shifts, *w)


def low_grads(scores, factor, shift, grads, delta):
    count = scores.shape[1] // 128
    probs = jnp.exp2(scores * factor - wide(shift, count))
    return (probs * (grads - wide(delta, count))).astype(BF)


def token_query_grad_kernel(
    data_count,
    factor,
    meta,
    starts,
    q_ref,
    ids_ref,
    lse_ref,
    delta_ref,
    do_ref,
    acc_in,
    in_own,
    in_other,
    mine_low,
    mine_high,
    theirs_low,
    theirs_high,
    dq_ref,
    acc_ref,
    x_ref,
    w_ref,
    id_ref,
    sem,
):
    size, dim = q_ref.shape[1], q_ref.shape[2] // 2
    base = meta[0] * size
    first, last = key_range(starts, base, base + size, data_count)
    first, last = first // size, (last + size - 1) // size
    gathered = (mine_low, mine_high, theirs_low, theirs_high)
    fetch_shards(meta, first, last, gathered, x_ref, sem)
    join_weights(meta, in_own, in_other, w_ref, 1)
    acc_ref[...] = acc_in[...]
    id_ref[...] = column_of(ids_ref[meta[1]])

    def step(shard, carry):
        raw_rows, line = load_shard(meta, shard, gathered, x_ref, sem)
        kv = mm(raw_rows, w_ref[...]).astype(BF)
        mask = wide(id_ref[...], size // 128) == line
        raw, grads, low = [], [], []
        for h in range(2):
            raw.append(mm_nt(q_ref[0, :, h * dim : (h + 1) * dim], kv[:, h * dim : (h + 1) * dim]))
            grads.append(
                mm_nt(
                    do_ref[pl.ds(0, size), h * dim : (h + 1) * dim],
                    kv[:, (2 + h) * dim : (3 + h) * dim],
                )
            )
        for h in range(2):
            scores = jnp.where(mask, raw[h], NEGATIVE)
            low.append(low_grads(scores, factor, lse_ref[h], grads[h], delta_ref[h]))
        for h in range(2):
            acc_ref[h] += mm(low[h], kv[:, h * dim : (h + 1) * dim])
        return carry

    lax.fori_loop(first, last, step, 0)
    for h in range(2):
        dq_ref[:, pl.ds(h * dim, dim)] = acc_ref[h] * dim ** (-0.5)


def token_query_grad(
    meta, starts, q_own, ids_rows, lse, delta, pack, acc, mine, theirs, in_own, in_other, factor, data_count
):
    size, dim = q_own.shape[1], q_own.shape[2] // 2
    width = in_own.shape[1]
    return pl.pallas_call(
        functools.partial(token_query_grad_kernel, data_count, factor),
        out_shape=jax.ShapeDtypeStruct((size, 2 * dim), F32),
        in_specs=[smem()] * 2 + [vmem()] * 8 + [hbm()] * 4,
        out_specs=vmem(),
        scratch_shapes=[
            pltpu.VMEM((2, size, dim), F32),
            shard_scratch(mine),
            pltpu.VMEM((width, 4 * dim), BF),
            pltpu.VMEM((size, 128), F32),
            pltpu.SemaphoreType.DMA((2 * mine[0].shape[0], 2)),
        ],
        compiler_params=params(*mine, *theirs),
        cost_estimate=cost(6e9, 16e6, 4e6),
        name="token_query_grad",
    )(
        meta,
        starts,
        q_own,
        ids_rows,
        lse,
        delta,
        pack,
        acc,
        in_own,
        in_other,
        *mine,
        *theirs,
    )


def prompt_query_grad_kernel(
    block,
    factor,
    meta,
    local,
    table,
    q_ref,
    ids_ref,
    lse_in,
    delta_in,
    pack_own,
    pack_other,
    in_own,
    in_other,
    mine_low,
    mine_high,
    theirs_low,
    theirs_high,
    dq_ref,
    send_ref,
    acc_ref,
    lse_ref,
    delta_ref,
    do_ref,
    raws,
    w_ref,
    kv_ref,
    id_ref,
    state,
    sem,
):
    size, dim = q_ref.shape[1], q_ref.shape[2] // 2
    rows_per = size // (2 * dim)
    sources = (mine_low, mine_high, theirs_low, theirs_high)
    fetch_prompts(meta, local, table, sources, raws, state, sem)
    join_weights(meta, in_own, in_other, w_ref, 1)
    acc_ref[...] = jnp.zeros(acc_ref.shape, F32)
    lse_ref[0] = lse_in[...]
    delta_ref[0] = delta_in[...]
    do_ref[0] = pack_own[pl.ds(0, size), :]
    do_ref[1] = pack_other[pl.ds(0, size), :]
    for h in range(2):
        for kind, ref in enumerate((lse_ref, delta_ref)):
            row = size + (h * 2 + kind) * 3 * rows_per
            ref[1, h] = column_of(load_line(pack_other, row, size))
    for slot in range(2):
        id_ref[slot] = column_of(ids_ref[meta[1] ^ slot])

    def prepare(number):
        project_prompt(meta, number, sources, raws, w_ref, kv_ref, state, sem)

    def update(slot, rows, data, number):
        mask = id_ref[slot, rows, :] == data.astype(F32)
        raw, grads, low = [], [], []
        for h in range(2):
            cols = pl.ds(h * dim, dim)
            raw.append(mm_nt(q_ref[slot, rows, cols], kv_ref[number, :, cols]))
            value = kv_ref[number, :, pl.ds((2 + h) * dim, dim)]
            grads.append(mm_nt(do_ref[slot, rows, cols], value))
        for h in range(2):
            shift = jnp.where(mask, lse_ref[slot, h, rows, :], -NEGATIVE)
            scores = prompt_mask(meta, raw[h], block)
            low.append(low_grads(scores, factor, shift, grads[h], delta_ref[slot, h, rows, :]))
        for h in range(2):
            acc_ref[slot, h, rows, :] += mm(low[h], kv_ref[number, :, pl.ds(h * dim, dim)])

    visit_prompts(meta, local, table, size, prepare, update)
    for h in range(2):
        cols = pl.ds(h * dim, dim)
        dq_ref[h] = acc_ref[0, h]
        send_ref[:, cols] = (acc_ref[1, h] * dim ** (-0.5)).astype(BF)


def prompt_query_grad(
    meta,
    local,
    table,
    q_own,
    ids_rows,
    lse,
    delta,
    pack,
    pack_other,
    prompt_mine,
    prompt_theirs,
    in_own,
    in_other,
    factor,
    block,
):
    size, dim = q_own.shape[1], q_own.shape[2] // 2
    buffers, flags = prompt_scratch(prompt_mine, in_own.shape[1], dim, block)
    return pl.pallas_call(
        functools.partial(prompt_query_grad_kernel, block, factor),
        out_shape=(
            jax.ShapeDtypeStruct((2, size, dim), F32),
            jax.ShapeDtypeStruct((size, 2 * dim), BF),
        ),
        in_specs=[smem()] * 3 + [vmem()] * 8 + [hbm()] * 4,
        out_specs=[vmem()] * 2,
        scratch_shapes=[
            pltpu.VMEM((2, 2, size, dim), F32),
            pltpu.VMEM((2, 2, size, 128), F32),
            pltpu.VMEM((2, 2, size, 128), F32),
            pltpu.VMEM((2, size, 2 * dim), BF),
            *buffers,
            pltpu.VMEM((2, size, 128), F32),
            *flags,
        ],
        compiler_params=params(*prompt_mine, *prompt_mine, *prompt_mine, *prompt_mine),
        cost_estimate=cost(6e9, 16e6, 4e6),
        name="prompt_query_grad",
    )(
        meta,
        local,
        table,
        q_own,
        ids_rows,
        lse,
        delta,
        pack,
        pack_other,
        in_own,
        in_other,
        *prompt_mine,
        *prompt_theirs,
    )


def half_shard(meta, index, q_ref, ids_ref, low_ref, high_ref):
    slots, rows, double = low_ref.shape
    half = q_ref.shape[1]
    size = rows - STATS
    shard, part = index // 2, index % 2
    slot = slot_of(shard ^ meta[0], meta[2], bit_orders(2 * slots))
    other = slot_of(shard ^ meta[0], 1 - meta[2], bit_orders(2 * slots))
    query = q_ref[jnp.where(part == meta[2], slot * 2, other * 2 + 1)]
    in_low = slot < slots
    place_low, place_high = jnp.minimum(slot, slots - 1), jnp.maximum(slot - slots, 0)
    span = pl.ds(pl.multiple_of(part * half, half), half)
    grad = jnp.where(in_low, low_ref[place_low, span, :], high_ref[place_high, span, :])
    line = ids_ref[slot]
    line = jnp.where(part == 0, line[:, :half], line[:, half : 2 * half])
    tail = pl.ds(size, STATS)
    stats = jnp.where(in_low, low_ref[place_low, tail, :], high_ref[place_high, tail, :])
    stats = stats.astype(F32)
    rows_per = size // double

    def stat(head, kind):
        total = 0.0
        for place in range(3):
            row = ((head * 2 + kind) * 3 + place) * rows_per
            term = stats[row : row + 1, :]
            for i in range(1, rows_per):
                term = jnp.where(part == i, stats[row + i : row + i + 1, :], term)
            total = total + term
        return total

    return query, grad, line, stat


def key_update(query, grad, kv_ref, mask, rows_mask, stat, factor, dk_ref, dv_ref):
    dim = query.shape[1] // 2
    cols = [slice(h * dim, (h + 1) * dim) for h in range(2)]
    raw = [mm_nt(kv_ref[:, cols[h]], query[:, cols[h]]) for h in range(2)]
    grads = [mm_nt(kv_ref[:, pl.ds((2 + h) * dim, dim)], grad[:, cols[h]]) for h in range(2)]
    probs, low = [], []
    for h in range(2):
        shift = stat(h, 0)
        scores = raw[h]
        if rows_mask is None:
            shift = jnp.where(mask, shift, -NEGATIVE)
        else:
            scores = jnp.where(rows_mask, scores, NEGATIVE)
        p = jnp.exp2(scores * factor - shift)
        probs.append(p.astype(BF))
        low.append((p * (grads[h] - stat(h, 1))).astype(BF))
    for h in range(2):
        dv_ref[:, cols[h]] += mm(probs[h], grad[:, cols[h]])
        dk_ref[:, cols[h]] += mm(low[h], query[:, cols[h]])


def prompt_grad_kernel(
    data_count,
    factor,
    meta,
    starts,
    table,
    q_ref,
    ids_ref,
    low_ref,
    high_ref,
    own_ref,
    in_own,
    in_other,
    keep_ref,
    send_ref,
    dk_ref,
    dv_ref,
    w_ref,
    kv_ref,
):
    half = q_ref.shape[1]
    block, width = own_ref.shape
    dim = in_own.shape[2]
    number = meta[0] * block // PLEN
    dk_ref[...] = jnp.zeros(dk_ref.shape, F32)
    dv_ref[...] = jnp.zeros(dv_ref.shape, F32)
    join_weights(meta, in_own, in_other, w_ref, 1)
    kv_ref[...] = mm(own_ref[...].astype(BF), w_ref[...]).astype(BF)

    def visit(data, carry):
        begin, end = starts[data], starts[data + 1]

        @pl.when((table[meta[1], data] == number) & (begin < end))
        def _():
            def step(index, inner):
                query, grad, line, stat = half_shard(meta, index, q_ref, ids_ref, low_ref, high_ref)
                key_update(
                    query, grad, kv_ref, line == data.astype(F32), None, stat, factor, dk_ref, dv_ref
                )
                return inner

            lax.fori_loop(begin // half, (end + half - 1) // half, step, 0)

        return carry

    lax.fori_loop(0, data_count, visit, 0)
    grads = jnp.concatenate(
        [(dk_ref[...] * dim ** (-0.5)).astype(BF), dv_ref[...].astype(BF)], axis=1
    )
    split = width // 2
    parity = meta[2]
    send = w_ref[pl.ds(pl.multiple_of((1 - parity) * split, split), split), :]
    keep = w_ref[pl.ds(pl.multiple_of(parity * split, split), split), :]
    send_ref[...] = mm_nt(grads, send).astype(BF)
    keep_ref[...] = mm_nt(grads, keep)


def prompt_grad(meta, starts, table, q_all, ids_all, packs, own, in_own, in_other, factor, data_count):
    block, width = own.shape
    dim = in_own.shape[2]
    return pl.pallas_call(
        functools.partial(prompt_grad_kernel, data_count, factor),
        out_shape=(
            jax.ShapeDtypeStruct((block, width // 2), F32),
            jax.ShapeDtypeStruct((block, width // 2), BF),
        ),
        in_specs=[smem()] * 3 + [vmem()] * 7,
        out_specs=[vmem(), vmem()],
        scratch_shapes=[
            pltpu.VMEM((block, 2 * dim), F32),
            pltpu.VMEM((block, 2 * dim), F32),
            pltpu.VMEM((width, 4 * dim), BF),
            pltpu.VMEM((block, 4 * dim), BF),
        ],
        compiler_params=params(q_all, *packs),
        cost_estimate=cost(6e9, 16e6, 4e6),
        name="prompt_grad",
    )(meta, starts, table, q_all, ids_all, *packs, own, in_own, in_other)


def token_grad_kernel(
    data_count,
    factor,
    meta,
    starts,
    q_ref,
    ids_ref,
    low_ref,
    high_ref,
    tok_ref,
    own_ids,
    dq_ref,
    dq_other,
    in_own,
    in_other,
    out_ref,
    dk_ref,
    dv_ref,
    w_ref,
    kv_ref,
    id_ref,
):
    size = tok_ref.shape[1]
    half = q_ref.shape[1]
    dim = in_own.shape[2]
    base = meta[0] * size
    first, last = key_range(starts, base, base + size, data_count)
    dk_ref[...] = jnp.zeros(dk_ref.shape, F32)
    dv_ref[...] = jnp.zeros(dv_ref.shape, F32)
    join_weights(meta, in_own, in_other, w_ref, 0)
    kv_ref[...] = mm(tok_ref[meta[1]], w_ref[:, 2 * dim :]).astype(BF)
    id_ref[...] = column_of(own_ids[meta[1]])

    def step(index, carry):
        query, grad, line, stat = half_shard(meta, index, q_ref, ids_ref, low_ref, high_ref)
        mask = wide(id_ref[...], half // 128) == line
        key_update(query, grad, kv_ref, None, mask, stat, factor, dk_ref, dv_ref)
        return carry

    lax.fori_loop(first // half, (last + half - 1) // half, step, 0)
    dq = (dq_ref[...] + dq_other[...].astype(F32)).astype(BF)
    grads = jnp.concatenate(
        [dq, (dk_ref[...] * dim ** (-0.5)).astype(BF), dv_ref[...].astype(BF)], axis=1
    )
    out_ref[...] = mm_nt(grads, w_ref[...]).astype(BF)


def token_grad(
    meta, starts, q_all, ids_all, packs, tokens, ids_rows, dq, in_own, in_other, factor, data_count
):
    size, width = tokens.shape[1:]
    dim = in_own.shape[2]
    return pl.pallas_call(
        functools.partial(token_grad_kernel, data_count, factor),
        out_shape=jax.ShapeDtypeStruct((size, width), BF),
        in_specs=[smem()] * 2 + [vmem()] * 10,
        out_specs=vmem(),
        scratch_shapes=[
            pltpu.VMEM((size, 2 * dim), F32),
            pltpu.VMEM((size, 2 * dim), F32),
            pltpu.VMEM((width, 6 * dim), BF),
            pltpu.VMEM((size, 4 * dim), BF),
            pltpu.VMEM((size, 128), F32),
        ],
        compiler_params=params(spare=VMEM_LIMIT),
        cost_estimate=cost(4e9, 16e6, 4e6),
        name="token_grad",
    )(meta, starts, q_all, ids_all, *packs, tokens, ids_rows, *dq, in_own, in_other)


def sum_prompt_kernel(a_ref, b_ref, sum_ref, square_ref):
    low = (a_ref[...].astype(F32) + b_ref[...].astype(F32)).astype(BF)
    sum_ref[...] = low
    value = low.astype(F32)
    square_ref[...] = jnp.broadcast_to(jnp.sum(value * value, keepdims=True), square_ref.shape)


def sum_prompt(a, b):
    return pl.pallas_call(
        sum_prompt_kernel,
        out_shape=(
            jax.ShapeDtypeStruct(a.shape, BF),
            jax.ShapeDtypeStruct((8, 128), F32),
        ),
        in_specs=[vmem(), vmem()],
        out_specs=[vmem(), vmem()],
        compiler_params=params(),
        cost_estimate=cost(4 * a.size, 6 * a.size),
        name="sum_prompt",
    )(a, b)


def optimizer_kernel(
    meta,
    biases,
    mine,
    theirs,
    squares,
    prompts,
    one_in,
    two_in,
    clip_out,
    one_out,
    two_out,
    new_out,
    held,
    sem,
):
    even = meta[2] == 0
    block = prompts.shape[0]
    tiles = sem.shape[1]
    tile = block // tiles
    norm = jnp.sqrt(squares[0:1, :])
    factor = jnp.minimum(1.0, CLIP_NORM / (norm + 1e-06))
    copies = []
    for index in range(tiles):
        rows = pl.ds(index * tile, tile)
        a, b = mine[rows, :].astype(F32), theirs[rows, :].astype(F32)
        grads = jnp.concatenate([jnp.where(even, a, b), jnp.where(even, b, a)], axis=1)
        clipped = grads * wide(factor, grads.shape[1] // 128)
        new_one = BETA_ONE * one_in[rows, :] + (1.0 - BETA_ONE) * clipped
        new_two = BETA_TWO * two_in[rows, :] + (1.0 - BETA_TWO) * clipped * clipped
        first_hat = new_one / biases[0]
        second_hat = new_two / biases[1]
        held[0, rows, :] = clipped
        held[1, rows, :] = new_one
        held[2, rows, :] = new_two
        held[3, rows, :] = prompts[rows, :] * (
            1.0 - LEARNING_RATE * DECAY_RATE
        ) - LEARNING_RATE * first_hat / (jnp.sqrt(second_hat) + EPSILON)
        for place, out in enumerate((clip_out, one_out, two_out, new_out)):
            copies.append(
                pltpu.make_async_copy(held.at[place, rows], out.at[rows], sem.at[place, index])
            )
            copies[-1].start()
    for copy in copies:
        copy.wait()


def optimizer(meta, biases, mine, theirs, squares, prompts, moment_one, moment_two):
    block, width = prompts.shape
    tiles = 5 if block % 40 == 0 else 1
    shape = jax.ShapeDtypeStruct((block, width), F32)
    return pl.pallas_call(
        optimizer_kernel,
        out_shape=(shape,) * 4,
        in_specs=[smem(), smem()] + [vmem()] * 6,
        out_specs=[hbm()] * 4,
        scratch_shapes=[
            pltpu.VMEM((4, block, width), F32),
            pltpu.SemaphoreType.DMA((4, tiles)),
        ],
        compiler_params=params(prompts, prompts),
        cost_estimate=cost(20 * block * width, 32 * block * width),
        name="optimizer",
    )(meta, biases, mine, theirs, squares, prompts, moment_one, moment_two)


def per_device(
    tokens,
    cotangent,
    dataset_ids,
    prompt_map,
    attn_in,
    attn_out,
    up_weight,
    up_bias,
    down_weight,
    down_bias,
    norm_gains,
    norm_shifts,
    prompts,
    moment_one,
    moment_two,
    step_count,
):
    size, width = tokens.shape[1:]
    dim = attn_in.shape[2]
    hid = up_weight.shape[1]
    data_count = prompt_map.shape[1]
    row_count = lax.axis_size("rows")
    head_count = lax.axis_size("head")
    factor = dim ** (-0.5) * LOG2E
    row = lax.axis_index("rows")
    head = lax.axis_index("head")
    batch, parity = head // 2, head % 2
    half = size // 2
    meta = jnp.stack([row, batch, parity]).astype(jnp.int32)

    block = prompts.shape[0]

    part = half_rows(block)
    prompt_own = lax.dynamic_slice(
        prompts, (batch * (block - part), parity * (width // 2)), (part, width // 2)
    ).astype(BF)
    in_other = swap_head(attn_in, 2, head_count)
    ids = jnp.where(batch == 0, dataset_ids[0], dataset_ids[1])
    tok_half = lax.dynamic_slice(tokens, (batch, parity * half, 0), (1, half, width))[0]
    id_rows = jnp.broadcast_to(ids.astype(BF)[None, :], (PACK, size))
    shard = jnp.concatenate([tok_half, id_rows], axis=0)

    bias_high = lax.reduce_precision(up_bias, 8, 7)
    bias_rest = up_bias - bias_high
    bias_mid = lax.reduce_precision(bias_rest, 8, 7)
    bias_low = bias_rest - bias_mid
    bias_rows = jnp.concatenate([bias_high, bias_mid, bias_low, bias_low]).astype(BF)
    bias_rows = jnp.pad(bias_rows.reshape(-1, width), ((0, PACK - 4 * hid // width), (0, 0)))
    w_own = jnp.concatenate([down_weight, attn_out, up_weight.T, bias_rows], axis=0)
    in_other, w_own = lax.optimization_barrier((in_other, w_own))
    w_along = swap_head(w_own, 2, head_count)
    step_value = step_count.astype(F32)
    biases = jnp.stack(
        [1.0 - jnp.power(BETA_ONE, step_value), 1.0 - jnp.power(BETA_TWO, step_value)]
    )
    numbers = jnp.arange(data_count + 1, dtype=jnp.int32)
    local = jnp.sum((dataset_ids[:, None, :] < numbers[None, :, None]).astype(jnp.int32), axis=2)
    ids_rows = dataset_ids.astype(F32).reshape(2, 1, size)
    tied = {}

    orders, later = bit_orders(row_count), prompt_orders(row_count)
    stages = len(orders[0])
    held, prompt_held = shard[None], prompt_own[None]

    def prompt_stage(place):
        other = gather_stage(prompt_held, place, later, row_count, head_count)
        return jnp.concatenate([prompt_held, other], axis=0)

    for place in range(stages):
        if place == stages - 1:
            held, in_other, w_along, meta, (biases, local, ids_rows) = lax.optimization_barrier(
                (held, in_other, w_along, meta, (biases, local, ids_rows))
            )
        if place != 1:
            held, prompt_held = lax.optimization_barrier((held, prompt_held))
        other = gather_stage(held, place, orders, row_count, head_count)
        if place != 1:
            prompt_held = prompt_stage(max(place - 1, 0))
        if place < stages - 1:
            held = jnp.concatenate([held, other], axis=0)
        if place == 0:
            held, prompt_held = lax.optimization_barrier((held, prompt_held))
    theirs_low = swap_head(held, 1, head_count)
    other, prompt_held = lax.optimization_barrier((other, prompt_held))
    mine = (held, other)
    prompt_high = gather_stage(prompt_held, stages - 1, later, row_count, head_count)
    theirs = (theirs_low, swap_head(other, 1, head_count))
    w_core = swap_head(w_own, 1, head_count)
    w_far = swap_head(w_along, 1, head_count)

    ids_all = jnp.concatenate([bank[:, half, :size] for bank in mine], axis=0).astype(F32)
    starts = jnp.sum(
        (ids_all.reshape(1, -1) < numbers.astype(F32)[:, None]).astype(jnp.int32), axis=1
    )
    ids_all = ids_all.reshape(row_count, 1, size)
    q_own, *state = token_forward(
        meta, starts, tokens, ids_rows, mine, theirs, attn_in, in_other, factor, data_count
    )
    prompt_theirs_low = swap_head(prompt_held, 1, head_count)
    prompt_high, state, prompt_theirs_low, w_core, w_far = lax.optimization_barrier(
        (prompt_high, state, prompt_theirs_low, w_core, w_far)
    )
    prompt_mine = (prompt_held, prompt_high)
    prompt_theirs = (prompt_theirs_low, swap_head(prompt_high, 1, head_count))
    wide_half, lse_half, send_half = prompt_forward(
        meta,
        local,
        prompt_map,
        q_own,
        ids_rows,
        state,
        prompt_mine,
        prompt_theirs,
        attn_in,
        in_other,
        factor,
        block,
    )
    o_mine, wide_out, lse = join_halves(wide_half, lse_half, swap_head(send_half, 2, head_count))
    o_theirs = swap_head(o_mine, 1, head_count)
    out, grad_sum, pack, delta = feed(
        meta,
        o_mine,
        o_theirs,
        wide_out,
        lse,
        tokens,
        cotangent,
        (w_own, w_along, w_core, w_far),
        down_bias.reshape(1, width),
        norm_gains,
        norm_shifts,
    )
    pack_other = swap_head(pack, 2, head_count)

    def tie_query_grads(stages_left, held):
        if stages_left == 3:
            held, here = lax.optimization_barrier((held, in_other))
            tied["q"] = project_query(meta, mine, theirs, attn_in, here)
        if stages_left == 2:
            held, other, tied["q"] = lax.optimization_barrier((held, pack_other, tied["q"]))
            tied["dq"] = prompt_query_grad(
                meta,
                local,
                prompt_map,
                q_own,
                ids_rows,
                lse,
                delta,
                pack,
                other,
                prompt_mine,
                prompt_theirs,
                attn_in,
                in_other,
                factor,
                block,
            )
        if stages_left == 1:
            held, (acc, dq_send) = lax.optimization_barrier((held, tied["dq"]))
            tied["dq_other"] = swap_head(dq_send, 2, head_count)
            tied["dq"] = token_query_grad(
                meta,
                starts,
                q_own,
                ids_rows,
                lse,
                delta,
                pack,
                acc,
                mine,
                theirs,
                attn_in,
                in_other,
                factor,
                data_count,
            )
        return held

    out_half = lax.dynamic_slice_in_dim(out, parity * half, half, 0)
    out_half = swap_head(out_half, 2, head_count)
    packs = gather_rows(pack, row_count, head_count, tie_query_grads)
    q_all = tied["q"]
    packs, dq, dq_other, out_half = lax.optimization_barrier(
        (packs, tied["dq"], tied["dq_other"], out_half)
    )
    keep, send = prompt_grad(
        meta, starts, prompt_map, q_all, ids_all, packs, prompts, attn_in, in_other, factor, data_count
    )

    pair = keep + swap_head(send, 1, head_count).astype(F32)
    pair_low = lax.reduce_precision(pair, 8, 7).astype(BF)
    dq, pair_low = lax.optimization_barrier((dq, pair_low))
    pair_other = swap_head(pair_low, 2, head_count)
    out_rest = swap_head(out_half, 1, head_count)
    token_part = token_grad(
        meta,
        starts,
        q_all,
        ids_all,
        packs,
        tokens,
        ids_rows,
        (dq, dq_other),
        attn_in,
        in_other,
        factor,
        data_count,
    )
    token_part, pair_other = lax.optimization_barrier((token_part, pair_other))
    full_low, squares = sum_prompt(pair_low, pair_other)
    full_other = swap_head(full_low, 1, head_count)

    def both_batches(own, here, rest):
        other = jnp.concatenate(
            [jnp.where(parity == 0, here, rest), jnp.where(parity == 0, rest, here)], axis=0
        )
        first = jnp.where(batch == 0, own, other)
        return jnp.stack([first, jnp.where(batch == 0, other, own)]).astype(F32)

    core_sum = token_part.astype(F32) + swap_head(token_part, 1, head_count).astype(F32)
    total = lax.reduce_precision(grad_sum + core_sum, 8, 7).astype(BF)
    mine_half = lax.dynamic_slice_in_dim(total, parity * half, half, 0)
    other_half = swap_head(mine_half, 2, head_count)
    layer_out = both_batches(out, out_half, out_rest)

    def tie_sum(stages_done, value):
        if stages_done == 1:
            value, _ = lax.optimization_barrier((value, total))
        if stages_done == 2:
            value, tied["half"], tied["out"] = lax.optimization_barrier(
                (value, other_half, layer_out)
            )
        return value

    squares = xor_sum(squares, row_count, head_count, tie_sum)
    other_half, layer_out = tied["half"], tied["out"]
    input_grad = both_batches(total, other_half, swap_head(other_half, 1, head_count))
    clipped, new_one, new_two, new_prompts = optimizer(
        meta, biases, full_low, full_other, squares, prompts, moment_one, moment_two
    )
    return (layer_out, input_grad, clipped, jnp.sqrt(squares[0, 0]), new_one, new_two, new_prompts)


def solution(mesh):
    in_specs = (
        P(None, "rows", None),
        P(None, "rows", None),
        P(None, "rows"),
        P(),
        P(None, None, "head"),
        P("head", None),
        P(None, "head"),
        P("head"),
        P("head", None),
        P(),
        P(),
        P(),
        P("rows", None),
        P("rows", None),
        P("rows", None),
        P(),
    )
    out_specs = (
        P(None, "rows", None),
        P(None, "rows", None),
        P("rows", None),
        P(),
        P("rows", None),
        P("rows", None),
        P("rows", None),
    )
    return jax.shard_map(
        per_device, mesh=mesh, in_specs=in_specs, out_specs=out_specs, check_vma=False
    )
```

```python
import functools

import jax
import jax.numpy as jnp
from jax import lax
from jax.experimental import pallas as pl
from jax.experimental.pallas import tpu as pltpu
from jax.sharding import PartitionSpec as P

PLEN = 1000
NEGATIVE = -1e30
BETA_ONE = 0.9
BETA_TWO = 0.999
LEARNING_RATE = 0.5
DECAY_RATE = 0.01
EPSILON = 1e-08
CLIP_NORM = 1.0
LOG2E = 1.4426950408889634
PACK = 16
STATS = 32
VMEM_LIMIT = 60 * 1024 * 1024
BF = jnp.bfloat16
F32 = jnp.float32
BOTH = ("rows", "head")


def params(*operands, spare=20 << 20):
    held = sum(x.size * x.dtype.itemsize for x in operands)
    return pltpu.CompilerParams(vmem_limit_bytes=min(VMEM_LIMIT, held + spare))


def cost(flops, bytes_accessed, transcendentals=0):
    return pl.CostEstimate(
        flops=int(flops), bytes_accessed=int(bytes_accessed), transcendentals=int(transcendentals)
    )


def mm(a, b):
    return lax.dot_general(a, b, (((1,), (0,)), ((), ())), preferred_element_type=F32)


def mm_nt(a, b):
    return lax.dot_general(a, b, (((1,), (1,)), ((), ())), preferred_element_type=F32)


def split3(value):
    high = value.astype(BF)
    rest = value - high.astype(F32)
    mid = rest.astype(BF)
    low = (rest - mid.astype(F32)).astype(BF)
    return high, mid, low


def bit_orders(row_count):
    bits = row_count.bit_length() - 1
    return ([0] + list(range(bits - 1, 0, -1)), list(range(bits - 1, 0, -1)) + [0])


def prompt_orders(row_count):
    bits = row_count.bit_length() - 1
    if bits < 2:
        return bit_orders(row_count)
    high = list(range(bits - 1, 1, -1))
    return (high + [0, 1], [1] + high + [0])


def slot_of(offset, parity, orders):
    def mapped(order):
        total = 0
        for place, bit in enumerate(order):
            total = total + (((offset >> bit) & 1) << place)
        return total

    return jnp.where(parity == 0, mapped(orders[0]), mapped(orders[1]))


def gather_stage(held, place, orders, row_count, head_count):
    pairs = []
    for row in range(row_count):
        for head in range(head_count):
            bit = orders[head % 2][place]
            pairs.append((row * head_count + head, (row ^ (1 << bit)) * head_count + head))
    return lax.ppermute(held, BOTH, pairs)


def gather_rows(block, row_count, head_count, before_send):
    held = block[None]
    orders = bit_orders(row_count)
    stages = len(orders[0])
    for place in range(stages):
        held = before_send(stages - place, held)
        other = gather_stage(held, place, orders, row_count, head_count)
        if place < stages - 1:
            held = jnp.concatenate([held, other], axis=0)
    return held, other


def xor_sum(value, row_count, head_count, after):
    def moved(mask):
        count = row_count * head_count
        return lax.ppermute(value, BOTH, [(i, i ^ mask) for i in range(count)])

    masks = [1]
    bit = head_count
    while bit < row_count * head_count:
        masks.append(bit)
        bit = bit * 2
    done = 0
    while masks:
        if len(masks) == 1:
            value = value + moved(masks[0])
        else:
            first, second, both = (moved(m) for m in (masks[0], masks[1], masks[0] ^ masks[1]))
            value = (value + first) + (second + both)
        masks = masks[2:]
        done = done + 1
        value = after(done, value)
    return value


def swap_head(value, mask, head_count):
    return lax.ppermute(value, "head", [(i, i ^ mask) for i in range(head_count)])


def smem():
    return pl.BlockSpec(memory_space=pltpu.SMEM)


def vmem():
    return pl.BlockSpec(memory_space=pltpu.VMEM)


def hbm():
    return pl.BlockSpec(memory_space=pltpu.HBM)


def flag_shape():
    return jax.ShapeDtypeStruct((8, 128), F32)


def raise_flag(ref):
    ref[...] = jnp.zeros(ref.shape, F32)


def join_weights(meta, own, other, target, kinds):
    dim = own.shape[2]
    for index, kind in enumerate(kinds):
        for place in range(2):
            column = (index * 2 + place) * dim
            target[:, column : column + dim] = jnp.where(meta[1] == place, own[kind], other[kind])


def wide(value, count):
    return jnp.concatenate([value] * count, axis=1)


def line_of(columns):
    return jnp.transpose(columns)[0:1, :]


def column_of(line):
    return jnp.transpose(jnp.broadcast_to(line, (128, line.shape[1])))


def project_query_kernel(a, b, c, d, weights, q_out, flag):
    raise_flag(flag)
    half = a.shape[1] - PACK
    for high, pair in enumerate(((a, b), (c, d))):
        for place, ref in enumerate(pair):
            q_out[high, 0, place] = mm(ref[0, :half], weights[...]).astype(BF)


def project_query(mine, theirs, weights):
    slots, rows, width = mine[0].shape
    half = rows - PACK
    double = weights.shape[1]
    block = pl.BlockSpec((1, rows, width), lambda g: (g, 0, 0))
    whole = pl.BlockSpec(weights.shape, lambda g: (0, 0))
    out, flag = pl.pallas_call(
        project_query_kernel,
        out_shape=(jax.ShapeDtypeStruct((2, slots, 2, half, double), BF), flag_shape()),
        grid=(slots,),
        in_specs=[block] * 4 + [whole],
        out_specs=[
            pl.BlockSpec((2, 1, 2, half, double), lambda g: (0, g, 0, 0, 0)),
            pl.BlockSpec((8, 128), lambda g: (0, 0)),
        ],
        compiler_params=params(),
        cost_estimate=cost(8 * slots * half * width * double, 8 * slots * half * width),
        name="project_query",
    )(mine[0], theirs[0], mine[1], theirs[1], weights)
    return out.reshape(4 * slots, half, double), flag


def key_range(starts, low, high, data_count):
    first = jnp.int32(1 << 30)
    last = jnp.int32(0)
    for data in range(data_count):
        begin, end = starts[data], starts[data + 1]
        hit = (begin < high) & (end > low) & (begin < end)
        first = jnp.where(hit, jnp.minimum(first, begin), first)
        last = jnp.where(hit, jnp.maximum(last, end), last)
    return first, last


def shard_copies(meta, shard, gathered, x_ref, sem):
    slots = gathered[0].shape[0]
    copies = []
    for place in range(2):
        slot = slot_of(shard ^ meta[0], meta[2] ^ place, bit_orders(2 * slots))
        for bank in range(2):
            here = (slot < slots) if bank == 0 else (slot >= slots)
            source = gathered[place * 2 + bank]
            copy = pltpu.make_async_copy(
                source.at[jnp.where(here, slot - bank * slots, 0)],
                x_ref.at[shard, place],
                sem.at[shard, place],
            )
            copies.append((here, copy))
    return copies


def fetch_shards(meta, first, last, gathered, x_ref, sem):
    def start(shard, carry):
        for here, copy in shard_copies(meta, shard, gathered, x_ref, sem):

            @pl.when(here)
            def _():
                copy.start()

        return carry

    lax.fori_loop(first, last, start, 0)


def load_shard(meta, shard, gathered, x_ref, sem):
    half = x_ref.shape[2] - PACK
    parity = meta[2]
    for place in range(2):
        pltpu.make_async_copy(gathered[0].at[0], x_ref.at[shard, place], sem.at[shard, place]).wait()
    line = x_ref[shard, 0, half : half + 1, :].astype(F32)
    first, second = line[:, :half], line[:, half : 2 * half]
    line = jnp.concatenate(
        [jnp.where(parity == 0, first, second), jnp.where(parity == 0, second, first)], axis=1
    )
    return jnp.concatenate([x_ref[shard, 0, :half, :], x_ref[shard, 1, :half, :]], axis=0), line


def online(scores, factor, mask, m_ref, place):
    old_max = m_ref[place]
    size = old_max.shape[0]
    top = jnp.broadcast_to(jnp.max(scores, axis=1, keepdims=True) * factor, (size, 128))
    new_max = jnp.maximum(old_max, top)
    shift = new_max
    if mask is not None:
        new_max = jnp.where(mask, new_max, old_max)
        shift = jnp.where(mask, new_max, -NEGATIVE)
    m_ref[place] = new_max
    probs = jnp.exp2(scores * factor - wide(shift, scores.shape[1] // 128))
    return probs.astype(BF), jnp.exp2(old_max - new_max)


def accumulate(acc_ref, place, alpha, probs, value):
    with_ones = jnp.concatenate([value, jnp.ones((value.shape[0], 128), BF)], axis=1)
    acc_ref[place] = acc_ref[place] * wide(alpha, with_ones.shape[1] // 128) + mm(probs, with_ones)


def token_forward_kernel(
    data_count,
    factor,
    meta,
    starts,
    ids_ref,
    in_own,
    in_other,
    tok_hbm,
    mine_low,
    mine_high,
    theirs_low,
    theirs_high,
    q_ref,
    kv_own,
    wq_ref,
    wkv_ref,
    m_out,
    l_out,
    acc_out,
    flag,
    m_ref,
    acc_ref,
    x_ref,
    id_ref,
    tok_ref,
    sem,
    tok_sem,
):
    raise_flag(flag)
    size, dim = tok_ref.shape[1], in_own.shape[2]
    tok_copy = pltpu.make_async_copy(tok_hbm, tok_ref, tok_sem)
    tok_copy.start()
    base = meta[0] * size
    first, last = key_range(starts, base, base + size, data_count)
    first, last = first // size, (last + size - 1) // size
    gathered = (mine_low, mine_high, theirs_low, theirs_high)
    fetch_shards(meta, first, last, gathered, x_ref, sem)
    join_weights(meta, in_own, in_other, wq_ref, (0,))
    join_weights(meta, in_own, in_other, wkv_ref, (1, 2))
    tok_copy.wait()
    for slot in range(2):
        q_ref[slot] = mm(tok_ref[meta[1] ^ slot], wq_ref[...]).astype(BF)
    kv_own[...] = mm(tok_ref[meta[1]], wkv_ref[...]).astype(BF)
    m_ref[...] = jnp.full(m_ref.shape, NEGATIVE, F32)
    acc_ref[...] = jnp.zeros(acc_ref.shape, F32)
    id_ref[...] = column_of(ids_ref[meta[1]])
    rows = pl.ds(0, size)

    def step(shard, carry):
        raw_rows, line = load_shard(meta, shard, gathered, x_ref, sem)
        kv = mm(raw_rows, wkv_ref[...]).astype(BF)
        mask = wide(id_ref[...], size // 128) == line
        raw = [
            mm_nt(q_ref[0, :, h * dim : (h + 1) * dim], kv[:, h * dim : (h + 1) * dim])
            for h in range(2)
        ]
        parts = [
            online(jnp.where(mask, raw[h], NEGATIVE), factor, None, m_ref, (h, rows))
            for h in range(2)
        ]
        for h in range(2):
            value = kv[:, (2 + h) * dim : (3 + h) * dim]
            accumulate(acc_ref, (h, rows), parts[h][1], parts[h][0], value)
        return carry

    lax.fori_loop(first, last, step, 0)
    for h in range(2):
        m_out[h : h + 1, :] = line_of(m_ref[h])
        l_out[h : h + 1, :] = line_of(acc_ref[h, :, dim:])
        acc_out[h] = acc_ref[h, :, :dim]


def shard_scratch(banks):
    slots, rows, width = banks[0].shape
    return pltpu.VMEM((2 * slots, 2, rows, width), BF)


def token_forward(meta, starts, tokens, ids_rows, mine, theirs, in_own, in_other, factor, data_count):
    size, width = tokens.shape[1:]
    dim = in_own.shape[2]
    return pl.pallas_call(
        functools.partial(token_forward_kernel, data_count, factor),
        out_shape=(
            jax.ShapeDtypeStruct((2, size, 2 * dim), BF),
            jax.ShapeDtypeStruct((size, 4 * dim), BF),
            jax.ShapeDtypeStruct((width, 2 * dim), BF),
            jax.ShapeDtypeStruct((width, 4 * dim), BF),
            jax.ShapeDtypeStruct((2, size), F32),
            jax.ShapeDtypeStruct((2, size), F32),
            jax.ShapeDtypeStruct((2, size, dim), F32),
            flag_shape(),
        ),
        in_specs=[smem(), smem()] + [vmem()] * 3 + [hbm()] * 5,
        out_specs=[vmem()] * 8,
        scratch_shapes=[
            pltpu.VMEM((2, size, 128), F32),
            pltpu.VMEM((2, size, dim + 128), F32),
            shard_scratch(mine),
            pltpu.VMEM((size, 128), F32),
            pltpu.VMEM(tokens.shape, BF),
            pltpu.SemaphoreType.DMA((2 * mine[0].shape[0], 2)),
            pltpu.SemaphoreType.DMA,
        ],
        compiler_params=params(spare=VMEM_LIMIT),
        cost_estimate=cost(8e9, 8e6, 2e6),
        name="token_forward",
    )(meta, starts, ids_rows, in_own, in_other, tokens, *mine, *theirs)


def half_rows(block):
    return -(-block // 32) * 16


def fetch_prompts(meta, local, table, sources, raws, state, sem):
    pieces = raws.shape[2]
    slots = sources[0].shape[0]
    for number in range(state.shape[0]):
        state[number] = 0
    for batch in range(2):
        for data in range(table.shape[1]):
            number = table[batch, data]
            used = local[batch, data + 1] > local[batch, data]
            state[number] = jnp.where(used, 1, state[number])

    def start(number, carry):
        @pl.when(state[number] == 1)
        def _():
            for piece in range(pieces):
                for place in range(2):
                    shard = number * pieces + piece
                    slot = slot_of(shard ^ meta[0], meta[2] ^ place, prompt_orders(2 * slots))
                    for bank in range(2):

                        @pl.when((slot < slots) if bank == 0 else (slot >= slots))
                        def _():
                            pltpu.make_async_copy(
                                sources[place * 2 + bank].at[slot - bank * slots],
                                raws.at[place, number, piece],
                                sem.at[place, number, piece],
                            ).start()

        return carry

    lax.fori_loop(0, state.shape[0], start, 0)


def project_prompt(meta, number, sources, raws, w_ref, kv_ref, state, sem):
    pieces, block = raws.shape[2:4]

    @pl.when(state[number] == 1)
    def _():
        even = meta[2] == 0
        for piece in range(pieces):
            for place in range(2):
                pltpu.make_async_copy(
                    sources[0].at[0], raws.at[place, number, piece], sem.at[place, number, piece]
                ).wait()
            a, b = raws[0, number, piece], raws[1, number, piece]
            rows = jnp.concatenate([jnp.where(even, a, b), jnp.where(even, b, a)], axis=1)
            kv_ref[number, pl.ds(piece * block, block), :] = mm(rows, w_ref[...]).astype(BF)
        full = pieces * block
        if full < kv_ref.shape[1]:
            kv_ref[number, full:, :] = jnp.zeros((kv_ref.shape[1] - full, kv_ref.shape[2]), BF)
        state[number] = 2


def prompt_mask(meta, scores, block):
    part = half_rows(block)
    pieces = PLEN // block
    doubled = 2 * part - block
    head = min(128, part) if pieces == 1 else scores.shape[1]
    lanes = lax.broadcasted_iota(jnp.int32, (scores.shape[0], head), 1)
    out = (lanes % part < doubled * meta[1]) | (lanes >= pieces * part)
    first = jnp.where(out, NEGATIVE, scores[:, :head])
    if head == scores.shape[1]:
        return first
    return jnp.concatenate([first, scores[:, head:]], axis=1)


def visit_prompts(meta, local, table, size, prepare, update):
    data_count = table.shape[1]

    def visit(index, carry):
        slot, data = index // data_count, index % data_count
        batch = meta[1] ^ slot
        begin, end = local[batch, data], local[batch, data + 1]

        @pl.when(begin < end)
        def _():
            number = table[batch, data]
            prepare(number)
            low = begin // 128
            count = (end + 127) // 128 - low
            for case in range(1, size // 128 + 1):

                @pl.when(count == case)
                def _():
                    rows = pl.ds(pl.multiple_of(low * 128, 128), case * 128)
                    update(slot, rows, data, number)

        return carry

    lax.fori_loop(0, 2 * data_count, visit, 0)


def store_line(ref, row, line):
    width = ref.shape[1]
    for term in split3(line):
        for low in range(0, line.shape[1], width):
            ref[row : row + 1, :] = term[:, low : low + width]
            row = row + 1
    return row


def load_line(ref, row, length):
    width = ref.shape[1]
    rows_per = length // width
    total = 0.0
    for place in range(3):
        first = row + place * rows_per
        pieces = [ref[first + i : first + i + 1, :].astype(F32) for i in range(rows_per)]
        total = total + jnp.concatenate(pieces, axis=1)
    return total


def prompt_forward_kernel(
    block,
    factor,
    meta,
    local,
    table,
    q_ref,
    ids_ref,
    m_in,
    l_in,
    acc_in,
    _,
    w_ref,
    mine_low,
    mine_high,
    theirs_low,
    theirs_high,
    wide_ref,
    lse_ref,
    send_ref,
    m_ref,
    acc_ref,
    raws,
    kv_ref,
    id_ref,
    state,
    sem,
):
    size, dim = q_ref.shape[1], q_ref.shape[2] // 2
    sources = (mine_low, mine_high, theirs_low, theirs_high)
    fetch_prompts(meta, local, table, sources, raws, state, sem)
    for h in range(2):
        m_ref[0, h] = column_of(m_in[h : h + 1, :])
        acc_ref[0, h, :, dim:] = column_of(l_in[h : h + 1, :])
        acc_ref[0, h, :, :dim] = acc_in[h]
    m_ref[1] = jnp.full(m_ref.shape[1:], NEGATIVE, F32)
    acc_ref[1] = jnp.zeros(acc_ref.shape[1:], F32)
    for slot in range(2):
        id_ref[slot] = column_of(ids_ref[meta[1] ^ slot])

    def prepare(number):
        project_prompt(meta, number, sources, raws, w_ref, kv_ref, state, sem)

    def update(slot, rows, data, number):
        mask = id_ref[slot, rows, :] == data.astype(F32)
        raw = [
            mm_nt(q_ref[slot, rows, pl.ds(h * dim, dim)], kv_ref[number, :, pl.ds(h * dim, dim)])
            for h in range(2)
        ]
        parts = [
            online(prompt_mask(meta, raw[h], block), factor, mask, m_ref, (slot, h, rows))
            for h in range(2)
        ]
        for h in range(2):
            value = kv_ref[number, :, pl.ds((2 + h) * dim, dim)]
            accumulate(acc_ref, (slot, h, rows), parts[h][1], parts[h][0], value)

    visit_prompts(meta, local, table, size, prepare, update)
    row = size
    send_ref[pl.ds(size, PACK), :] = jnp.zeros((PACK, 2 * dim), BF)
    for h in range(2):
        cols = pl.ds(h * dim, dim)
        total = acc_ref[0, h, :, dim:]
        wide_ref[:, cols] = acc_ref[0, h, :, :dim] / total
        lse_ref[h : h + 1, :] = line_of(m_ref[0, h] + jnp.log2(total))
        total = acc_ref[1, h, :, dim:]
        send_ref[pl.ds(0, size), cols] = (acc_ref[1, h, :, :dim] / total).astype(BF)
        line = line_of(m_ref[1, h] + jnp.log2(total))
        row = store_line(send_ref, row, line)


def prompt_scratch(prompt_banks, dim, block):
    slots, part, columns = prompt_banks[0].shape
    pieces = PLEN // block
    count = 2 * slots // pieces
    return [
        pltpu.VMEM((2, count, pieces, part, columns), BF),
        pltpu.VMEM((count, -(-pieces * part // 128) * 128, 4 * dim), BF),
    ], [pltpu.SMEM((count,), jnp.int32), pltpu.SemaphoreType.DMA((2, count, pieces))]


def prompt_forward(
    meta, local, table, q_own, ids_rows, state, flag, prompt_mine, prompt_theirs, weights, factor, block
):
    size, dim = q_own.shape[1], q_own.shape[2] // 2
    buffers, flags = prompt_scratch(prompt_mine, dim, block)
    return pl.pallas_call(
        functools.partial(prompt_forward_kernel, block, factor),
        out_shape=(
            jax.ShapeDtypeStruct((size, 2 * dim), F32),
            jax.ShapeDtypeStruct((2, size), F32),
            jax.ShapeDtypeStruct((size + PACK, 2 * dim), BF),
        ),
        in_specs=[smem()] * 3 + [vmem()] * 7 + [hbm()] * 4,
        out_specs=[vmem()] * 3,
        scratch_shapes=[
            pltpu.VMEM((2, 2, size, 128), F32),
            pltpu.VMEM((2, 2, size, dim + 128), F32),
            *buffers,
            pltpu.VMEM((2, size, 128), F32),
            *flags,
        ],
        compiler_params=params(spare=VMEM_LIMIT),
        cost_estimate=cost(4e9, 8e6, 2e6),
        name="prompt_forward",
    )(meta, local, table, q_own, ids_rows, *state, flag, weights, *prompt_mine, *prompt_theirs)


def join_kernel(wide_in, lse_in, other_ref, o_ref, wide_ref, lse_ref):
    size, dim = wide_in.shape[0], wide_in.shape[1] // 2
    rows_per = size // (2 * dim)
    for h in range(2):
        cols = pl.ds(h * dim, dim)
        first = column_of(lse_in[h : h + 1, :])
        second = column_of(load_line(other_ref, size + h * 3 * rows_per, size))
        top = jnp.maximum(first, second)
        first, second = jnp.exp2(first - top), jnp.exp2(second - top)
        total = first + second
        other = other_ref[pl.ds(0, size), cols].astype(F32)
        attended = (first * wide_in[:, cols] + second * other) / total
        wide_ref[:, cols] = attended
        o_ref[:, cols] = attended.astype(BF)
        lse_ref[h : h + 1, :] = line_of(top + jnp.log2(total))


def join_halves(wide_half, lse_half, other):
    return pl.pallas_call(
        join_kernel,
        out_shape=(
            jax.ShapeDtypeStruct(wide_half.shape, BF),
            jax.ShapeDtypeStruct(wide_half.shape, F32),
            jax.ShapeDtypeStruct(lse_half.shape, F32),
        ),
        in_specs=[vmem()] * 3,
        out_specs=[vmem()] * 3,
        compiler_params=params(),
        cost_estimate=cost(4e6, 3e6, 1e6),
        name="join_halves",
    )(wide_half, lse_half, other)


def norm_parts(value):
    center = value - jnp.mean(value, axis=-1, keepdims=True)
    scale = lax.rsqrt(jnp.mean(center * center, axis=-1, keepdims=True) + 1e-05)
    return center * scale, scale


def norm_back(grad, unit, scale, gain):
    part = grad * gain
    return scale * (
        part
        - jnp.mean(part, axis=-1, keepdims=True)
        - unit * jnp.mean(part * unit, axis=-1, keepdims=True)
    )


def feed_kernel(
    meta,
    mine,
    theirs,
    wide_ref,
    lse_ref,
    tok_ref,
    cot_ref,
    down_bias,
    gains,
    shifts,
    w_own,
    w_along,
    w_core,
    w_far,
    out_ref,
    da_ref,
    pack_ref,
    delta_ref,
    w_ref,
    sem,
):
    size, width = tok_ref.shape
    dim = mine.shape[1] // 2
    heads = w_ref.shape[0]
    hid = (w_ref.shape[1] - PACK - dim) // 2
    batch, parity = meta[1], meta[2]
    even = parity == 0
    cuts = (pl.ds(hid, dim), pl.ds(hid + dim, hid + PACK), pl.ds(0, hid))

    def arrived(part):
        for q in range(heads):
            pltpu.make_async_copy(
                w_own.at[cuts[part]], w_ref.at[q, cuts[part]], sem.at[q, part]
            ).wait()

    for q in range(heads):
        for place, ref in enumerate((w_own, w_along, w_core, w_far)):

            @pl.when((2 * batch + parity) == (q ^ (0, 2, 1, 3)[place]))
            def _():
                for part, rows in enumerate(cuts):
                    pltpu.make_async_copy(
                        ref.at[rows], w_ref.at[q, rows], sem.at[q, part]
                    ).start()

    place_out = slice(hid, hid + dim)
    place_up = slice(hid + dim, 2 * hid + dim)
    place_bias = 2 * hid + dim
    sub = min(256, size)
    pack_ref[pl.ds(size, STATS), :] = jnp.zeros((STATS, 2 * dim), BF)
    g0, g1 = gains[0:1, :], gains[1:2, :]
    for part in range(size // sub):
        rows = pl.ds(part * sub, sub)
        a, b = mine[rows, :], theirs[rows, :]
        if part == 0:
            arrived(0)
        first = jnp.where(even, a, b)
        second = jnp.where(even, b, a)
        attn = mm(first[:, :dim], w_ref[0, place_out, :])
        attn += mm(second[:, :dim], w_ref[1, place_out, :])
        attn += mm(first[:, dim:], w_ref[2, place_out, :])
        attn += mm(second[:, dim:], w_ref[3, place_out, :])
        unit_one, scale_one = norm_parts(tok_ref[rows, :].astype(F32) + attn)
        normed = unit_one * g0 + shifts[0:1, :]
        normed_low = normed.astype(BF)
        branch = down_bias[...]
        slopes = []
        if part == 0:
            arrived(1)
            arrived(2)
        for q in range(heads):
            bias = (
                w_ref[q, place_bias : place_bias + 1, :hid].astype(F32)
                + w_ref[q, place_bias : place_bias + 1, hid : 2 * hid].astype(F32)
                + w_ref[q, place_bias + 1 : place_bias + 2, :hid].astype(F32)
            )
            pre = mm_nt(normed_low, w_ref[q, place_up, :]) + bias
            cdf = 0.5 * (1.0 + lax.erf(pre * 0.7071067811865476))
            slopes.append(cdf + pre * (jnp.exp(-0.5 * pre * pre) * 0.3989422804014327))
            branch = branch + mm((pre * cdf).astype(BF), w_ref[q, :hid, :])
        unit_two, scale_two = norm_parts(normed + branch)
        out_ref[rows, :] = (unit_two * g1 + shifts[1:2, :]).astype(BF)
        grad_mixed = norm_back(cot_ref[rows, :].astype(F32), unit_two, scale_two, g1)
        mixed_low = grad_mixed.astype(BF)
        grad_normed = grad_mixed
        for q in range(heads):
            grad_pre = mm_nt(mixed_low, w_ref[q, :hid, :]) * slopes[q]
            grad_normed = grad_normed + mm(grad_pre.astype(BF), w_ref[q, place_up, :])
        grad_sum = norm_back(grad_normed, unit_one, scale_one, g0)
        da_ref[rows, :] = grad_sum
        sum_low = grad_sum.astype(BF)
        for head in range(2):
            cols = pl.ds(head * dim, dim)
            grad_out = mm_nt(sum_low, w_ref[2 * head + parity, place_out, :]).astype(BF)
            pack_ref[rows, cols] = grad_out
            delta = jnp.sum(grad_out.astype(F32) * wide_ref[rows, cols], axis=1, keepdims=True)
            delta_ref[head : head + 1, rows] = line_of(jnp.broadcast_to(delta, (sub, 128)))
    row = size
    for head in range(2):
        for ref in (lse_ref, delta_ref):
            row = store_line(pack_ref, row, ref[head : head + 1, :])


def feed(meta, mine, theirs, wide_out, lse, tokens, cotangent, w, down_bias, gains, shifts):
    size, width = tokens.shape
    dim = mine.shape[1] // 2
    return pl.pallas_call(
        feed_kernel,
        out_shape=(
            jax.ShapeDtypeStruct((size, width), BF),
            jax.ShapeDtypeStruct((size, width), F32),
            jax.ShapeDtypeStruct((size + STATS, 2 * dim), BF),
            jax.ShapeDtypeStruct((2, size), F32),
        ),
        in_specs=[smem()] + [vmem()] * 9 + [hbm()] * 4,
        out_specs=[vmem()] * 4,
        scratch_shapes=[pltpu.VMEM((4,) + w[0].shape, BF), pltpu.SemaphoreType.DMA((4, 3))],
        compiler_params=params(),
        cost_estimate=cost(3e9, 8e6, 1e6),
        name="feed",
    )(meta, mine, theirs, wide_out, lse, tokens, cotangent, down_bias, gains, shifts, *w)


def low_grads(scores, factor, shift, grads, delta):
    count = scores.shape[1] // 128
    probs = jnp.exp2(scores * factor - wide(shift, count))
    return (probs * (grads - wide(delta, count))).astype(BF)


def token_query_grad_kernel(
    data_count,
    factor,
    meta,
    starts,
    q_ref,
    ids_ref,
    lse_ref,
    delta_ref,
    do_ref,
    acc_in,
    w_ref,
    mine_low,
    mine_high,
    theirs_low,
    theirs_high,
    dq_ref,
    flag,
    acc_ref,
    x_ref,
    id_ref,
    lse_cols,
    delta_cols,
    sem,
):
    raise_flag(flag)
    size, dim = q_ref.shape[1], q_ref.shape[2] // 2
    base = meta[0] * size
    first, last = key_range(starts, base, base + size, data_count)
    first, last = first // size, (last + size - 1) // size
    gathered = (mine_low, mine_high, theirs_low, theirs_high)
    fetch_shards(meta, first, last, gathered, x_ref, sem)
    for h in range(2):
        lse_cols[h] = column_of(lse_ref[h : h + 1, :])
        delta_cols[h] = column_of(delta_ref[h : h + 1, :])
    acc_ref[...] = acc_in[...]
    id_ref[...] = column_of(ids_ref[meta[1]])

    def step(shard, carry):
        raw_rows, line = load_shard(meta, shard, gathered, x_ref, sem)
        kv = mm(raw_rows, w_ref[...]).astype(BF)
        mask = wide(id_ref[...], size // 128) == line
        raw, grads, low = [], [], []
        for h in range(2):
            raw.append(mm_nt(q_ref[0, :, h * dim : (h + 1) * dim], kv[:, h * dim : (h + 1) * dim]))
            grads.append(
                mm_nt(
                    do_ref[pl.ds(0, size), h * dim : (h + 1) * dim],
                    kv[:, (2 + h) * dim : (3 + h) * dim],
                )
            )
        for h in range(2):
            scores = jnp.where(mask, raw[h], NEGATIVE)
            low.append(low_grads(scores, factor, lse_cols[h], grads[h], delta_cols[h]))
        for h in range(2):
            acc_ref[h] += mm(low[h], kv[:, h * dim : (h + 1) * dim])
        return carry

    lax.fori_loop(first, last, step, 0)
    for h in range(2):
        dq_ref[:, pl.ds(h * dim, dim)] = acc_ref[h] * dim ** (-0.5)


def token_query_grad(
    meta, starts, q_own, ids_rows, lse, delta, pack, acc, mine, theirs, weights, factor, data_count
):
    size, dim = q_own.shape[1], q_own.shape[2] // 2
    return pl.pallas_call(
        functools.partial(token_query_grad_kernel, data_count, factor),
        out_shape=(jax.ShapeDtypeStruct((size, 2 * dim), F32), flag_shape()),
        in_specs=[smem()] * 2 + [vmem()] * 7 + [hbm()] * 4,
        out_specs=[vmem()] * 2,
        scratch_shapes=[
            pltpu.VMEM((2, size, dim), F32),
            shard_scratch(mine),
            pltpu.VMEM((size, 128), F32),
            pltpu.VMEM((2, size, 128), F32),
            pltpu.VMEM((2, size, 128), F32),
            pltpu.SemaphoreType.DMA((2 * mine[0].shape[0], 2)),
        ],
        compiler_params=params(*mine, *theirs),
        cost_estimate=cost(6e9, 16e6, 4e6),
        name="token_query_grad",
    )(
        meta,
        starts,
        q_own,
        ids_rows,
        lse,
        delta,
        pack,
        acc,
        weights,
        *mine,
        *theirs,
    )


def prompt_query_grad_kernel(
    block,
    factor,
    meta,
    local,
    table,
    q_ref,
    ids_ref,
    lse_in,
    delta_in,
    pack_own,
    pack_other,
    _,
    w_ref,
    mine_low,
    mine_high,
    theirs_low,
    theirs_high,
    dq_ref,
    send_ref,
    acc_ref,
    lse_ref,
    delta_ref,
    do_ref,
    raws,
    kv_ref,
    id_ref,
    state,
    sem,
):
    size, dim = q_ref.shape[1], q_ref.shape[2] // 2
    rows_per = size // (2 * dim)
    sources = (mine_low, mine_high, theirs_low, theirs_high)
    fetch_prompts(meta, local, table, sources, raws, state, sem)
    acc_ref[...] = jnp.zeros(acc_ref.shape, F32)
    for h in range(2):
        lse_ref[0, h] = column_of(lse_in[h : h + 1, :])
        delta_ref[0, h] = column_of(delta_in[h : h + 1, :])
    do_ref[0] = pack_own[pl.ds(0, size), :]
    do_ref[1] = pack_other[pl.ds(0, size), :]
    for h in range(2):
        for kind, ref in enumerate((lse_ref, delta_ref)):
            row = size + (h * 2 + kind) * 3 * rows_per
            ref[1, h] = column_of(load_line(pack_other, row, size))
    for slot in range(2):
        id_ref[slot] = column_of(ids_ref[meta[1] ^ slot])

    def prepare(number):
        project_prompt(meta, number, sources, raws, w_ref, kv_ref, state, sem)

    def update(slot, rows, data, number):
        mask = id_ref[slot, rows, :] == data.astype(F32)
        raw, grads, low = [], [], []
        for h in range(2):
            cols = pl.ds(h * dim, dim)
            raw.append(mm_nt(q_ref[slot, rows, cols], kv_ref[number, :, cols]))
            value = kv_ref[number, :, pl.ds((2 + h) * dim, dim)]
            grads.append(mm_nt(do_ref[slot, rows, cols], value))
        for h in range(2):
            shift = jnp.where(mask, lse_ref[slot, h, rows, :], -NEGATIVE)
            scores = prompt_mask(meta, raw[h], block)
            low.append(low_grads(scores, factor, shift, grads[h], delta_ref[slot, h, rows, :]))
        for h in range(2):
            acc_ref[slot, h, rows, :] += mm(low[h], kv_ref[number, :, pl.ds(h * dim, dim)])

    visit_prompts(meta, local, table, size, prepare, update)
    for h in range(2):
        cols = pl.ds(h * dim, dim)
        dq_ref[h] = acc_ref[0, h]
        send_ref[:, cols] = (acc_ref[1, h] * dim ** (-0.5)).astype(BF)


def prompt_query_grad(
    meta,
    local,
    table,
    q_own,
    ids_rows,
    lse,
    delta,
    pack,
    pack_other,
    flag,
    prompt_mine,
    prompt_theirs,
    weights,
    factor,
    block,
):
    size, dim = q_own.shape[1], q_own.shape[2] // 2
    buffers, flags = prompt_scratch(prompt_mine, dim, block)
    return pl.pallas_call(
        functools.partial(prompt_query_grad_kernel, block, factor),
        out_shape=(
            jax.ShapeDtypeStruct((2, size, dim), F32),
            jax.ShapeDtypeStruct((size, 2 * dim), BF),
        ),
        in_specs=[smem()] * 3 + [vmem()] * 8 + [hbm()] * 4,
        out_specs=[vmem()] * 2,
        scratch_shapes=[
            pltpu.VMEM((2, 2, size, dim), F32),
            pltpu.VMEM((2, 2, size, 128), F32),
            pltpu.VMEM((2, 2, size, 128), F32),
            pltpu.VMEM((2, size, 2 * dim), BF),
            *buffers,
            pltpu.VMEM((2, size, 128), F32),
            *flags,
        ],
        compiler_params=params(*prompt_mine, *prompt_mine, *prompt_mine, *prompt_mine),
        cost_estimate=cost(6e9, 16e6, 4e6),
        name="prompt_query_grad",
    )(
        meta,
        local,
        table,
        q_own,
        ids_rows,
        lse,
        delta,
        pack,
        pack_other,
        flag,
        weights,
        *prompt_mine,
        *prompt_theirs,
    )


def half_shard(meta, index, q_ref, ids_ref, low_ref, high_ref):
    slots, rows, double = low_ref.shape
    half = q_ref.shape[1]
    size = rows - STATS
    shard, part = index // 2, index % 2
    slot = slot_of(shard ^ meta[0], meta[2], bit_orders(2 * slots))
    other = slot_of(shard ^ meta[0], 1 - meta[2], bit_orders(2 * slots))
    query = q_ref[jnp.where(part == meta[2], slot * 2, other * 2 + 1)]
    in_low = slot < slots
    place_low, place_high = jnp.minimum(slot, slots - 1), jnp.maximum(slot - slots, 0)
    span = pl.ds(pl.multiple_of(part * half, half), half)
    grad = jnp.where(in_low, low_ref[place_low, span, :], high_ref[place_high, span, :])
    line = ids_ref[slot]
    line = jnp.where(part == 0, line[:, :half], line[:, half : 2 * half])
    tail = pl.ds(size, STATS)
    stats = jnp.where(in_low, low_ref[place_low, tail, :], high_ref[place_high, tail, :])
    stats = stats.astype(F32)
    rows_per = size // double

    def stat(head, kind):
        total = 0.0
        for place in range(3):
            row = ((head * 2 + kind) * 3 + place) * rows_per
            term = stats[row : row + 1, :]
            for i in range(1, rows_per):
                term = jnp.where(part == i, stats[row + i : row + i + 1, :], term)
            total = total + term
        return total

    return query, grad, line, stat


def key_update(query, grad, kv_ref, mask, rows_mask, stat, factor, dk_ref, dv_ref):
    dim = query.shape[1] // 2
    cols = [slice(h * dim, (h + 1) * dim) for h in range(2)]
    raw = [mm_nt(kv_ref[:, cols[h]], query[:, cols[h]]) for h in range(2)]
    grads = [mm_nt(kv_ref[:, pl.ds((2 + h) * dim, dim)], grad[:, cols[h]]) for h in range(2)]
    probs, low = [], []
    for h in range(2):
        shift = stat(h, 0)
        scores = raw[h]
        if rows_mask is None:
            shift = jnp.where(mask, shift, -NEGATIVE)
        else:
            scores = jnp.where(rows_mask, scores, NEGATIVE)
        p = jnp.exp2(scores * factor - shift)
        probs.append(p.astype(BF))
        low.append((p * (grads[h] - stat(h, 1))).astype(BF))
    for h in range(2):
        dv_ref[:, cols[h]] += mm(probs[h], grad[:, cols[h]])
        dk_ref[:, cols[h]] += mm(low[h], query[:, cols[h]])


def prompt_grad_kernel(
    data_count,
    factor,
    meta,
    starts,
    table,
    q_ref,
    ids_ref,
    low_ref,
    high_ref,
    kv_ref,
    _,
    w_ref,
    keep_ref,
    send_ref,
    dk_ref,
    dv_ref,
):
    half = q_ref.shape[1]
    block, width = kv_ref.shape[0], w_ref.shape[0]
    dim = kv_ref.shape[1] // 4
    number = meta[0] * block // PLEN
    dk_ref[...] = jnp.zeros(dk_ref.shape, F32)
    dv_ref[...] = jnp.zeros(dv_ref.shape, F32)

    def visit(data, carry):
        begin, end = starts[data], starts[data + 1]

        @pl.when((table[meta[1], data] == number) & (begin < end))
        def _():
            def step(index, inner):
                query, grad, line, stat = half_shard(meta, index, q_ref, ids_ref, low_ref, high_ref)
                key_update(
                    query, grad, kv_ref, line == data.astype(F32), None, stat, factor, dk_ref, dv_ref
                )
                return inner

            lax.fori_loop(begin // half, (end + half - 1) // half, step, 0)

        return carry

    lax.fori_loop(0, data_count, visit, 0)
    grads = jnp.concatenate(
        [(dk_ref[...] * dim ** (-0.5)).astype(BF), dv_ref[...].astype(BF)], axis=1
    )
    split = width // 2
    parity = meta[2]
    send = w_ref[pl.ds(pl.multiple_of((1 - parity) * split, split), split), :]
    keep = w_ref[pl.ds(pl.multiple_of(parity * split, split), split), :]
    send_ref[...] = mm_nt(grads, send).astype(BF)
    keep_ref[...] = mm_nt(grads, keep)


def prompt_grad(meta, starts, table, q_all, ids_all, packs, kv, flag, weights, factor, data_count):
    block, width = kv.shape[0], weights.shape[0]
    dim = kv.shape[1] // 4
    return pl.pallas_call(
        functools.partial(prompt_grad_kernel, data_count, factor),
        out_shape=(
            jax.ShapeDtypeStruct((block, width // 2), F32),
            jax.ShapeDtypeStruct((block, width // 2), BF),
        ),
        in_specs=[smem()] * 3 + [vmem()] * 7,
        out_specs=[vmem(), vmem()],
        scratch_shapes=[
            pltpu.VMEM((block, 2 * dim), F32),
            pltpu.VMEM((block, 2 * dim), F32),
        ],
        compiler_params=params(q_all, *packs),
        cost_estimate=cost(6e9, 16e6, 4e6),
        name="prompt_grad",
    )(meta, starts, table, q_all, ids_all, *packs, kv, flag, weights)


def token_grad_kernel(
    data_count,
    factor,
    meta,
    starts,
    q_ref,
    ids_ref,
    low_ref,
    high_ref,
    kv_ref,
    own_ids,
    dq_ref,
    dq_other,
    wq_ref,
    wkv_ref,
    out_ref,
    flag,
    dk_ref,
    dv_ref,
    id_ref,
):
    raise_flag(flag)
    size = kv_ref.shape[0]
    half = q_ref.shape[1]
    dim = kv_ref.shape[1] // 4
    base = meta[0] * size
    first, last = key_range(starts, base, base + size, data_count)
    dk_ref[...] = jnp.zeros(dk_ref.shape, F32)
    dv_ref[...] = jnp.zeros(dv_ref.shape, F32)
    id_ref[...] = column_of(own_ids[meta[1]])

    def step(index, carry):
        query, grad, line, stat = half_shard(meta, index, q_ref, ids_ref, low_ref, high_ref)
        mask = wide(id_ref[...], half // 128) == line
        key_update(query, grad, kv_ref, None, mask, stat, factor, dk_ref, dv_ref)
        return carry

    lax.fori_loop(first // half, (last + half - 1) // half, step, 0)
    dq = (dq_ref[...] + dq_other[...].astype(F32)).astype(BF)
    grads = jnp.concatenate(
        [(dk_ref[...] * dim ** (-0.5)).astype(BF), dv_ref[...].astype(BF)], axis=1
    )
    out_ref[...] = (mm_nt(dq, wq_ref[...]) + mm_nt(grads, wkv_ref[...])).astype(BF)


def token_grad(
    meta, starts, q_all, ids_all, packs, kv_own, ids_rows, dq, weights, factor, data_count
):
    size, dim = kv_own.shape[0], kv_own.shape[1] // 4
    width = weights[0].shape[0]
    return pl.pallas_call(
        functools.partial(token_grad_kernel, data_count, factor),
        out_shape=(jax.ShapeDtypeStruct((size, width), BF), flag_shape()),
        in_specs=[smem()] * 2 + [vmem()] * 10,
        out_specs=[vmem()] * 2,
        scratch_shapes=[
            pltpu.VMEM((size, 2 * dim), F32),
            pltpu.VMEM((size, 2 * dim), F32),
            pltpu.VMEM((size, 128), F32),
        ],
        compiler_params=params(spare=VMEM_LIMIT),
        cost_estimate=cost(4e9, 16e6, 4e6),
        name="token_grad",
    )(meta, starts, q_all, ids_all, *packs, kv_own, ids_rows, *dq, *weights)


def sum_prompt_kernel(a_ref, b_ref, _, sum_ref, square_ref):
    low = (a_ref[...].astype(F32) + b_ref[...].astype(F32)).astype(BF)
    sum_ref[...] = low
    value = low.astype(F32)
    square_ref[...] = jnp.broadcast_to(jnp.sum(value * value, keepdims=True), square_ref.shape)


def sum_prompt(a, b, flag):
    return pl.pallas_call(
        sum_prompt_kernel,
        out_shape=(
            jax.ShapeDtypeStruct(a.shape, BF),
            jax.ShapeDtypeStruct((8, 128), F32),
        ),
        in_specs=[vmem()] * 3,
        out_specs=[vmem(), vmem()],
        compiler_params=params(),
        cost_estimate=cost(4 * a.size, 6 * a.size),
        name="sum_prompt",
    )(a, b, flag)


def optimizer_kernel(
    meta,
    biases,
    mine,
    theirs,
    squares,
    prompts,
    one_in,
    two_in,
    clip_out,
    one_out,
    two_out,
    new_out,
    norm_ref,
    held,
    sem,
):
    even = meta[2] == 0
    block = prompts.shape[0]
    tiles = sem.shape[1]
    tile = block // tiles
    norm_ref[...] = jnp.sqrt(squares[...])
    norm = norm_ref[0:1, :]
    factor = jnp.minimum(1.0, CLIP_NORM / (norm + 1e-06))
    copies = []
    for index in range(tiles):
        rows = pl.ds(index * tile, tile)
        a, b = mine[rows, :].astype(F32), theirs[rows, :].astype(F32)
        grads = jnp.concatenate([jnp.where(even, a, b), jnp.where(even, b, a)], axis=1)
        clipped = grads * wide(factor, grads.shape[1] // 128)
        new_one = BETA_ONE * one_in[rows, :] + (1.0 - BETA_ONE) * clipped
        new_two = BETA_TWO * two_in[rows, :] + (1.0 - BETA_TWO) * clipped * clipped
        first_hat = new_one / biases[0]
        second_hat = new_two / biases[1]
        held[0, rows, :] = clipped
        held[1, rows, :] = new_one
        held[2, rows, :] = new_two
        held[3, rows, :] = prompts[rows, :] * (
            1.0 - LEARNING_RATE * DECAY_RATE
        ) - LEARNING_RATE * first_hat / (jnp.sqrt(second_hat) + EPSILON)
        for place, out in enumerate((clip_out, one_out, two_out, new_out)):
            copies.append(
                pltpu.make_async_copy(held.at[place, rows], out.at[rows], sem.at[place, index])
            )
            copies[-1].start()
    for copy in copies:
        copy.wait()


def optimizer(meta, biases, mine, theirs, squares, prompts, moment_one, moment_two):
    block, width = prompts.shape
    tiles = 5 if block % 40 == 0 else 1
    shape = jax.ShapeDtypeStruct((block, width), F32)
    return pl.pallas_call(
        optimizer_kernel,
        out_shape=(shape,) * 4 + (jax.ShapeDtypeStruct(squares.shape, F32),),
        in_specs=[smem(), smem()] + [vmem()] * 6,
        out_specs=[hbm()] * 4 + [vmem()],
        scratch_shapes=[
            pltpu.VMEM((4, block, width), F32),
            pltpu.SemaphoreType.DMA((4, tiles)),
        ],
        compiler_params=params(prompts, prompts),
        cost_estimate=cost(20 * block * width, 32 * block * width),
        name="optimizer",
    )(meta, biases, mine, theirs, squares, prompts, moment_one, moment_two)


def per_device(
    tokens,
    cotangent,
    dataset_ids,
    prompt_map,
    attn_in,
    attn_out,
    up_weight,
    up_bias,
    down_weight,
    down_bias,
    norm_gains,
    norm_shifts,
    prompts,
    moment_one,
    moment_two,
    step_count,
):
    size, width = tokens.shape[1:]
    dim = attn_in.shape[2]
    hid = up_weight.shape[1]
    data_count = prompt_map.shape[1]
    row_count = lax.axis_size("rows")
    head_count = lax.axis_size("head")
    factor = dim ** (-0.5) * LOG2E
    row = lax.axis_index("rows")
    head = lax.axis_index("head")
    batch, parity = head // 2, head % 2
    half = size // 2
    meta = jnp.stack([row, batch, parity]).astype(jnp.int32)

    block = prompts.shape[0]

    part = half_rows(block)
    prompt_own = lax.dynamic_slice(
        prompts, (batch * (block - part), parity * (width // 2)), (part, width // 2)
    ).astype(BF)
    in_other = swap_head(attn_in, 2, head_count)
    ids = jnp.where(batch == 0, dataset_ids[0], dataset_ids[1])
    tok_half = lax.dynamic_slice(tokens, (batch, parity * half, 0), (1, half, width))[0]
    id_rows = jnp.broadcast_to(ids.astype(BF)[None, :], (PACK, size))
    shard = jnp.concatenate([tok_half, id_rows], axis=0)

    bias_high = lax.reduce_precision(up_bias, 8, 7)
    bias_rest = up_bias - bias_high
    bias_mid = lax.reduce_precision(bias_rest, 8, 7)
    bias_low = bias_rest - bias_mid
    bias_rows = jnp.concatenate([bias_high, bias_mid, bias_low, bias_low]).astype(BF)
    bias_rows = jnp.pad(bias_rows.reshape(-1, width), ((0, PACK - 4 * hid // width), (0, 0)))
    w_own = jnp.concatenate([down_weight, attn_out, up_weight.T, bias_rows], axis=0)
    in_other, w_own = lax.optimization_barrier((in_other, w_own))
    w_along = swap_head(w_own, 2, head_count)
    step_value = step_count.astype(F32)
    biases = jnp.stack(
        [1.0 - jnp.power(BETA_ONE, step_value), 1.0 - jnp.power(BETA_TWO, step_value)]
    )
    numbers = jnp.arange(data_count + 1, dtype=jnp.int32)
    local = jnp.sum((dataset_ids[:, None, :] < numbers[None, :, None]).astype(jnp.int32), axis=2)
    ids_rows = dataset_ids.astype(F32).reshape(2, 1, size)
    tied = {}

    orders, later = bit_orders(row_count), prompt_orders(row_count)
    stages = len(orders[0])
    held, prompt_held = shard[None], prompt_own[None]
    tok = lax.dynamic_index_in_dim(tokens, batch, 0, keepdims=False)
    cot = lax.dynamic_index_in_dim(cotangent, batch, 0, keepdims=False)

    def prompt_stage(place):
        other = gather_stage(prompt_held, place, later, row_count, head_count)
        return jnp.concatenate([prompt_held, other], axis=0)

    for place in range(stages):
        if place == stages - 1:
            held, in_other, meta, (biases, local, ids_rows, tok, cot) = lax.optimization_barrier(
                (held, in_other, meta, (biases, local, ids_rows, tok, cot))
            )
        if place != 1:
            held, prompt_held = lax.optimization_barrier((held, prompt_held))
        other = gather_stage(held, place, orders, row_count, head_count)
        if place != 1:
            prompt_held = prompt_stage(max(place - 1, 0))
        if place < stages - 1:
            held = jnp.concatenate([held, other], axis=0)
        if place == 0:
            held, prompt_held = lax.optimization_barrier((held, prompt_held))
    theirs_low = swap_head(held, 1, head_count)
    other, prompt_held, w_along = lax.optimization_barrier((other, prompt_held, w_along))
    mine = (held, other)
    prompt_high = gather_stage(prompt_held, stages - 1, later, row_count, head_count)
    theirs = (theirs_low, swap_head(other, 1, head_count))
    w_core = swap_head(w_own, 1, head_count)
    w_far = swap_head(w_along, 1, head_count)

    ids_all = jnp.concatenate([bank[:, half, :size] for bank in mine], axis=0).astype(F32)
    starts = jnp.sum(
        (ids_all.reshape(1, -1) < numbers.astype(F32)[:, None]).astype(jnp.int32), axis=1
    )
    ids_all = ids_all.reshape(row_count, 1, size)
    q_own, kv_own, w_q, w_kv, *state, flag = token_forward(
        meta, starts, tokens, ids_rows, mine, theirs, attn_in, in_other, factor, data_count
    )
    prompt_theirs_low = swap_head(prompt_held, 1, head_count)
    prompt_high, flag, prompt_theirs_low, w_core, w_far = lax.optimization_barrier(
        (prompt_high, flag, prompt_theirs_low, w_core, w_far)
    )
    prompt_mine = (prompt_held, prompt_high)
    prompt_theirs = (prompt_theirs_low, swap_head(prompt_high, 1, head_count))
    wide_half, lse_half, send_half = prompt_forward(
        meta,
        local,
        prompt_map,
        q_own,
        ids_rows,
        state,
        flag,
        prompt_mine,
        prompt_theirs,
        w_kv,
        factor,
        block,
    )
    prompt_low, send_half = lax.optimization_barrier((prompts.astype(BF), send_half))
    prompt_kv = jnp.dot(prompt_low, w_kv, preferred_element_type=F32).astype(BF)
    o_mine, wide_out, lse = join_halves(wide_half, lse_half, swap_head(send_half, 2, head_count))
    o_mine, prompt_kv = lax.optimization_barrier((o_mine, prompt_kv))
    o_theirs = swap_head(o_mine, 1, head_count)
    out, grad_sum, pack, delta = feed(
        meta,
        o_mine,
        o_theirs,
        wide_out,
        lse,
        tok,
        cot,
        (w_own, w_along, w_core, w_far),
        down_bias.reshape(1, width),
        norm_gains,
        norm_shifts,
    )
    pack_other = swap_head(pack, 2, head_count)

    def tie_query_grads(stages_left, held):
        if stages_left == 3:
            held, here = lax.optimization_barrier((held, w_q))
            tied["q"], tied["flag"] = project_query(mine, theirs, here)
        if stages_left == 2:
            held, other, flag = lax.optimization_barrier((held, pack_other, tied["flag"]))
            tied["dq"] = prompt_query_grad(
                meta,
                local,
                prompt_map,
                q_own,
                ids_rows,
                lse,
                delta,
                pack,
                other,
                flag,
                prompt_mine,
                prompt_theirs,
                w_kv,
                factor,
                block,
            )
        if stages_left == 1:
            acc, dq_send = tied["dq"]
            held, dq_send, ids_here = lax.optimization_barrier((held, dq_send, ids_rows))
            tied["dq_other"] = swap_head(dq_send, 2, head_count)
            tied["dq"], tied["flag"] = token_query_grad(
                meta,
                starts,
                q_own,
                ids_here,
                lse,
                delta,
                pack,
                acc,
                mine,
                theirs,
                w_kv,
                factor,
                data_count,
            )
        return held

    out_half = lax.dynamic_slice_in_dim(out, parity * half, half, 0)
    out_half = swap_head(out_half, 2, head_count)
    packs = gather_rows(pack, row_count, head_count, tie_query_grads)
    q_all = tied["q"]
    dq = tied["dq"]
    packs, dq_other, out_half, flag = lax.optimization_barrier(
        (packs, tied["dq_other"], out_half, tied["flag"])
    )
    keep, send = prompt_grad(
        meta, starts, prompt_map, q_all, ids_all, packs, prompt_kv, flag, w_kv, factor, data_count
    )

    pair = keep + swap_head(send, 1, head_count).astype(F32)
    pair_low = lax.reduce_precision(pair, 8, 7).astype(BF)
    pair_low, ids_here = lax.optimization_barrier((pair_low, ids_rows))
    pair_other = swap_head(pair_low, 2, head_count)
    out_rest = swap_head(out_half, 1, head_count)
    token_part, flag = token_grad(
        meta,
        starts,
        q_all,
        ids_all,
        packs,
        kv_own,
        ids_here,
        (dq, dq_other),
        (w_q, w_kv),
        factor,
        data_count,
    )
    pair_other, flag = lax.optimization_barrier((pair_other, flag))
    full_low, squares = sum_prompt(pair_low, pair_other, flag)
    full_other = swap_head(full_low, 1, head_count)

    def both_batches(own, here, rest):
        other = jnp.concatenate(
            [jnp.where(parity == 0, here, rest), jnp.where(parity == 0, rest, here)], axis=0
        )
        first = jnp.where(batch == 0, own, other)
        return jnp.stack([first, jnp.where(batch == 0, other, own)]).astype(F32)

    core_sum = token_part.astype(F32) + swap_head(token_part, 1, head_count).astype(F32)
    total = lax.reduce_precision(grad_sum + core_sum, 8, 7).astype(BF)
    mine_half = lax.dynamic_slice_in_dim(total, parity * half, half, 0)
    other_half = swap_head(mine_half, 2, head_count)
    layer_out = both_batches(out, out_half, out_rest)

    def tie_sum(stages_done, value):
        if stages_done == 1:
            value, _ = lax.optimization_barrier((value, total))
        if stages_done == 2:
            value, tied["out"] = lax.optimization_barrier((value, layer_out))
        return value

    squares = xor_sum(squares, row_count, head_count, tie_sum)
    clipped, new_one, new_two, new_prompts, norm = optimizer(
        meta, biases, full_low, full_other, squares, prompts, moment_one, moment_two
    )
    other_half, norm = lax.optimization_barrier((other_half, norm))
    input_grad = both_batches(total, other_half, swap_head(other_half, 1, head_count))
    return (tied["out"], input_grad, clipped, norm[0, 0], new_one, new_two, new_prompts)


def solution(mesh):
    in_specs = (
        P(None, "rows", None),
        P(None, "rows", None),
        P(None, "rows"),
        P(),
        P(None, None, "head"),
        P("head", None),
        P(None, "head"),
        P("head"),
        P("head", None),
        P(),
        P(),
        P(),
        P("rows", None),
        P("rows", None),
        P("rows", None),
        P(),
    )
    out_specs = (
        P(None, "rows", None),
        P(None, "rows", None),
        P("rows", None),
        P(),
        P("rows", None),
        P("rows", None),
        P("rows", None),
    )
    return jax.shard_map(
        per_device, mesh=mesh, in_specs=in_specs, out_specs=out_specs, check_vma=False
    )
```

```python
import functools

import jax
import jax.numpy as jnp
from jax import lax
from jax.experimental import pallas as pl
from jax.experimental.pallas import tpu as pltpu
from jax.sharding import PartitionSpec as P

PLEN = 1000
NEGATIVE = -1e30
BETA_ONE = 0.9
BETA_TWO = 0.999
LEARNING_RATE = 0.5
DECAY_RATE = 0.01
EPSILON = 1e-08
CLIP_NORM = 1.0
LOG2E = 1.4426950408889634
PACK = 16
STATS = 32
VMEM_LIMIT = 60 * 1024 * 1024
BF = jnp.bfloat16
F32 = jnp.float32
BOTH = ("rows", "head")


def params(*operands, spare=20 << 20):
    held = sum(x.size * x.dtype.itemsize for x in operands)
    return pltpu.CompilerParams(vmem_limit_bytes=min(VMEM_LIMIT, held + spare))


def cost(flops, bytes_accessed, transcendentals=0):
    return pl.CostEstimate(
        flops=int(flops), bytes_accessed=int(bytes_accessed), transcendentals=int(transcendentals)
    )


def mm(a, b):
    return lax.dot_general(a, b, (((1,), (0,)), ((), ())), preferred_element_type=F32)


def mm_nt(a, b):
    return lax.dot_general(a, b, (((1,), (1,)), ((), ())), preferred_element_type=F32)


def split3(value):
    high = value.astype(BF)
    rest = value - high.astype(F32)
    mid = rest.astype(BF)
    low = (rest - mid.astype(F32)).astype(BF)
    return high, mid, low


def bit_orders(row_count):
    bits = row_count.bit_length() - 1
    return ([0] + list(range(bits - 1, 0, -1)), list(range(bits - 1, 0, -1)) + [0])


def prompt_orders(row_count):
    bits = row_count.bit_length() - 1
    if bits < 2:
        return bit_orders(row_count)
    high = list(range(bits - 1, 1, -1))
    return (high + [0, 1], [1] + high + [0])


def slot_of(offset, parity, orders):
    def mapped(order):
        total = 0
        for place, bit in enumerate(order):
            total = total + (((offset >> bit) & 1) << place)
        return total

    return jnp.where(parity == 0, mapped(orders[0]), mapped(orders[1]))


def gather_stage(held, place, orders, row_count, head_count):
    pairs = []
    for row in range(row_count):
        for head in range(head_count):
            bit = orders[head % 2][place]
            pairs.append((row * head_count + head, (row ^ (1 << bit)) * head_count + head))
    return lax.ppermute(held, BOTH, pairs)


def gather_rows(block, row_count, head_count, before_send):
    held = block[None]
    orders = bit_orders(row_count)
    stages = len(orders[0])
    for place in range(stages):
        held = before_send(stages - place, held)
        other = gather_stage(held, place, orders, row_count, head_count)
        if place < stages - 1:
            held = jnp.concatenate([held, other], axis=0)
    return held, other


def xor_sum(value, row_count, head_count, after):
    def moved(mask):
        count = row_count * head_count
        return lax.ppermute(value, BOTH, [(i, i ^ mask) for i in range(count)])

    masks = [1]
    bit = head_count
    while bit < row_count * head_count:
        masks.append(bit)
        bit = bit * 2
    done = 0
    while masks:
        if len(masks) == 1:
            value = value + moved(masks[0])
        else:
            first, second, both = (moved(m) for m in (masks[0], masks[1], masks[0] ^ masks[1]))
            value = (value + first) + (second + both)
        masks = masks[2:]
        done = done + 1
        value = after(done, value)
    return value


def swap_head(value, mask, head_count):
    return lax.ppermute(value, "head", [(i, i ^ mask) for i in range(head_count)])


def smem():
    return pl.BlockSpec(memory_space=pltpu.SMEM)


def vmem():
    return pl.BlockSpec(memory_space=pltpu.VMEM)


def hbm():
    return pl.BlockSpec(memory_space=pltpu.HBM)


def flag_shape():
    return jax.ShapeDtypeStruct((8, 128), F32)


def raise_flag(ref):
    ref[...] = jnp.zeros(ref.shape, F32)


def join_weights(meta, own, other, target, kinds):
    dim = own.shape[2]
    for index, kind in enumerate(kinds):
        for place in range(2):
            column = (index * 2 + place) * dim
            target[:, column : column + dim] = jnp.where(meta[1] == place, own[kind], other[kind])


def wide(value, count):
    return jnp.concatenate([value] * count, axis=1)


def line_of(columns):
    return jnp.transpose(columns)[0:1, :]


def column_of(line):
    return jnp.transpose(jnp.broadcast_to(line, (128, line.shape[1])))


def project_query_kernel(a, b, c, d, weights, q_out, flag):
    raise_flag(flag)
    half = a.shape[1] - PACK
    for high, pair in enumerate(((a, b), (c, d))):
        for place, ref in enumerate(pair):
            q_out[high, 0, place] = mm(ref[0, :half], weights[...]).astype(BF)


def project_query(mine, theirs, weights):
    slots, rows, width = mine[0].shape
    half = rows - PACK
    double = weights.shape[1]
    block = pl.BlockSpec((1, rows, width), lambda g: (g, 0, 0))
    whole = pl.BlockSpec(weights.shape, lambda g: (0, 0))
    out, flag = pl.pallas_call(
        project_query_kernel,
        out_shape=(jax.ShapeDtypeStruct((2, slots, 2, half, double), BF), flag_shape()),
        grid=(slots,),
        in_specs=[block] * 4 + [whole],
        out_specs=[
            pl.BlockSpec((2, 1, 2, half, double), lambda g: (0, g, 0, 0, 0)),
            pl.BlockSpec((8, 128), lambda g: (0, 0)),
        ],
        compiler_params=params(),
        cost_estimate=cost(8 * slots * half * width * double, 8 * slots * half * width),
        name="project_query",
    )(mine[0], theirs[0], mine[1], theirs[1], weights)
    return out.reshape(4 * slots, half, double), flag


def key_range(starts, low, high, data_count):
    first = jnp.int32(1 << 30)
    last = jnp.int32(0)
    for data in range(data_count):
        begin, end = starts[data], starts[data + 1]
        hit = (begin < high) & (end > low) & (begin < end)
        first = jnp.where(hit, jnp.minimum(first, begin), first)
        last = jnp.where(hit, jnp.maximum(last, end), last)
    return first, last


def shard_copies(meta, shard, gathered, x_ref, sem):
    slots = gathered[0].shape[0]
    copies = []
    for place in range(2):
        slot = slot_of(shard ^ meta[0], meta[2] ^ place, bit_orders(2 * slots))
        for bank in range(2):
            here = (slot < slots) if bank == 0 else (slot >= slots)
            source = gathered[place * 2 + bank]
            copy = pltpu.make_async_copy(
                source.at[jnp.where(here, slot - bank * slots, 0)],
                x_ref.at[shard, place],
                sem.at[shard, place],
            )
            copies.append((here, copy))
    return copies


def fetch_shards(meta, first, last, gathered, x_ref, sem):
    def start(shard, carry):
        for here, copy in shard_copies(meta, shard, gathered, x_ref, sem):

            @pl.when(here)
            def _():
                copy.start()

        return carry

    lax.fori_loop(first, last, start, 0)


def load_shard(meta, shard, gathered, x_ref, sem):
    half = x_ref.shape[2] - PACK
    parity = meta[2]
    for place in range(2):
        pltpu.make_async_copy(gathered[0].at[0], x_ref.at[shard, place], sem.at[shard, place]).wait()
    line = x_ref[shard, 0, half : half + 1, :].astype(F32)
    first, second = line[:, :half], line[:, half : 2 * half]
    line = jnp.concatenate(
        [jnp.where(parity == 0, first, second), jnp.where(parity == 0, second, first)], axis=1
    )
    return jnp.concatenate([x_ref[shard, 0, :half, :], x_ref[shard, 1, :half, :]], axis=0), line


def online(scores, factor, mask, m_ref, place):
    old_max = m_ref[place]
    size = old_max.shape[0]
    top = jnp.broadcast_to(jnp.max(scores, axis=1, keepdims=True) * factor, (size, 128))
    new_max = jnp.maximum(old_max, top)
    shift = new_max
    if mask is not None:
        new_max = jnp.where(mask, new_max, old_max)
        shift = jnp.where(mask, new_max, -NEGATIVE)
    m_ref[place] = new_max
    probs = jnp.exp2(scores * factor - wide(shift, scores.shape[1] // 128))
    return probs.astype(BF), jnp.exp2(old_max - new_max)


def accumulate(acc_ref, place, alpha, probs, value):
    with_ones = jnp.concatenate([value, jnp.ones((value.shape[0], 128), BF)], axis=1)
    acc_ref[place] = acc_ref[place] * wide(alpha, with_ones.shape[1] // 128) + mm(probs, with_ones)


def token_forward_kernel(
    data_count,
    factor,
    meta,
    starts,
    ids_ref,
    in_own,
    in_other,
    tok_hbm,
    mine_low,
    mine_high,
    theirs_low,
    theirs_high,
    q_ref,
    kv_own,
    wq_ref,
    wkv_ref,
    m_out,
    l_out,
    acc_out,
    flag,
    m_ref,
    acc_ref,
    x_ref,
    id_ref,
    tok_ref,
    sem,
    tok_sem,
):
    raise_flag(flag)
    size, dim = tok_ref.shape[1], in_own.shape[2]
    tok_copy = pltpu.make_async_copy(tok_hbm, tok_ref, tok_sem)
    tok_copy.start()
    base = meta[0] * size
    first, last = key_range(starts, base, base + size, data_count)
    first, last = first // size, (last + size - 1) // size
    gathered = (mine_low, mine_high, theirs_low, theirs_high)
    fetch_shards(meta, first, last, gathered, x_ref, sem)
    join_weights(meta, in_own, in_other, wq_ref, (0,))
    join_weights(meta, in_own, in_other, wkv_ref, (1, 2))
    tok_copy.wait()
    for slot in range(2):
        q_ref[slot] = mm(tok_ref[meta[1] ^ slot], wq_ref[...]).astype(BF)
    kv_own[...] = mm(tok_ref[meta[1]], wkv_ref[...]).astype(BF)
    m_ref[...] = jnp.full(m_ref.shape, NEGATIVE, F32)
    acc_ref[...] = jnp.zeros(acc_ref.shape, F32)
    id_ref[...] = column_of(ids_ref[meta[1]])
    rows = pl.ds(0, size)

    def step(shard, carry):
        raw_rows, line = load_shard(meta, shard, gathered, x_ref, sem)
        kv = mm(raw_rows, wkv_ref[...]).astype(BF)
        mask = wide(id_ref[...], size // 128) == line
        raw = [
            mm_nt(q_ref[0, :, h * dim : (h + 1) * dim], kv[:, h * dim : (h + 1) * dim])
            for h in range(2)
        ]
        parts = [
            online(jnp.where(mask, raw[h], NEGATIVE), factor, None, m_ref, (h, rows))
            for h in range(2)
        ]
        for h in range(2):
            value = kv[:, (2 + h) * dim : (3 + h) * dim]
            accumulate(acc_ref, (h, rows), parts[h][1], parts[h][0], value)
        return carry

    lax.fori_loop(first, last, step, 0)
    for h in range(2):
        m_out[h : h + 1, :] = line_of(m_ref[h])
        l_out[h : h + 1, :] = line_of(acc_ref[h, :, dim:])
        acc_out[h] = acc_ref[h, :, :dim]


def shard_scratch(banks):
    slots, rows, width = banks[0].shape
    return pltpu.VMEM((2 * slots, 2, rows, width), BF)


def token_forward(meta, starts, tokens, ids_rows, mine, theirs, in_own, in_other, factor, data_count):
    size, width = tokens.shape[1:]
    dim = in_own.shape[2]
    return pl.pallas_call(
        functools.partial(token_forward_kernel, data_count, factor),
        out_shape=(
            jax.ShapeDtypeStruct((2, size, 2 * dim), BF),
            jax.ShapeDtypeStruct((size, 4 * dim), BF),
            jax.ShapeDtypeStruct((width, 2 * dim), BF),
            jax.ShapeDtypeStruct((width, 4 * dim), BF),
            jax.ShapeDtypeStruct((2, size), F32),
            jax.ShapeDtypeStruct((2, size), F32),
            jax.ShapeDtypeStruct((2, size, dim), F32),
            flag_shape(),
        ),
        in_specs=[smem(), smem()] + [vmem()] * 3 + [hbm()] * 5,
        out_specs=[vmem()] * 8,
        scratch_shapes=[
            pltpu.VMEM((2, size, 128), F32),
            pltpu.VMEM((2, size, dim + 128), F32),
            shard_scratch(mine),
            pltpu.VMEM((size, 128), F32),
            pltpu.VMEM(tokens.shape, BF),
            pltpu.SemaphoreType.DMA((2 * mine[0].shape[0], 2)),
            pltpu.SemaphoreType.DMA,
        ],
        compiler_params=params(spare=VMEM_LIMIT),
        cost_estimate=cost(8e9, 8e6, 2e6),
        name="token_forward",
    )(meta, starts, ids_rows, in_own, in_other, tokens, *mine, *theirs)


def half_rows(block):
    return -(-block // 32) * 16


def fetch_prompts(meta, local, table, sources, raws, state, sem):
    pieces = raws.shape[2]
    slots = sources[0].shape[0]
    for number in range(state.shape[0]):
        state[number] = 0
    for batch in range(2):
        for data in range(table.shape[1]):
            number = table[batch, data]
            used = local[batch, data + 1] > local[batch, data]
            state[number] = jnp.where(used, 1, state[number])

    def start(number, carry):
        @pl.when(state[number] == 1)
        def _():
            for piece in range(pieces):
                for place in range(2):
                    shard = number * pieces + piece
                    slot = slot_of(shard ^ meta[0], meta[2] ^ place, prompt_orders(2 * slots))
                    for bank in range(2):

                        @pl.when((slot < slots) if bank == 0 else (slot >= slots))
                        def _():
                            pltpu.make_async_copy(
                                sources[place * 2 + bank].at[slot - bank * slots],
                                raws.at[place, number, piece],
                                sem.at[place, number, piece],
                            ).start()

        return carry

    lax.fori_loop(0, state.shape[0], start, 0)


def project_prompt(meta, number, sources, raws, w_ref, kv_ref, state, sem):
    pieces, block = raws.shape[2:4]

    @pl.when(state[number] == 1)
    def _():
        even = meta[2] == 0
        for piece in range(pieces):
            for place in range(2):
                pltpu.make_async_copy(
                    sources[0].at[0], raws.at[place, number, piece], sem.at[place, number, piece]
                ).wait()
            a, b = raws[0, number, piece], raws[1, number, piece]
            rows = jnp.concatenate([jnp.where(even, a, b), jnp.where(even, b, a)], axis=1)
            kv_ref[number, pl.ds(piece * block, block), :] = mm(rows, w_ref[...]).astype(BF)
        full = pieces * block
        if full < kv_ref.shape[1]:
            kv_ref[number, full:, :] = jnp.zeros((kv_ref.shape[1] - full, kv_ref.shape[2]), BF)
        state[number] = 2


def prompt_mask(meta, scores, block):
    part = half_rows(block)
    pieces = PLEN // block
    doubled = 2 * part - block
    head = min(128, part) if pieces == 1 else scores.shape[1]
    lanes = lax.broadcasted_iota(jnp.int32, (scores.shape[0], head), 1)
    out = (lanes % part < doubled * meta[1]) | (lanes >= pieces * part)
    first = jnp.where(out, NEGATIVE, scores[:, :head])
    if head == scores.shape[1]:
        return first
    return jnp.concatenate([first, scores[:, head:]], axis=1)


def visit_prompts(meta, local, table, size, prepare, update):
    data_count = table.shape[1]

    def visit(index, carry):
        slot, data = index // data_count, index % data_count
        batch = meta[1] ^ slot
        begin, end = local[batch, data], local[batch, data + 1]

        @pl.when(begin < end)
        def _():
            number = table[batch, data]
            prepare(number)
            low = begin // 128
            count = (end + 127) // 128 - low
            for case in range(1, size // 128 + 1):

                @pl.when(count == case)
                def _():
                    rows = pl.ds(pl.multiple_of(low * 128, 128), case * 128)
                    update(slot, rows, data, number)

        return carry

    lax.fori_loop(0, 2 * data_count, visit, 0)


def store_line(ref, row, line):
    width = ref.shape[1]
    for term in split3(line):
        for low in range(0, line.shape[1], width):
            ref[row : row + 1, :] = term[:, low : low + width]
            row = row + 1
    return row


def load_line(ref, row, length):
    width = ref.shape[1]
    rows_per = length // width
    total = 0.0
    for place in range(3):
        first = row + place * rows_per
        pieces = [ref[first + i : first + i + 1, :].astype(F32) for i in range(rows_per)]
        total = total + jnp.concatenate(pieces, axis=1)
    return total


def prompt_forward_kernel(
    block,
    factor,
    meta,
    local,
    table,
    q_ref,
    ids_ref,
    m_in,
    l_in,
    acc_in,
    _,
    w_ref,
    mine_low,
    mine_high,
    theirs_low,
    theirs_high,
    wide_ref,
    lse_ref,
    send_ref,
    m_ref,
    acc_ref,
    raws,
    kv_ref,
    id_ref,
    state,
    sem,
):
    size, dim = q_ref.shape[1], q_ref.shape[2] // 2
    sources = (mine_low, mine_high, theirs_low, theirs_high)
    fetch_prompts(meta, local, table, sources, raws, state, sem)
    for h in range(2):
        m_ref[0, h] = column_of(m_in[h : h + 1, :])
        acc_ref[0, h, :, dim:] = column_of(l_in[h : h + 1, :])
        acc_ref[0, h, :, :dim] = acc_in[h]
    m_ref[1] = jnp.full(m_ref.shape[1:], NEGATIVE, F32)
    acc_ref[1] = jnp.zeros(acc_ref.shape[1:], F32)
    for slot in range(2):
        id_ref[slot] = column_of(ids_ref[meta[1] ^ slot])

    def prepare(number):
        project_prompt(meta, number, sources, raws, w_ref, kv_ref, state, sem)

    def update(slot, rows, data, number):
        mask = id_ref[slot, rows, :] == data.astype(F32)
        raw = [
            mm_nt(q_ref[slot, rows, pl.ds(h * dim, dim)], kv_ref[number, :, pl.ds(h * dim, dim)])
            for h in range(2)
        ]
        parts = [
            online(prompt_mask(meta, raw[h], block), factor, mask, m_ref, (slot, h, rows))
            for h in range(2)
        ]
        for h in range(2):
            value = kv_ref[number, :, pl.ds((2 + h) * dim, dim)]
            accumulate(acc_ref, (slot, h, rows), parts[h][1], parts[h][0], value)

    visit_prompts(meta, local, table, size, prepare, update)
    row = size
    send_ref[pl.ds(size, PACK), :] = jnp.zeros((PACK, 2 * dim), BF)
    for h in range(2):
        cols = pl.ds(h * dim, dim)
        total = acc_ref[0, h, :, dim:]
        wide_ref[:, cols] = acc_ref[0, h, :, :dim] / total
        lse_ref[h : h + 1, :] = line_of(m_ref[0, h] + jnp.log2(total))
        total = acc_ref[1, h, :, dim:]
        send_ref[pl.ds(0, size), cols] = (acc_ref[1, h, :, :dim] / total).astype(BF)
        line = line_of(m_ref[1, h] + jnp.log2(total))
        row = store_line(send_ref, row, line)


def prompt_scratch(prompt_banks, dim, block):
    slots, part, columns = prompt_banks[0].shape
    pieces = PLEN // block
    count = 2 * slots // pieces
    return [
        pltpu.VMEM((2, count, pieces, part, columns), BF),
        pltpu.VMEM((count, -(-pieces * part // 128) * 128, 4 * dim), BF),
    ], [pltpu.SMEM((count,), jnp.int32), pltpu.SemaphoreType.DMA((2, count, pieces))]


def prompt_forward(
    meta, local, table, q_own, ids_rows, state, flag, prompt_mine, prompt_theirs, weights, factor, block
):
    size, dim = q_own.shape[1], q_own.shape[2] // 2
    buffers, flags = prompt_scratch(prompt_mine, dim, block)
    return pl.pallas_call(
        functools.partial(prompt_forward_kernel, block, factor),
        out_shape=(
            jax.ShapeDtypeStruct((size, 2 * dim), F32),
            jax.ShapeDtypeStruct((2, size), F32),
            jax.ShapeDtypeStruct((size + PACK, 2 * dim), BF),
        ),
        in_specs=[smem()] * 3 + [vmem()] * 7 + [hbm()] * 4,
        out_specs=[vmem()] * 3,
        scratch_shapes=[
            pltpu.VMEM((2, 2, size, 128), F32),
            pltpu.VMEM((2, 2, size, dim + 128), F32),
            *buffers,
            pltpu.VMEM((2, size, 128), F32),
            *flags,
        ],
        compiler_params=params(spare=VMEM_LIMIT),
        cost_estimate=cost(4e9, 8e6, 2e6),
        name="prompt_forward",
    )(meta, local, table, q_own, ids_rows, *state, flag, weights, *prompt_mine, *prompt_theirs)


def join_kernel(wide_in, lse_in, other_ref, o_ref, wide_ref, lse_ref):
    size, dim = wide_in.shape[0], wide_in.shape[1] // 2
    rows_per = size // (2 * dim)
    for h in range(2):
        cols = pl.ds(h * dim, dim)
        first = column_of(lse_in[h : h + 1, :])
        second = column_of(load_line(other_ref, size + h * 3 * rows_per, size))
        top = jnp.maximum(first, second)
        first, second = jnp.exp2(first - top), jnp.exp2(second - top)
        total = first + second
        other = other_ref[pl.ds(0, size), cols].astype(F32)
        attended = (first * wide_in[:, cols] + second * other) / total
        wide_ref[:, cols] = attended
        o_ref[:, cols] = attended.astype(BF)
        lse_ref[h : h + 1, :] = line_of(top + jnp.log2(total))


def join_halves(wide_half, lse_half, other):
    return pl.pallas_call(
        join_kernel,
        out_shape=(
            jax.ShapeDtypeStruct(wide_half.shape, BF),
            jax.ShapeDtypeStruct(wide_half.shape, F32),
            jax.ShapeDtypeStruct(lse_half.shape, F32),
        ),
        in_specs=[vmem()] * 3,
        out_specs=[vmem()] * 3,
        compiler_params=params(),
        cost_estimate=cost(4e6, 3e6, 1e6),
        name="join_halves",
    )(wide_half, lse_half, other)


def norm_parts(value):
    center = value - jnp.mean(value, axis=-1, keepdims=True)
    scale = lax.rsqrt(jnp.mean(center * center, axis=-1, keepdims=True) + 1e-05)
    return center * scale, scale


def norm_back(grad, unit, scale, gain):
    part = grad * gain
    return scale * (
        part
        - jnp.mean(part, axis=-1, keepdims=True)
        - unit * jnp.mean(part * unit, axis=-1, keepdims=True)
    )


def feed_kernel(
    meta,
    mine,
    theirs,
    wide_ref,
    lse_ref,
    tok_ref,
    cot_ref,
    down_bias,
    gains,
    shifts,
    w_own,
    w_along,
    w_core,
    w_far,
    out_ref,
    da_ref,
    pack_ref,
    delta_ref,
    w_ref,
    sem,
):
    size, width = tok_ref.shape
    dim = mine.shape[1] // 2
    heads = w_ref.shape[0]
    hid = (w_ref.shape[1] - PACK - dim) // 2
    batch, parity = meta[1], meta[2]
    even = parity == 0
    cuts = (pl.ds(hid, dim), pl.ds(hid + dim, hid + PACK), pl.ds(0, hid))

    def arrived(part):
        for q in range(heads):
            pltpu.make_async_copy(
                w_own.at[cuts[part]], w_ref.at[q, cuts[part]], sem.at[q, part]
            ).wait()

    for q in range(heads):
        for place, ref in enumerate((w_own, w_along, w_core, w_far)):

            @pl.when((2 * batch + parity) == (q ^ (0, 2, 1, 3)[place]))
            def _():
                for part, rows in enumerate(cuts):
                    pltpu.make_async_copy(
                        ref.at[rows], w_ref.at[q, rows], sem.at[q, part]
                    ).start()

    place_out = slice(hid, hid + dim)
    place_up = slice(hid + dim, 2 * hid + dim)
    place_bias = 2 * hid + dim
    sub = size
    pack_ref[pl.ds(size, STATS), :] = jnp.zeros((STATS, 2 * dim), BF)
    g0, g1 = gains[0:1, :], gains[1:2, :]
    for part in range(size // sub):
        rows = pl.ds(part * sub, sub)
        a, b = mine[rows, :], theirs[rows, :]
        if part == 0:
            arrived(0)
        first = jnp.where(even, a, b)
        second = jnp.where(even, b, a)
        attn = mm(first[:, :dim], w_ref[0, place_out, :])
        attn += mm(second[:, :dim], w_ref[1, place_out, :])
        attn += mm(first[:, dim:], w_ref[2, place_out, :])
        attn += mm(second[:, dim:], w_ref[3, place_out, :])
        unit_one, scale_one = norm_parts(tok_ref[rows, :].astype(F32) + attn)
        normed = unit_one * g0 + shifts[0:1, :]
        normed_low = normed.astype(BF)
        branch = down_bias[...]
        slopes = []
        if part == 0:
            arrived(1)
            arrived(2)
        for q in range(heads):
            bias = (
                w_ref[q, place_bias : place_bias + 1, :hid].astype(F32)
                + w_ref[q, place_bias : place_bias + 1, hid : 2 * hid].astype(F32)
                + w_ref[q, place_bias + 1 : place_bias + 2, :hid].astype(F32)
            )
            pre = mm_nt(normed_low, w_ref[q, place_up, :]) + bias
            cdf = 0.5 * (1.0 + lax.erf(pre * 0.7071067811865476))
            slopes.append(cdf + pre * (jnp.exp(-0.5 * pre * pre) * 0.3989422804014327))
            branch = branch + mm((pre * cdf).astype(BF), w_ref[q, :hid, :])
        unit_two, scale_two = norm_parts(normed + branch)
        out_ref[rows, :] = (unit_two * g1 + shifts[1:2, :]).astype(BF)
        grad_mixed = norm_back(cot_ref[rows, :].astype(F32), unit_two, scale_two, g1)
        mixed_low = grad_mixed.astype(BF)
        grad_normed = grad_mixed
        for q in range(heads):
            grad_pre = mm_nt(mixed_low, w_ref[q, :hid, :]) * slopes[q]
            grad_normed = grad_normed + mm(grad_pre.astype(BF), w_ref[q, place_up, :])
        grad_sum = norm_back(grad_normed, unit_one, scale_one, g0)
        da_ref[rows, :] = grad_sum
        sum_low = grad_sum.astype(BF)
        for head in range(2):
            cols = pl.ds(head * dim, dim)
            grad_out = mm_nt(sum_low, w_ref[2 * head + parity, place_out, :]).astype(BF)
            pack_ref[rows, cols] = grad_out
            delta = jnp.sum(grad_out.astype(F32) * wide_ref[rows, cols], axis=1, keepdims=True)
            delta_ref[head : head + 1, rows] = line_of(jnp.broadcast_to(delta, (sub, 128)))
    row = size
    for head in range(2):
        for ref in (lse_ref, delta_ref):
            row = store_line(pack_ref, row, ref[head : head + 1, :])


def feed(meta, mine, theirs, wide_out, lse, tokens, cotangent, w, down_bias, gains, shifts):
    size, width = tokens.shape
    dim = mine.shape[1] // 2
    return pl.pallas_call(
        feed_kernel,
        out_shape=(
            jax.ShapeDtypeStruct((size, width), BF),
            jax.ShapeDtypeStruct((size, width), F32),
            jax.ShapeDtypeStruct((size + STATS, 2 * dim), BF),
            jax.ShapeDtypeStruct((2, size), F32),
        ),
        in_specs=[smem()] + [vmem()] * 9 + [hbm()] * 4,
        out_specs=[vmem()] * 4,
        scratch_shapes=[pltpu.VMEM((4,) + w[0].shape, BF), pltpu.SemaphoreType.DMA((4, 3))],
        compiler_params=params(),
        cost_estimate=cost(3e9, 8e6, 1e6),
        name="feed",
    )(meta, mine, theirs, wide_out, lse, tokens, cotangent, down_bias, gains, shifts, *w)


def low_grads(scores, factor, shift, grads, delta):
    count = scores.shape[1] // 128
    probs = jnp.exp2(scores * factor - wide(shift, count))
    return (probs * (grads - wide(delta, count))).astype(BF)


def token_query_grad_kernel(
    data_count,
    factor,
    meta,
    starts,
    q_ref,
    ids_ref,
    lse_ref,
    delta_ref,
    do_ref,
    acc_in,
    w_ref,
    mine_low,
    mine_high,
    theirs_low,
    theirs_high,
    dq_ref,
    flag,
    acc_ref,
    x_ref,
    id_ref,
    lse_cols,
    delta_cols,
    sem,
):
    raise_flag(flag)
    size, dim = q_ref.shape[1], q_ref.shape[2] // 2
    base = meta[0] * size
    first, last = key_range(starts, base, base + size, data_count)
    first, last = first // size, (last + size - 1) // size
    gathered = (mine_low, mine_high, theirs_low, theirs_high)
    fetch_shards(meta, first, last, gathered, x_ref, sem)
    for h in range(2):
        lse_cols[h] = column_of(lse_ref[h : h + 1, :])
        delta_cols[h] = column_of(delta_ref[h : h + 1, :])
    acc_ref[...] = acc_in[...]
    id_ref[...] = column_of(ids_ref[meta[1]])

    def step(shard, carry):
        raw_rows, line = load_shard(meta, shard, gathered, x_ref, sem)
        kv = mm(raw_rows, w_ref[...]).astype(BF)
        mask = wide(id_ref[...], size // 128) == line
        raw, grads, low = [], [], []
        for h in range(2):
            raw.append(mm_nt(q_ref[0, :, h * dim : (h + 1) * dim], kv[:, h * dim : (h + 1) * dim]))
            grads.append(
                mm_nt(
                    do_ref[pl.ds(0, size), h * dim : (h + 1) * dim],
                    kv[:, (2 + h) * dim : (3 + h) * dim],
                )
            )
        for h in range(2):
            scores = jnp.where(mask, raw[h], NEGATIVE)
            low.append(low_grads(scores, factor, lse_cols[h], grads[h], delta_cols[h]))
        for h in range(2):
            acc_ref[h] += mm(low[h], kv[:, h * dim : (h + 1) * dim])
        return carry

    lax.fori_loop(first, last, step, 0)
    for h in range(2):
        dq_ref[:, pl.ds(h * dim, dim)] = acc_ref[h] * dim ** (-0.5)


def token_query_grad(
    meta, starts, q_own, ids_rows, lse, delta, pack, acc, mine, theirs, weights, factor, data_count
):
    size, dim = q_own.shape[1], q_own.shape[2] // 2
    return pl.pallas_call(
        functools.partial(token_query_grad_kernel, data_count, factor),
        out_shape=(jax.ShapeDtypeStruct((size, 2 * dim), F32), flag_shape()),
        in_specs=[smem()] * 2 + [vmem()] * 7 + [hbm()] * 4,
        out_specs=[vmem()] * 2,
        scratch_shapes=[
            pltpu.VMEM((2, size, dim), F32),
            shard_scratch(mine),
            pltpu.VMEM((size, 128), F32),
            pltpu.VMEM((2, size, 128), F32),
            pltpu.VMEM((2, size, 128), F32),
            pltpu.SemaphoreType.DMA((2 * mine[0].shape[0], 2)),
        ],
        compiler_params=params(*mine, *theirs),
        cost_estimate=cost(6e9, 16e6, 4e6),
        name="token_query_grad",
    )(
        meta,
        starts,
        q_own,
        ids_rows,
        lse,
        delta,
        pack,
        acc,
        weights,
        *mine,
        *theirs,
    )


def prompt_query_grad_kernel(
    block,
    factor,
    meta,
    local,
    table,
    q_ref,
    ids_ref,
    lse_in,
    delta_in,
    pack_own,
    pack_other,
    _,
    w_ref,
    mine_low,
    mine_high,
    theirs_low,
    theirs_high,
    dq_ref,
    send_ref,
    acc_ref,
    lse_ref,
    delta_ref,
    do_ref,
    raws,
    kv_ref,
    id_ref,
    state,
    sem,
):
    size, dim = q_ref.shape[1], q_ref.shape[2] // 2
    rows_per = size // (2 * dim)
    sources = (mine_low, mine_high, theirs_low, theirs_high)
    fetch_prompts(meta, local, table, sources, raws, state, sem)
    acc_ref[...] = jnp.zeros(acc_ref.shape, F32)
    for h in range(2):
        lse_ref[0, h] = column_of(lse_in[h : h + 1, :])
        delta_ref[0, h] = column_of(delta_in[h : h + 1, :])
    do_ref[0] = pack_own[pl.ds(0, size), :]
    do_ref[1] = pack_other[pl.ds(0, size), :]
    for h in range(2):
        for kind, ref in enumerate((lse_ref, delta_ref)):
            row = size + (h * 2 + kind) * 3 * rows_per
            ref[1, h] = column_of(load_line(pack_other, row, size))
    for slot in range(2):
        id_ref[slot] = column_of(ids_ref[meta[1] ^ slot])

    def prepare(number):
        project_prompt(meta, number, sources, raws, w_ref, kv_ref, state, sem)

    def update(slot, rows, data, number):
        mask = id_ref[slot, rows, :] == data.astype(F32)
        raw, grads, low = [], [], []
        for h in range(2):
            cols = pl.ds(h * dim, dim)
            raw.append(mm_nt(q_ref[slot, rows, cols], kv_ref[number, :, cols]))
            value = kv_ref[number, :, pl.ds((2 + h) * dim, dim)]
            grads.append(mm_nt(do_ref[slot, rows, cols], value))
        for h in range(2):
            shift = jnp.where(mask, lse_ref[slot, h, rows, :], -NEGATIVE)
            scores = prompt_mask(meta, raw[h], block)
            low.append(low_grads(scores, factor, shift, grads[h], delta_ref[slot, h, rows, :]))
        for h in range(2):
            acc_ref[slot, h, rows, :] += mm(low[h], kv_ref[number, :, pl.ds(h * dim, dim)])

    visit_prompts(meta, local, table, size, prepare, update)
    for h in range(2):
        cols = pl.ds(h * dim, dim)
        dq_ref[h] = acc_ref[0, h]
        send_ref[:, cols] = (acc_ref[1, h] * dim ** (-0.5)).astype(BF)


def prompt_query_grad(
    meta,
    local,
    table,
    q_own,
    ids_rows,
    lse,
    delta,
    pack,
    pack_other,
    flag,
    prompt_mine,
    prompt_theirs,
    weights,
    factor,
    block,
):
    size, dim = q_own.shape[1], q_own.shape[2] // 2
    buffers, flags = prompt_scratch(prompt_mine, dim, block)
    return pl.pallas_call(
        functools.partial(prompt_query_grad_kernel, block, factor),
        out_shape=(
            jax.ShapeDtypeStruct((2, size, dim), F32),
            jax.ShapeDtypeStruct((size, 2 * dim), BF),
        ),
        in_specs=[smem()] * 3 + [vmem()] * 8 + [hbm()] * 4,
        out_specs=[vmem()] * 2,
        scratch_shapes=[
            pltpu.VMEM((2, 2, size, dim), F32),
            pltpu.VMEM((2, 2, size, 128), F32),
            pltpu.VMEM((2, 2, size, 128), F32),
            pltpu.VMEM((2, size, 2 * dim), BF),
            *buffers,
            pltpu.VMEM((2, size, 128), F32),
            *flags,
        ],
        compiler_params=params(*prompt_mine, *prompt_mine, *prompt_mine, *prompt_mine),
        cost_estimate=cost(6e9, 16e6, 4e6),
        name="prompt_query_grad",
    )(
        meta,
        local,
        table,
        q_own,
        ids_rows,
        lse,
        delta,
        pack,
        pack_other,
        flag,
        weights,
        *prompt_mine,
        *prompt_theirs,
    )


def in_bank(meta, index, bank, slots):
    slot = slot_of((index // 2) ^ meta[0], meta[2], bit_orders(2 * slots))
    return (slot < slots) if bank == 0 else (slot >= slots)


def half_shard(meta, index, q_ref, ids_ref, low_ref, high_ref):
    slots, rows, double = (high_ref if low_ref is None else low_ref).shape
    half = q_ref.shape[1]
    size = rows - STATS
    shard, part = index // 2, index % 2
    slot = slot_of(shard ^ meta[0], meta[2], bit_orders(2 * slots))
    other = slot_of(shard ^ meta[0], 1 - meta[2], bit_orders(2 * slots))
    query = q_ref[jnp.where(part == meta[2], slot * 2, other * 2 + 1)]
    in_low = slot < slots
    place_low, place_high = jnp.minimum(slot, slots - 1), jnp.maximum(slot - slots, 0)
    span = pl.ds(pl.multiple_of(part * half, half), half)
    tail = pl.ds(size, STATS)

    def take(rows):
        if high_ref is None:
            return low_ref[place_low, rows, :]
        if low_ref is None:
            return high_ref[place_high, rows, :]
        return jnp.where(in_low, low_ref[place_low, rows, :], high_ref[place_high, rows, :])

    grad = take(span)
    line = ids_ref[slot]
    line = jnp.where(part == 0, line[:, :half], line[:, half : 2 * half])
    stats = take(tail).astype(F32)
    rows_per = size // double

    def stat(head, kind):
        total = 0.0
        for place in range(3):
            row = ((head * 2 + kind) * 3 + place) * rows_per
            term = stats[row : row + 1, :]
            for i in range(1, rows_per):
                term = jnp.where(part == i, stats[row + i : row + i + 1, :], term)
            total = total + term
        return total

    return query, grad, line, stat


def key_update(query, grad, kv_ref, mask, rows_mask, stat, factor, dk_ref, dv_ref):
    dim = query.shape[1] // 2
    cols = [slice(h * dim, (h + 1) * dim) for h in range(2)]
    raw = [mm_nt(kv_ref[:, cols[h]], query[:, cols[h]]) for h in range(2)]
    grads = [mm_nt(kv_ref[:, pl.ds((2 + h) * dim, dim)], grad[:, cols[h]]) for h in range(2)]
    probs, low = [], []
    for h in range(2):
        shift = stat(h, 0)
        scores = raw[h]
        if rows_mask is None:
            shift = jnp.where(mask, shift, -NEGATIVE)
        else:
            scores = jnp.where(rows_mask, scores, NEGATIVE)
        p = jnp.exp2(scores * factor - shift)
        probs.append(p.astype(BF))
        low.append((p * (grads[h] - stat(h, 1))).astype(BF))
    for h in range(2):
        dv_ref[:, cols[h]] += mm(probs[h], grad[:, cols[h]])
        dk_ref[:, cols[h]] += mm(low[h], query[:, cols[h]])


def prompt_terms(data_count, factor, bank, meta, starts, table, q_ref, ids_ref, pack_ref, kv_ref, dk_ref, dv_ref):
    half = q_ref.shape[1]
    number = meta[0] * kv_ref.shape[0] // PLEN
    low_ref, high_ref = (pack_ref, None) if bank == 0 else (None, pack_ref)

    def visit(data, carry):
        begin, end = starts[data], starts[data + 1]

        @pl.when((table[meta[1], data] == number) & (begin < end))
        def _():
            def step(index, inner):
                @pl.when(in_bank(meta, index, bank, pack_ref.shape[0]))
                def _():
                    query, grad, line, stat = half_shard(
                        meta, index, q_ref, ids_ref, low_ref, high_ref
                    )
                    mask = line == data.astype(F32)
                    key_update(query, grad, kv_ref, mask, None, stat, factor, dk_ref, dv_ref)

                return inner

            lax.fori_loop(begin // half, (end + half - 1) // half, step, 0)

        return carry

    lax.fori_loop(0, data_count, visit, 0)


def prompt_grad_first_kernel(
    data_count,
    factor,
    meta,
    starts,
    table,
    q_ref,
    ids_ref,
    pack_ref,
    kv_ref,
    _,
    dk_ref,
    dv_ref,
    flag,
):
    raise_flag(flag)
    dk_ref[...] = jnp.zeros(dk_ref.shape, F32)
    dv_ref[...] = jnp.zeros(dv_ref.shape, F32)
    prompt_terms(
        data_count, factor, 0, meta, starts, table, q_ref, ids_ref, pack_ref, kv_ref, dk_ref, dv_ref
    )


def prompt_grad_last_kernel(
    data_count,
    factor,
    meta,
    starts,
    table,
    q_ref,
    ids_ref,
    pack_ref,
    kv_ref,
    dk_in,
    dv_in,
    w_ref,
    keep_ref,
    send_ref,
    dk_ref,
    dv_ref,
):
    width = w_ref.shape[0]
    dim = kv_ref.shape[1] // 4
    dk_ref[...] = dk_in[...]
    dv_ref[...] = dv_in[...]
    prompt_terms(
        data_count, factor, 1, meta, starts, table, q_ref, ids_ref, pack_ref, kv_ref, dk_ref, dv_ref
    )
    grads = jnp.concatenate(
        [(dk_ref[...] * dim ** (-0.5)).astype(BF), dv_ref[...].astype(BF)], axis=1
    )
    split = width // 2
    parity = meta[2]
    send = w_ref[pl.ds(pl.multiple_of((1 - parity) * split, split), split), :]
    keep = w_ref[pl.ds(pl.multiple_of(parity * split, split), split), :]
    send_ref[...] = mm_nt(grads, send).astype(BF)
    keep_ref[...] = mm_nt(grads, keep)


def prompt_grad_first(meta, starts, table, q_all, ids_all, pack, kv, flag, factor, data_count):
    block, dim = kv.shape[0], kv.shape[1] // 4
    shape = jax.ShapeDtypeStruct((block, 2 * dim), F32)
    return pl.pallas_call(
        functools.partial(prompt_grad_first_kernel, data_count, factor),
        out_shape=(shape, shape, flag_shape()),
        in_specs=[smem()] * 3 + [vmem()] * 5,
        out_specs=[vmem()] * 3,
        compiler_params=params(q_all, pack),
        cost_estimate=cost(6e9, 16e6, 4e6),
        name="prompt_grad_first",
    )(meta, starts, table, q_all, ids_all, pack, kv, flag)


def prompt_grad_last(meta, starts, table, q_all, ids_all, pack, kv, terms, weights, factor, data_count):
    block, width = kv.shape[0], weights.shape[0]
    dim = kv.shape[1] // 4
    return pl.pallas_call(
        functools.partial(prompt_grad_last_kernel, data_count, factor),
        out_shape=(
            jax.ShapeDtypeStruct((block, width // 2), F32),
            jax.ShapeDtypeStruct((block, width // 2), BF),
        ),
        in_specs=[smem()] * 3 + [vmem()] * 7,
        out_specs=[vmem(), vmem()],
        scratch_shapes=[
            pltpu.VMEM((block, 2 * dim), F32),
            pltpu.VMEM((block, 2 * dim), F32),
        ],
        compiler_params=params(q_all, pack),
        cost_estimate=cost(6e9, 16e6, 4e6),
        name="prompt_grad_last",
    )(meta, starts, table, q_all, ids_all, pack, kv, *terms, weights)


def token_grad_kernel(
    data_count,
    factor,
    meta,
    starts,
    q_ref,
    ids_ref,
    low_ref,
    high_ref,
    kv_ref,
    own_ids,
    dq_ref,
    dq_other,
    wq_ref,
    wkv_ref,
    out_ref,
    flag,
    dk_ref,
    dv_ref,
    id_ref,
):
    raise_flag(flag)
    size = kv_ref.shape[0]
    half = q_ref.shape[1]
    dim = kv_ref.shape[1] // 4
    base = meta[0] * size
    first, last = key_range(starts, base, base + size, data_count)
    dk_ref[...] = jnp.zeros(dk_ref.shape, F32)
    dv_ref[...] = jnp.zeros(dv_ref.shape, F32)
    id_ref[...] = column_of(own_ids[meta[1]])

    def step(index, carry):
        query, grad, line, stat = half_shard(meta, index, q_ref, ids_ref, low_ref, high_ref)
        mask = wide(id_ref[...], half // 128) == line
        key_update(query, grad, kv_ref, None, mask, stat, factor, dk_ref, dv_ref)
        return carry

    lax.fori_loop(first // half, (last + half - 1) // half, step, 0)
    dq = (dq_ref[...] + dq_other[...].astype(F32)).astype(BF)
    grads = jnp.concatenate(
        [(dk_ref[...] * dim ** (-0.5)).astype(BF), dv_ref[...].astype(BF)], axis=1
    )
    out_ref[...] = (mm_nt(dq, wq_ref[...]) + mm_nt(grads, wkv_ref[...])).astype(BF)


def token_grad(
    meta, starts, q_all, ids_all, packs, kv_own, ids_rows, dq, weights, factor, data_count
):
    size, dim = kv_own.shape[0], kv_own.shape[1] // 4
    width = weights[0].shape[0]
    return pl.pallas_call(
        functools.partial(token_grad_kernel, data_count, factor),
        out_shape=(jax.ShapeDtypeStruct((size, width), BF), flag_shape()),
        in_specs=[smem()] * 2 + [vmem()] * 10,
        out_specs=[vmem()] * 2,
        scratch_shapes=[
            pltpu.VMEM((size, 2 * dim), F32),
            pltpu.VMEM((size, 2 * dim), F32),
            pltpu.VMEM((size, 128), F32),
        ],
        compiler_params=params(spare=VMEM_LIMIT),
        cost_estimate=cost(4e9, 16e6, 4e6),
        name="token_grad",
    )(meta, starts, q_all, ids_all, *packs, kv_own, ids_rows, *dq, *weights)


def sum_prompt_kernel(a_ref, b_ref, _, sum_ref, square_ref):
    low = (a_ref[...].astype(F32) + b_ref[...].astype(F32)).astype(BF)
    sum_ref[...] = low
    value = low.astype(F32)
    square_ref[...] = jnp.broadcast_to(jnp.sum(value * value, keepdims=True), square_ref.shape)


def sum_prompt(a, b, flag):
    return pl.pallas_call(
        sum_prompt_kernel,
        out_shape=(
            jax.ShapeDtypeStruct(a.shape, BF),
            jax.ShapeDtypeStruct((8, 128), F32),
        ),
        in_specs=[vmem()] * 3,
        out_specs=[vmem(), vmem()],
        compiler_params=params(),
        cost_estimate=cost(4 * a.size, 6 * a.size),
        name="sum_prompt",
    )(a, b, flag)


def optimizer_kernel(
    meta,
    biases,
    mine,
    theirs,
    squares,
    prompts,
    one_in,
    two_in,
    clip_out,
    one_out,
    two_out,
    new_out,
    norm_ref,
    held,
    sem,
):
    even = meta[2] == 0
    block = prompts.shape[0]
    tiles = sem.shape[1]
    tile = block // tiles
    norm_ref[...] = jnp.sqrt(squares[...])
    norm = norm_ref[0:1, :]
    factor = jnp.minimum(1.0, CLIP_NORM / (norm + 1e-06))
    copies = []
    for index in range(tiles):
        rows = pl.ds(index * tile, tile)
        a, b = mine[rows, :].astype(F32), theirs[rows, :].astype(F32)
        grads = jnp.concatenate([jnp.where(even, a, b), jnp.where(even, b, a)], axis=1)
        clipped = grads * wide(factor, grads.shape[1] // 128)
        new_one = BETA_ONE * one_in[rows, :] + (1.0 - BETA_ONE) * clipped
        new_two = BETA_TWO * two_in[rows, :] + (1.0 - BETA_TWO) * clipped * clipped
        first_hat = new_one / biases[0]
        second_hat = new_two / biases[1]
        held[0, rows, :] = clipped
        held[1, rows, :] = new_one
        held[2, rows, :] = new_two
        held[3, rows, :] = prompts[rows, :] * (
            1.0 - LEARNING_RATE * DECAY_RATE
        ) - LEARNING_RATE * first_hat / (jnp.sqrt(second_hat) + EPSILON)
        for place, out in enumerate((clip_out, one_out, two_out, new_out)):
            copies.append(
                pltpu.make_async_copy(held.at[place, rows], out.at[rows], sem.at[place, index])
            )
            copies[-1].start()
    for copy in copies:
        copy.wait()


def optimizer(meta, biases, mine, theirs, squares, prompts, moment_one, moment_two):
    block, width = prompts.shape
    tiles = 5 if block % 40 == 0 else 1
    shape = jax.ShapeDtypeStruct((block, width), F32)
    return pl.pallas_call(
        optimizer_kernel,
        out_shape=(shape,) * 4 + (jax.ShapeDtypeStruct(squares.shape, F32),),
        in_specs=[smem(), smem()] + [vmem()] * 6,
        out_specs=[hbm()] * 4 + [vmem()],
        scratch_shapes=[
            pltpu.VMEM((4, block, width), F32),
            pltpu.SemaphoreType.DMA((4, tiles)),
        ],
        compiler_params=params(prompts, prompts),
        cost_estimate=cost(20 * block * width, 32 * block * width),
        name="optimizer",
    )(meta, biases, mine, theirs, squares, prompts, moment_one, moment_two)


def per_device(
    tokens,
    cotangent,
    dataset_ids,
    prompt_map,
    attn_in,
    attn_out,
    up_weight,
    up_bias,
    down_weight,
    down_bias,
    norm_gains,
    norm_shifts,
    prompts,
    moment_one,
    moment_two,
    step_count,
):
    size, width = tokens.shape[1:]
    dim = attn_in.shape[2]
    hid = up_weight.shape[1]
    data_count = prompt_map.shape[1]
    row_count = lax.axis_size("rows")
    head_count = lax.axis_size("head")
    factor = dim ** (-0.5) * LOG2E
    row = lax.axis_index("rows")
    head = lax.axis_index("head")
    batch, parity = head // 2, head % 2
    half = size // 2
    meta = jnp.stack([row, batch, parity]).astype(jnp.int32)

    block = prompts.shape[0]

    part = half_rows(block)
    prompt_own = lax.dynamic_slice(
        prompts, (batch * (block - part), parity * (width // 2)), (part, width // 2)
    ).astype(BF)
    in_other = swap_head(attn_in, 2, head_count)
    ids = jnp.where(batch == 0, dataset_ids[0], dataset_ids[1])
    tok_half = lax.dynamic_slice(tokens, (batch, parity * half, 0), (1, half, width))[0]
    id_rows = jnp.broadcast_to(ids.astype(BF)[None, :], (PACK, size))
    shard = jnp.concatenate([tok_half, id_rows], axis=0)

    bias_high = lax.reduce_precision(up_bias, 8, 7)
    bias_rest = up_bias - bias_high
    bias_mid = lax.reduce_precision(bias_rest, 8, 7)
    bias_low = bias_rest - bias_mid
    bias_rows = jnp.concatenate([bias_high, bias_mid, bias_low, bias_low]).astype(BF)
    bias_rows = jnp.pad(bias_rows.reshape(-1, width), ((0, PACK - 4 * hid // width), (0, 0)))
    w_own = jnp.concatenate([down_weight, attn_out, up_weight.T, bias_rows], axis=0)
    in_other, w_own = lax.optimization_barrier((in_other, w_own))
    w_along = swap_head(w_own, 2, head_count)
    step_value = step_count.astype(F32)
    biases = jnp.stack(
        [1.0 - jnp.power(BETA_ONE, step_value), 1.0 - jnp.power(BETA_TWO, step_value)]
    )
    numbers = jnp.arange(data_count + 1, dtype=jnp.int32)
    local = jnp.sum((dataset_ids[:, None, :] < numbers[None, :, None]).astype(jnp.int32), axis=2)
    ids_rows = dataset_ids.astype(F32).reshape(2, 1, size)
    tied = {}

    orders, later = bit_orders(row_count), prompt_orders(row_count)
    stages = len(orders[0])
    held, prompt_held = shard[None], prompt_own[None]
    tok = lax.dynamic_index_in_dim(tokens, batch, 0, keepdims=False)
    cot = lax.dynamic_index_in_dim(cotangent, batch, 0, keepdims=False)

    def prompt_stage(place):
        other = gather_stage(prompt_held, place, later, row_count, head_count)
        return jnp.concatenate([prompt_held, other], axis=0)

    for place in range(stages):
        if place == stages - 1:
            held, in_other, meta, (biases, local, ids_rows, tok, cot) = lax.optimization_barrier(
                (held, in_other, meta, (biases, local, ids_rows, tok, cot))
            )
        if place != 1:
            held, prompt_held = lax.optimization_barrier((held, prompt_held))
        other = gather_stage(held, place, orders, row_count, head_count)
        if place != 1:
            prompt_held = prompt_stage(max(place - 1, 0))
        if place < stages - 1:
            held = jnp.concatenate([held, other], axis=0)
        if place == 0:
            held, prompt_held = lax.optimization_barrier((held, prompt_held))
    theirs_low = swap_head(held, 1, head_count)
    other, prompt_held, w_along = lax.optimization_barrier((other, prompt_held, w_along))
    mine = (held, other)
    prompt_high = gather_stage(prompt_held, stages - 1, later, row_count, head_count)
    theirs = (theirs_low, swap_head(other, 1, head_count))
    w_core = swap_head(w_own, 1, head_count)
    w_far = swap_head(w_along, 1, head_count)

    ids_all = jnp.concatenate([bank[:, half, :size] for bank in mine], axis=0).astype(F32)
    starts = jnp.sum(
        (ids_all.reshape(1, -1) < numbers.astype(F32)[:, None]).astype(jnp.int32), axis=1
    )
    ids_all = ids_all.reshape(row_count, 1, size)
    q_own, kv_own, w_q, w_kv, *state, flag = token_forward(
        meta, starts, tokens, ids_rows, mine, theirs, attn_in, in_other, factor, data_count
    )
    prompt_theirs_low = swap_head(prompt_held, 1, head_count)
    prompt_high, flag, prompt_theirs_low, w_core, w_far = lax.optimization_barrier(
        (prompt_high, flag, prompt_theirs_low, w_core, w_far)
    )
    prompt_mine = (prompt_held, prompt_high)
    prompt_theirs = (prompt_theirs_low, swap_head(prompt_high, 1, head_count))
    wide_half, lse_half, send_half = prompt_forward(
        meta,
        local,
        prompt_map,
        q_own,
        ids_rows,
        state,
        flag,
        prompt_mine,
        prompt_theirs,
        w_kv,
        factor,
        block,
    )
    prompt_low, send_half = lax.optimization_barrier((prompts.astype(BF), send_half))
    prompt_kv = jnp.dot(prompt_low, w_kv, preferred_element_type=F32).astype(BF)
    o_mine, wide_out, lse = join_halves(wide_half, lse_half, swap_head(send_half, 2, head_count))
    o_mine, prompt_kv = lax.optimization_barrier((o_mine, prompt_kv))
    o_theirs = swap_head(o_mine, 1, head_count)
    out, grad_sum, pack, delta = feed(
        meta,
        o_mine,
        o_theirs,
        wide_out,
        lse,
        tok,
        cot,
        (w_own, w_along, w_core, w_far),
        down_bias.reshape(1, width),
        norm_gains,
        norm_shifts,
    )
    pack_other = swap_head(pack, 2, head_count)

    def tie_query_grads(stages_left, held):
        if stages_left == 3:
            held, here = lax.optimization_barrier((held, w_q))
            tied["q"], tied["flag"] = project_query(mine, theirs, here)
        if stages_left == 2:
            held, other, flag = lax.optimization_barrier((held, pack_other, tied["flag"]))
            tied["dq"] = prompt_query_grad(
                meta,
                local,
                prompt_map,
                q_own,
                ids_rows,
                lse,
                delta,
                pack,
                other,
                flag,
                prompt_mine,
                prompt_theirs,
                w_kv,
                factor,
                block,
            )
        if stages_left == 1:
            acc, dq_send = tied["dq"]
            held, dq_send, ids_here = lax.optimization_barrier((held, dq_send, ids_rows))
            tied["dq_other"] = swap_head(dq_send, 2, head_count)
            tied["dq"], tied["flag"] = token_query_grad(
                meta,
                starts,
                q_own,
                ids_here,
                lse,
                delta,
                pack,
                acc,
                mine,
                theirs,
                w_kv,
                factor,
                data_count,
            )
            *tied["terms"], tied["flag"] = prompt_grad_first(
                meta,
                starts,
                prompt_map,
                tied["q"],
                ids_all,
                held,
                prompt_kv,
                tied["flag"],
                factor,
                data_count,
            )
        return held

    out_half = lax.dynamic_slice_in_dim(out, parity * half, half, 0)
    out_half = swap_head(out_half, 2, head_count)
    packs = gather_rows(pack, row_count, head_count, tie_query_grads)
    q_all = tied["q"]
    dq = tied["dq"]
    packs, dq_other, out_half = lax.optimization_barrier((packs, tied["dq_other"], out_half))
    keep, send = prompt_grad_last(
        meta,
        starts,
        prompt_map,
        q_all,
        ids_all,
        packs[1],
        prompt_kv,
        tied["terms"],
        w_kv,
        factor,
        data_count,
    )

    pair = keep + swap_head(send, 1, head_count).astype(F32)
    pair_low = lax.reduce_precision(pair, 8, 7).astype(BF)
    pair_low, ids_here = lax.optimization_barrier((pair_low, ids_rows))
    pair_other = swap_head(pair_low, 2, head_count)
    out_rest = swap_head(out_half, 1, head_count)
    token_part, flag = token_grad(
        meta,
        starts,
        q_all,
        ids_all,
        packs,
        kv_own,
        ids_here,
        (dq, dq_other),
        (w_q, w_kv),
        factor,
        data_count,
    )
    pair_other, flag = lax.optimization_barrier((pair_other, flag))
    full_low, squares = sum_prompt(pair_low, pair_other, flag)
    full_other = swap_head(full_low, 1, head_count)

    def both_batches(own, here, rest):
        other = jnp.concatenate(
            [jnp.where(parity == 0, here, rest), jnp.where(parity == 0, rest, here)], axis=0
        )
        first = jnp.where(batch == 0, own, other)
        return jnp.stack([first, jnp.where(batch == 0, other, own)]).astype(F32)

    core_sum = token_part.astype(F32) + swap_head(token_part, 1, head_count).astype(F32)
    total = lax.reduce_precision(grad_sum + core_sum, 8, 7).astype(BF)
    mine_half = lax.dynamic_slice_in_dim(total, parity * half, half, 0)
    other_half = swap_head(mine_half, 2, head_count)
    layer_out = both_batches(out, out_half, out_rest)

    def tie_sum(stages_done, value):
        if stages_done == 1:
            value, _ = lax.optimization_barrier((value, total))
        if stages_done == 2:
            value, tied["out"] = lax.optimization_barrier((value, layer_out))
        return value

    squares = xor_sum(squares, row_count, head_count, tie_sum)
    clipped, new_one, new_two, new_prompts, norm = optimizer(
        meta, biases, full_low, full_other, squares, prompts, moment_one, moment_two
    )
    other_half, norm = lax.optimization_barrier((other_half, norm))
    input_grad = both_batches(total, other_half, swap_head(other_half, 1, head_count))
    return (tied["out"], input_grad, clipped, norm[0, 0], new_one, new_two, new_prompts)


def solution(mesh):
    in_specs = (
        P(None, "rows", None),
        P(None, "rows", None),
        P(None, "rows"),
        P(),
        P(None, None, "head"),
        P("head", None),
        P(None, "head"),
        P("head"),
        P("head", None),
        P(),
        P(),
        P(),
        P("rows", None),
        P("rows", None),
        P("rows", None),
        P(),
    )
    out_specs = (
        P(None, "rows", None),
        P(None, "rows", None),
        P("rows", None),
        P(),
        P("rows", None),
        P("rows", None),
        P("rows", None),
    )
    return jax.shard_map(
        per_device, mesh=mesh, in_specs=in_specs, out_specs=out_specs, check_vma=False
    )
```

```python
import functools

import jax
import jax.numpy as jnp
from jax import lax
from jax.experimental import pallas as pl
from jax.experimental.pallas import tpu as pltpu
from jax.sharding import PartitionSpec as P

PLEN = 1000
NEGATIVE = -1e30
BETA_ONE = 0.9
BETA_TWO = 0.999
LEARNING_RATE = 0.5
DECAY_RATE = 0.01
EPSILON = 1e-08
CLIP_NORM = 1.0
LOG2E = 1.4426950408889634
PACK = 16
STATS = 32
VMEM_LIMIT = 60 * 1024 * 1024
BF = jnp.bfloat16
F32 = jnp.float32
BOTH = ("rows", "head")


def params(*operands, spare=20 << 20):
    held = sum(x.size * x.dtype.itemsize for x in operands)
    return pltpu.CompilerParams(vmem_limit_bytes=min(VMEM_LIMIT, held + spare))


def cost(flops, bytes_accessed, transcendentals=0):
    return pl.CostEstimate(
        flops=int(flops), bytes_accessed=int(bytes_accessed), transcendentals=int(transcendentals)
    )


def mm(a, b):
    return lax.dot_general(a, b, (((1,), (0,)), ((), ())), preferred_element_type=F32)


def mm_nt(a, b):
    return lax.dot_general(a, b, (((1,), (1,)), ((), ())), preferred_element_type=F32)


def split3(value):
    high = value.astype(BF)
    rest = value - high.astype(F32)
    mid = rest.astype(BF)
    low = (rest - mid.astype(F32)).astype(BF)
    return high, mid, low


def bit_orders(row_count):
    bits = row_count.bit_length() - 1
    return ([0] + list(range(bits - 1, 0, -1)), list(range(bits - 1, 0, -1)) + [0])


def prompt_orders(row_count):
    bits = row_count.bit_length() - 1
    if bits < 2:
        return bit_orders(row_count)
    high = list(range(bits - 1, 1, -1))
    return (high + [0, 1], [1] + high + [0])


def slot_of(offset, parity, orders):
    def mapped(order):
        total = 0
        for place, bit in enumerate(order):
            total = total + (((offset >> bit) & 1) << place)
        return total

    return jnp.where(parity == 0, mapped(orders[0]), mapped(orders[1]))


def gather_stage(held, place, orders, row_count, head_count):
    pairs = []
    for row in range(row_count):
        for head in range(head_count):
            bit = orders[head % 2][place]
            pairs.append((row * head_count + head, (row ^ (1 << bit)) * head_count + head))
    return lax.ppermute(held, BOTH, pairs)


def gather_rows(block, row_count, head_count, before_send):
    held = block[None]
    orders = bit_orders(row_count)
    stages = len(orders[0])
    for place in range(stages):
        held = before_send(stages - place, held)
        other = gather_stage(held, place, orders, row_count, head_count)
        if place < stages - 1:
            held = jnp.concatenate([held, other], axis=0)
    return held, other


def xor_sum(value, row_count, head_count, after):
    def moved(mask):
        count = row_count * head_count
        return lax.ppermute(value, BOTH, [(i, i ^ mask) for i in range(count)])

    masks = [1]
    bit = head_count
    while bit < row_count * head_count:
        masks.append(bit)
        bit = bit * 2
    done = 0
    while masks:
        if len(masks) == 1:
            value = value + moved(masks[0])
        else:
            first, second, both = (moved(m) for m in (masks[0], masks[1], masks[0] ^ masks[1]))
            value = (value + first) + (second + both)
        masks = masks[2:]
        done = done + 1
        value = after(done, value)
    return value


def swap_head(value, mask, head_count):
    return lax.ppermute(value, "head", [(i, i ^ mask) for i in range(head_count)])


def smem():
    return pl.BlockSpec(memory_space=pltpu.SMEM)


def vmem():
    return pl.BlockSpec(memory_space=pltpu.VMEM)


def hbm():
    return pl.BlockSpec(memory_space=pltpu.HBM)


def flag_shape():
    return jax.ShapeDtypeStruct((8, 128), F32)


def raise_flag(ref):
    ref[...] = jnp.zeros(ref.shape, F32)


def join_weights(meta, own, other, target, kinds):
    dim = own.shape[2]
    for index, kind in enumerate(kinds):
        for place in range(2):
            column = (index * 2 + place) * dim
            target[:, column : column + dim] = jnp.where(meta[1] == place, own[kind], other[kind])


def wide(value, count):
    return jnp.concatenate([value] * count, axis=1)


def line_of(columns):
    return jnp.transpose(columns)[0:1, :]


def column_of(line):
    return jnp.transpose(jnp.broadcast_to(line, (128, line.shape[1])))


def project_query_kernel(a, b, c, d, weights, q_out, flag):
    raise_flag(flag)
    half = a.shape[1] - PACK
    for high, pair in enumerate(((a, b), (c, d))):
        for place, ref in enumerate(pair):
            q_out[high, 0, place] = mm(ref[0, :half], weights[...]).astype(BF)


def project_query(mine, theirs, weights):
    slots, rows, width = mine[0].shape
    half = rows - PACK
    double = weights.shape[1]
    block = pl.BlockSpec((1, rows, width), lambda g: (g, 0, 0))
    whole = pl.BlockSpec(weights.shape, lambda g: (0, 0))
    out, flag = pl.pallas_call(
        project_query_kernel,
        out_shape=(jax.ShapeDtypeStruct((2, slots, 2, half, double), BF), flag_shape()),
        grid=(slots,),
        in_specs=[block] * 4 + [whole],
        out_specs=[
            pl.BlockSpec((2, 1, 2, half, double), lambda g: (0, g, 0, 0, 0)),
            pl.BlockSpec((8, 128), lambda g: (0, 0)),
        ],
        compiler_params=params(),
        cost_estimate=cost(8 * slots * half * width * double, 8 * slots * half * width),
        name="project_query",
    )(mine[0], theirs[0], mine[1], theirs[1], weights)
    return out.reshape(4 * slots, half, double), flag


def key_range(starts, low, high, data_count):
    first = jnp.int32(1 << 30)
    last = jnp.int32(0)
    for data in range(data_count):
        begin, end = starts[data], starts[data + 1]
        hit = (begin < high) & (end > low) & (begin < end)
        first = jnp.where(hit, jnp.minimum(first, begin), first)
        last = jnp.where(hit, jnp.maximum(last, end), last)
    return first, last


def shard_copies(meta, shard, gathered, x_ref, sem):
    slots = gathered[0].shape[0]
    copies = []
    for place in range(2):
        slot = slot_of(shard ^ meta[0], meta[2] ^ place, bit_orders(2 * slots))
        for bank in range(2):
            here = (slot < slots) if bank == 0 else (slot >= slots)
            source = gathered[place * 2 + bank]
            copy = pltpu.make_async_copy(
                source.at[jnp.where(here, slot - bank * slots, 0)],
                x_ref.at[shard, place],
                sem.at[shard, place],
            )
            copies.append((here, copy))
    return copies


def fetch_shards(meta, first, last, gathered, x_ref, sem):
    def start(shard, carry):
        for here, copy in shard_copies(meta, shard, gathered, x_ref, sem):

            @pl.when(here)
            def _():
                copy.start()

        return carry

    lax.fori_loop(first, last, start, 0)


def load_shard(meta, shard, gathered, x_ref, sem):
    half = x_ref.shape[2] - PACK
    parity = meta[2]
    for place in range(2):
        pltpu.make_async_copy(gathered[0].at[0], x_ref.at[shard, place], sem.at[shard, place]).wait()
    line = x_ref[shard, 0, half : half + 1, :].astype(F32)
    first, second = line[:, :half], line[:, half : 2 * half]
    line = jnp.concatenate(
        [jnp.where(parity == 0, first, second), jnp.where(parity == 0, second, first)], axis=1
    )
    return jnp.concatenate([x_ref[shard, 0, :half, :], x_ref[shard, 1, :half, :]], axis=0), line


def online(scores, factor, mask, m_ref, place):
    old_max = m_ref[place]
    size = old_max.shape[0]
    top = jnp.broadcast_to(jnp.max(scores, axis=1, keepdims=True) * factor, (size, 128))
    new_max = jnp.maximum(old_max, top)
    shift = new_max
    if mask is not None:
        new_max = jnp.where(mask, new_max, old_max)
        shift = jnp.where(mask, new_max, -NEGATIVE)
    m_ref[place] = new_max
    probs = jnp.exp2(scores * factor - wide(shift, scores.shape[1] // 128))
    return probs.astype(BF), jnp.exp2(old_max - new_max)


def accumulate(acc_ref, place, alpha, probs, value):
    with_ones = jnp.concatenate([value, jnp.ones((value.shape[0], 128), BF)], axis=1)
    acc_ref[place] = acc_ref[place] * wide(alpha, with_ones.shape[1] // 128) + mm(probs, with_ones)


def token_forward_kernel(
    data_count,
    factor,
    meta,
    starts,
    ids_ref,
    in_own,
    in_other,
    tok_hbm,
    mine_low,
    mine_high,
    theirs_low,
    theirs_high,
    q_ref,
    kv_own,
    wq_ref,
    wkv_ref,
    m_out,
    l_out,
    acc_out,
    flag,
    m_ref,
    acc_ref,
    x_ref,
    id_ref,
    tok_ref,
    sem,
    tok_sem,
):
    raise_flag(flag)
    size, dim = tok_ref.shape[1], in_own.shape[2]
    tok_copy = pltpu.make_async_copy(tok_hbm, tok_ref, tok_sem)
    tok_copy.start()
    base = meta[0] * size
    first, last = key_range(starts, base, base + size, data_count)
    first, last = first // size, (last + size - 1) // size
    gathered = (mine_low, mine_high, theirs_low, theirs_high)
    fetch_shards(meta, first, last, gathered, x_ref, sem)
    join_weights(meta, in_own, in_other, wq_ref, (0,))
    join_weights(meta, in_own, in_other, wkv_ref, (1, 2))
    tok_copy.wait()
    for slot in range(2):
        q_ref[slot] = mm(tok_ref[meta[1] ^ slot], wq_ref[...]).astype(BF)
    kv_own[...] = mm(tok_ref[meta[1]], wkv_ref[...]).astype(BF)
    m_ref[...] = jnp.full(m_ref.shape, NEGATIVE, F32)
    acc_ref[...] = jnp.zeros(acc_ref.shape, F32)
    id_ref[...] = column_of(ids_ref[meta[1]])
    rows = pl.ds(0, size)

    def step(shard, carry):
        raw_rows, line = load_shard(meta, shard, gathered, x_ref, sem)
        kv = mm(raw_rows, wkv_ref[...]).astype(BF)
        mask = wide(id_ref[...], size // 128) == line
        raw = [
            mm_nt(q_ref[0, :, h * dim : (h + 1) * dim], kv[:, h * dim : (h + 1) * dim])
            for h in range(2)
        ]
        parts = [
            online(jnp.where(mask, raw[h], NEGATIVE), factor, None, m_ref, (h, rows))
            for h in range(2)
        ]
        for h in range(2):
            value = kv[:, (2 + h) * dim : (3 + h) * dim]
            accumulate(acc_ref, (h, rows), parts[h][1], parts[h][0], value)
        return carry

    lax.fori_loop(first, last, step, 0)
    for h in range(2):
        m_out[h : h + 1, :] = line_of(m_ref[h])
        l_out[h : h + 1, :] = line_of(acc_ref[h, :, dim:])
        acc_out[h] = acc_ref[h, :, :dim]


def shard_scratch(banks):
    slots, rows, width = banks[0].shape
    return pltpu.VMEM((2 * slots, 2, rows, width), BF)


def token_forward(meta, starts, tokens, ids_rows, mine, theirs, in_own, in_other, factor, data_count):
    size, width = tokens.shape[1:]
    dim = in_own.shape[2]
    return pl.pallas_call(
        functools.partial(token_forward_kernel, data_count, factor),
        out_shape=(
            jax.ShapeDtypeStruct((2, size, 2 * dim), BF),
            jax.ShapeDtypeStruct((size, 4 * dim), BF),
            jax.ShapeDtypeStruct((width, 2 * dim), BF),
            jax.ShapeDtypeStruct((width, 4 * dim), BF),
            jax.ShapeDtypeStruct((2, size), F32),
            jax.ShapeDtypeStruct((2, size), F32),
            jax.ShapeDtypeStruct((2, size, dim), F32),
            flag_shape(),
        ),
        in_specs=[smem(), smem()] + [vmem()] * 3 + [hbm()] * 5,
        out_specs=[vmem()] * 8,
        scratch_shapes=[
            pltpu.VMEM((2, size, 128), F32),
            pltpu.VMEM((2, size, dim + 128), F32),
            shard_scratch(mine),
            pltpu.VMEM((size, 128), F32),
            pltpu.VMEM(tokens.shape, BF),
            pltpu.SemaphoreType.DMA((2 * mine[0].shape[0], 2)),
            pltpu.SemaphoreType.DMA,
        ],
        compiler_params=params(spare=VMEM_LIMIT),
        cost_estimate=cost(8e9, 8e6, 2e6),
        name="token_forward",
    )(meta, starts, ids_rows, in_own, in_other, tokens, *mine, *theirs)


def half_rows(block):
    return -(-block // 32) * 16


def fetch_prompts(meta, local, table, sources, raws, state, sem):
    pieces = raws.shape[2]
    slots = sources[0].shape[0]
    for number in range(state.shape[0]):
        state[number] = 0
    for batch in range(2):
        for data in range(table.shape[1]):
            number = table[batch, data]
            used = local[batch, data + 1] > local[batch, data]
            state[number] = jnp.where(used, 1, state[number])

    def start(number, carry):
        @pl.when(state[number] == 1)
        def _():
            for piece in range(pieces):
                for place in range(2):
                    shard = number * pieces + piece
                    slot = slot_of(shard ^ meta[0], meta[2] ^ place, prompt_orders(2 * slots))
                    for bank in range(2):

                        @pl.when((slot < slots) if bank == 0 else (slot >= slots))
                        def _():
                            pltpu.make_async_copy(
                                sources[place * 2 + bank].at[slot - bank * slots],
                                raws.at[place, number, piece],
                                sem.at[place, number, piece],
                            ).start()

        return carry

    lax.fori_loop(0, state.shape[0], start, 0)


def project_prompt(meta, number, sources, raws, w_ref, kv_ref, state, sem):
    pieces, block = raws.shape[2:4]

    @pl.when(state[number] == 1)
    def _():
        even = meta[2] == 0
        for piece in range(pieces):
            for place in range(2):
                pltpu.make_async_copy(
                    sources[0].at[0], raws.at[place, number, piece], sem.at[place, number, piece]
                ).wait()
            a, b = raws[0, number, piece], raws[1, number, piece]
            rows = jnp.concatenate([jnp.where(even, a, b), jnp.where(even, b, a)], axis=1)
            kv_ref[number, pl.ds(piece * block, block), :] = mm(rows, w_ref[...]).astype(BF)
        full = pieces * block
        if full < kv_ref.shape[1]:
            kv_ref[number, full:, :] = jnp.zeros((kv_ref.shape[1] - full, kv_ref.shape[2]), BF)
        state[number] = 2


def prompt_mask(meta, scores, block):
    part = half_rows(block)
    pieces = PLEN // block
    doubled = 2 * part - block
    head = min(128, part) if pieces == 1 else scores.shape[1]
    lanes = lax.broadcasted_iota(jnp.int32, (scores.shape[0], head), 1)
    out = (lanes % part < doubled * meta[1]) | (lanes >= pieces * part)
    first = jnp.where(out, NEGATIVE, scores[:, :head])
    if head == scores.shape[1]:
        return first
    return jnp.concatenate([first, scores[:, head:]], axis=1)


def visit_prompts(meta, local, table, size, prepare, update):
    data_count = table.shape[1]

    def visit(index, carry):
        slot, data = index // data_count, index % data_count
        batch = meta[1] ^ slot
        begin, end = local[batch, data], local[batch, data + 1]

        @pl.when(begin < end)
        def _():
            number = table[batch, data]
            prepare(number)
            low = begin // 128
            count = (end + 127) // 128 - low
            for case in range(1, size // 128 + 1):

                @pl.when(count == case)
                def _():
                    rows = pl.ds(pl.multiple_of(low * 128, 128), case * 128)
                    update(slot, rows, data, number)

        return carry

    lax.fori_loop(0, 2 * data_count, visit, 0)


def store_line(ref, row, line):
    width = ref.shape[1]
    for term in split3(line):
        for low in range(0, line.shape[1], width):
            ref[row : row + 1, :] = term[:, low : low + width]
            row = row + 1
    return row


def load_line(ref, row, length):
    width = ref.shape[1]
    rows_per = length // width
    total = 0.0
    for place in range(3):
        first = row + place * rows_per
        pieces = [ref[first + i : first + i + 1, :].astype(F32) for i in range(rows_per)]
        total = total + jnp.concatenate(pieces, axis=1)
    return total


def prompt_forward_kernel(
    block,
    factor,
    meta,
    local,
    table,
    q_ref,
    ids_ref,
    m_in,
    l_in,
    acc_in,
    _,
    w_ref,
    mine_low,
    mine_high,
    theirs_low,
    theirs_high,
    wide_ref,
    lse_ref,
    send_ref,
    m_ref,
    acc_ref,
    raws,
    kv_ref,
    id_ref,
    state,
    sem,
):
    size, dim = q_ref.shape[1], q_ref.shape[2] // 2
    sources = (mine_low, mine_high, theirs_low, theirs_high)
    fetch_prompts(meta, local, table, sources, raws, state, sem)
    for h in range(2):
        m_ref[0, h] = column_of(m_in[h : h + 1, :])
        acc_ref[0, h, :, dim:] = column_of(l_in[h : h + 1, :])
        acc_ref[0, h, :, :dim] = acc_in[h]
    m_ref[1] = jnp.full(m_ref.shape[1:], NEGATIVE, F32)
    acc_ref[1] = jnp.zeros(acc_ref.shape[1:], F32)
    for slot in range(2):
        id_ref[slot] = column_of(ids_ref[meta[1] ^ slot])

    def prepare(number):
        project_prompt(meta, number, sources, raws, w_ref, kv_ref, state, sem)

    def update(slot, rows, data, number):
        mask = id_ref[slot, rows, :] == data.astype(F32)
        raw = [
            mm_nt(q_ref[slot, rows, pl.ds(h * dim, dim)], kv_ref[number, :, pl.ds(h * dim, dim)])
            for h in range(2)
        ]
        parts = [
            online(prompt_mask(meta, raw[h], block), factor, mask, m_ref, (slot, h, rows))
            for h in range(2)
        ]
        for h in range(2):
            value = kv_ref[number, :, pl.ds((2 + h) * dim, dim)]
            accumulate(acc_ref, (slot, h, rows), parts[h][1], parts[h][0], value)

    visit_prompts(meta, local, table, size, prepare, update)
    row = size
    send_ref[pl.ds(size, PACK), :] = jnp.zeros((PACK, 2 * dim), BF)
    for h in range(2):
        cols = pl.ds(h * dim, dim)
        total = acc_ref[0, h, :, dim:]
        wide_ref[:, cols] = acc_ref[0, h, :, :dim] / total
        lse_ref[h : h + 1, :] = line_of(m_ref[0, h] + jnp.log2(total))
        total = acc_ref[1, h, :, dim:]
        send_ref[pl.ds(0, size), cols] = (acc_ref[1, h, :, :dim] / total).astype(BF)
        line = line_of(m_ref[1, h] + jnp.log2(total))
        row = store_line(send_ref, row, line)


def prompt_scratch(prompt_banks, dim, block):
    slots, part, columns = prompt_banks[0].shape
    pieces = PLEN // block
    count = 2 * slots // pieces
    return [
        pltpu.VMEM((2, count, pieces, part, columns), BF),
        pltpu.VMEM((count, -(-pieces * part // 128) * 128, 4 * dim), BF),
    ], [pltpu.SMEM((count,), jnp.int32), pltpu.SemaphoreType.DMA((2, count, pieces))]


def prompt_forward(
    meta, local, table, q_own, ids_rows, state, flag, prompt_mine, prompt_theirs, weights, factor, block
):
    size, dim = q_own.shape[1], q_own.shape[2] // 2
    buffers, flags = prompt_scratch(prompt_mine, dim, block)
    return pl.pallas_call(
        functools.partial(prompt_forward_kernel, block, factor),
        out_shape=(
            jax.ShapeDtypeStruct((size, 2 * dim), F32),
            jax.ShapeDtypeStruct((2, size), F32),
            jax.ShapeDtypeStruct((size + PACK, 2 * dim), BF),
        ),
        in_specs=[smem()] * 3 + [vmem()] * 7 + [hbm()] * 4,
        out_specs=[vmem()] * 3,
        scratch_shapes=[
            pltpu.VMEM((2, 2, size, 128), F32),
            pltpu.VMEM((2, 2, size, dim + 128), F32),
            *buffers,
            pltpu.VMEM((2, size, 128), F32),
            *flags,
        ],
        compiler_params=params(*prompt_mine, *prompt_mine, *prompt_mine),
        cost_estimate=cost(4e9, 8e6, 2e6),
        name="prompt_forward",
    )(meta, local, table, q_own, ids_rows, *state, flag, weights, *prompt_mine, *prompt_theirs)


def join_kernel(wide_in, lse_in, other_ref, o_ref, wide_ref, lse_ref):
    size, dim = wide_in.shape[0], wide_in.shape[1] // 2
    rows_per = size // (2 * dim)
    for h in range(2):
        cols = pl.ds(h * dim, dim)
        first = column_of(lse_in[h : h + 1, :])
        second = column_of(load_line(other_ref, size + h * 3 * rows_per, size))
        top = jnp.maximum(first, second)
        first, second = jnp.exp2(first - top), jnp.exp2(second - top)
        total = first + second
        other = other_ref[pl.ds(0, size), cols].astype(F32)
        attended = (first * wide_in[:, cols] + second * other) / total
        wide_ref[:, cols] = attended
        o_ref[:, cols] = attended.astype(BF)
        lse_ref[h : h + 1, :] = line_of(top + jnp.log2(total))


def join_halves(wide_half, lse_half, other):
    return pl.pallas_call(
        join_kernel,
        out_shape=(
            jax.ShapeDtypeStruct(wide_half.shape, BF),
            jax.ShapeDtypeStruct(wide_half.shape, F32),
            jax.ShapeDtypeStruct(lse_half.shape, F32),
        ),
        in_specs=[vmem()] * 3,
        out_specs=[vmem()] * 3,
        compiler_params=params(),
        cost_estimate=cost(4e6, 3e6, 1e6),
        name="join_halves",
    )(wide_half, lse_half, other)


def norm_parts(value):
    center = value - jnp.mean(value, axis=-1, keepdims=True)
    scale = lax.rsqrt(jnp.mean(center * center, axis=-1, keepdims=True) + 1e-05)
    return center * scale, scale


def norm_back(grad, unit, scale, gain):
    part = grad * gain
    return scale * (
        part
        - jnp.mean(part, axis=-1, keepdims=True)
        - unit * jnp.mean(part * unit, axis=-1, keepdims=True)
    )


def feed_kernel(
    meta,
    mine,
    theirs,
    wide_ref,
    lse_ref,
    tok_ref,
    cot_ref,
    down_bias,
    gains,
    shifts,
    w_own,
    w_along,
    w_core,
    w_far,
    out_ref,
    da_ref,
    pack_ref,
    delta_ref,
    w_ref,
    sem,
):
    size, width = tok_ref.shape
    dim = mine.shape[1] // 2
    heads = w_ref.shape[0]
    hid = (w_ref.shape[1] - PACK - dim) // 2
    batch, parity = meta[1], meta[2]
    even = parity == 0
    cuts = (pl.ds(hid, dim), pl.ds(hid + dim, hid + PACK), pl.ds(0, hid))

    def arrived(part):
        for q in range(heads):
            pltpu.make_async_copy(
                w_own.at[cuts[part]], w_ref.at[q, cuts[part]], sem.at[q, part]
            ).wait()

    for q in range(heads):
        for place, ref in enumerate((w_own, w_along, w_core, w_far)):

            @pl.when((2 * batch + parity) == (q ^ (0, 2, 1, 3)[place]))
            def _():
                for part, rows in enumerate(cuts):
                    pltpu.make_async_copy(
                        ref.at[rows], w_ref.at[q, rows], sem.at[q, part]
                    ).start()

    place_out = slice(hid, hid + dim)
    place_up = slice(hid + dim, 2 * hid + dim)
    place_bias = 2 * hid + dim
    sub = size
    pack_ref[pl.ds(size, STATS), :] = jnp.zeros((STATS, 2 * dim), BF)
    g0, g1 = gains[0:1, :], gains[1:2, :]
    for part in range(size // sub):
        rows = pl.ds(part * sub, sub)
        a, b = mine[rows, :], theirs[rows, :]
        if part == 0:
            arrived(0)
        first = jnp.where(even, a, b)
        second = jnp.where(even, b, a)
        attn = mm(first[:, :dim], w_ref[0, place_out, :])
        attn += mm(second[:, :dim], w_ref[1, place_out, :])
        attn += mm(first[:, dim:], w_ref[2, place_out, :])
        attn += mm(second[:, dim:], w_ref[3, place_out, :])
        unit_one, scale_one = norm_parts(tok_ref[rows, :].astype(F32) + attn)
        normed = unit_one * g0 + shifts[0:1, :]
        normed_low = normed.astype(BF)
        branch = down_bias[...]
        slopes = []
        if part == 0:
            arrived(1)
            arrived(2)
        for q in range(heads):
            bias = (
                w_ref[q, place_bias : place_bias + 1, :hid].astype(F32)
                + w_ref[q, place_bias : place_bias + 1, hid : 2 * hid].astype(F32)
                + w_ref[q, place_bias + 1 : place_bias + 2, :hid].astype(F32)
            )
            pre = mm_nt(normed_low, w_ref[q, place_up, :]) + bias
            cdf = 0.5 * (1.0 + lax.erf(pre * 0.7071067811865476))
            slopes.append(cdf + pre * (jnp.exp(-0.5 * pre * pre) * 0.3989422804014327))
            branch = branch + mm((pre * cdf).astype(BF), w_ref[q, :hid, :])
        unit_two, scale_two = norm_parts(normed + branch)
        out_ref[rows, :] = (unit_two * g1 + shifts[1:2, :]).astype(BF)
        grad_mixed = norm_back(cot_ref[rows, :].astype(F32), unit_two, scale_two, g1)
        mixed_low = grad_mixed.astype(BF)
        grad_normed = grad_mixed
        for q in range(heads):
            grad_pre = mm_nt(mixed_low, w_ref[q, :hid, :]) * slopes[q]
            grad_normed = grad_normed + mm(grad_pre.astype(BF), w_ref[q, place_up, :])
        grad_sum = norm_back(grad_normed, unit_one, scale_one, g0)
        da_ref[rows, :] = grad_sum
        sum_low = grad_sum.astype(BF)
        for head in range(2):
            cols = pl.ds(head * dim, dim)
            grad_out = mm_nt(sum_low, w_ref[2 * head + parity, place_out, :]).astype(BF)
            pack_ref[rows, cols] = grad_out
            delta = jnp.sum(grad_out.astype(F32) * wide_ref[rows, cols], axis=1, keepdims=True)
            delta_ref[head : head + 1, rows] = line_of(jnp.broadcast_to(delta, (sub, 128)))
    row = size
    for head in range(2):
        for ref in (lse_ref, delta_ref):
            row = store_line(pack_ref, row, ref[head : head + 1, :])


def feed(meta, mine, theirs, wide_out, lse, tokens, cotangent, w, down_bias, gains, shifts):
    size, width = tokens.shape
    dim = mine.shape[1] // 2
    return pl.pallas_call(
        feed_kernel,
        out_shape=(
            jax.ShapeDtypeStruct((size, width), BF),
            jax.ShapeDtypeStruct((size, width), F32),
            jax.ShapeDtypeStruct((size + STATS, 2 * dim), BF),
            jax.ShapeDtypeStruct((2, size), F32),
        ),
        in_specs=[smem()] + [vmem()] * 9 + [hbm()] * 4,
        out_specs=[vmem()] * 4,
        scratch_shapes=[pltpu.VMEM((4,) + w[0].shape, BF), pltpu.SemaphoreType.DMA((4, 3))],
        compiler_params=params(),
        cost_estimate=cost(3e9, 8e6, 1e6),
        name="feed",
    )(meta, mine, theirs, wide_out, lse, tokens, cotangent, down_bias, gains, shifts, *w)


def low_grads(scores, factor, shift, grads, delta):
    count = scores.shape[1] // 128
    probs = jnp.exp2(scores * factor - wide(shift, count))
    return (probs * (grads - wide(delta, count))).astype(BF)


def token_query_grad_kernel(
    data_count,
    factor,
    meta,
    starts,
    q_ref,
    ids_ref,
    lse_ref,
    delta_ref,
    do_ref,
    acc_in,
    w_ref,
    mine_low,
    mine_high,
    theirs_low,
    theirs_high,
    dq_ref,
    flag,
    acc_ref,
    x_ref,
    id_ref,
    lse_cols,
    delta_cols,
    sem,
):
    raise_flag(flag)
    size, dim = q_ref.shape[1], q_ref.shape[2] // 2
    base = meta[0] * size
    first, last = key_range(starts, base, base + size, data_count)
    first, last = first // size, (last + size - 1) // size
    gathered = (mine_low, mine_high, theirs_low, theirs_high)
    fetch_shards(meta, first, last, gathered, x_ref, sem)
    for h in range(2):
        lse_cols[h] = column_of(lse_ref[h : h + 1, :])
        delta_cols[h] = column_of(delta_ref[h : h + 1, :])
    acc_ref[...] = acc_in[...]
    id_ref[...] = column_of(ids_ref[meta[1]])

    def step(shard, carry):
        raw_rows, line = load_shard(meta, shard, gathered, x_ref, sem)
        kv = mm(raw_rows, w_ref[...]).astype(BF)
        mask = wide(id_ref[...], size // 128) == line
        raw, grads, low = [], [], []
        for h in range(2):
            raw.append(mm_nt(q_ref[0, :, h * dim : (h + 1) * dim], kv[:, h * dim : (h + 1) * dim]))
            grads.append(
                mm_nt(
                    do_ref[pl.ds(0, size), h * dim : (h + 1) * dim],
                    kv[:, (2 + h) * dim : (3 + h) * dim],
                )
            )
        for h in range(2):
            scores = jnp.where(mask, raw[h], NEGATIVE)
            low.append(low_grads(scores, factor, lse_cols[h], grads[h], delta_cols[h]))
        for h in range(2):
            acc_ref[h] += mm(low[h], kv[:, h * dim : (h + 1) * dim])
        return carry

    lax.fori_loop(first, last, step, 0)
    for h in range(2):
        dq_ref[:, pl.ds(h * dim, dim)] = acc_ref[h] * dim ** (-0.5)


def token_query_grad(
    meta, starts, q_own, ids_rows, lse, delta, pack, acc, mine, theirs, weights, factor, data_count
):
    size, dim = q_own.shape[1], q_own.shape[2] // 2
    return pl.pallas_call(
        functools.partial(token_query_grad_kernel, data_count, factor),
        out_shape=(jax.ShapeDtypeStruct((size, 2 * dim), F32), flag_shape()),
        in_specs=[smem()] * 2 + [vmem()] * 7 + [hbm()] * 4,
        out_specs=[vmem()] * 2,
        scratch_shapes=[
            pltpu.VMEM((2, size, dim), F32),
            shard_scratch(mine),
            pltpu.VMEM((size, 128), F32),
            pltpu.VMEM((2, size, 128), F32),
            pltpu.VMEM((2, size, 128), F32),
            pltpu.SemaphoreType.DMA((2 * mine[0].shape[0], 2)),
        ],
        compiler_params=params(*mine, *theirs),
        cost_estimate=cost(6e9, 16e6, 4e6),
        name="token_query_grad",
    )(
        meta,
        starts,
        q_own,
        ids_rows,
        lse,
        delta,
        pack,
        acc,
        weights,
        *mine,
        *theirs,
    )


def prompt_query_grad_kernel(
    block,
    factor,
    meta,
    local,
    table,
    q_ref,
    ids_ref,
    lse_in,
    delta_in,
    pack_own,
    pack_other,
    _,
    w_ref,
    mine_low,
    mine_high,
    theirs_low,
    theirs_high,
    dq_ref,
    send_ref,
    acc_ref,
    lse_ref,
    delta_ref,
    do_ref,
    raws,
    kv_ref,
    id_ref,
    state,
    sem,
):
    size, dim = q_ref.shape[1], q_ref.shape[2] // 2
    rows_per = size // (2 * dim)
    sources = (mine_low, mine_high, theirs_low, theirs_high)
    fetch_prompts(meta, local, table, sources, raws, state, sem)
    acc_ref[...] = jnp.zeros(acc_ref.shape, F32)
    for h in range(2):
        lse_ref[0, h] = column_of(lse_in[h : h + 1, :])
        delta_ref[0, h] = column_of(delta_in[h : h + 1, :])
    do_ref[0] = pack_own[pl.ds(0, size), :]
    do_ref[1] = pack_other[pl.ds(0, size), :]
    for h in range(2):
        for kind, ref in enumerate((lse_ref, delta_ref)):
            row = size + (h * 2 + kind) * 3 * rows_per
            ref[1, h] = column_of(load_line(pack_other, row, size))
    for slot in range(2):
        id_ref[slot] = column_of(ids_ref[meta[1] ^ slot])

    def prepare(number):
        project_prompt(meta, number, sources, raws, w_ref, kv_ref, state, sem)

    def update(slot, rows, data, number):
        mask = id_ref[slot, rows, :] == data.astype(F32)
        raw, grads, low = [], [], []
        for h in range(2):
            cols = pl.ds(h * dim, dim)
            raw.append(mm_nt(q_ref[slot, rows, cols], kv_ref[number, :, cols]))
            value = kv_ref[number, :, pl.ds((2 + h) * dim, dim)]
            grads.append(mm_nt(do_ref[slot, rows, cols], value))
        for h in range(2):
            shift = jnp.where(mask, lse_ref[slot, h, rows, :], -NEGATIVE)
            scores = prompt_mask(meta, raw[h], block)
            low.append(low_grads(scores, factor, shift, grads[h], delta_ref[slot, h, rows, :]))
        for h in range(2):
            acc_ref[slot, h, rows, :] += mm(low[h], kv_ref[number, :, pl.ds(h * dim, dim)])

    visit_prompts(meta, local, table, size, prepare, update)
    for h in range(2):
        cols = pl.ds(h * dim, dim)
        dq_ref[h] = acc_ref[0, h]
        send_ref[:, cols] = (acc_ref[1, h] * dim ** (-0.5)).astype(BF)


def prompt_query_grad(
    meta,
    local,
    table,
    q_own,
    ids_rows,
    lse,
    delta,
    pack,
    pack_other,
    flag,
    prompt_mine,
    prompt_theirs,
    weights,
    factor,
    block,
):
    size, dim = q_own.shape[1], q_own.shape[2] // 2
    buffers, flags = prompt_scratch(prompt_mine, dim, block)
    return pl.pallas_call(
        functools.partial(prompt_query_grad_kernel, block, factor),
        out_shape=(
            jax.ShapeDtypeStruct((2, size, dim), F32),
            jax.ShapeDtypeStruct((size, 2 * dim), BF),
        ),
        in_specs=[smem()] * 3 + [vmem()] * 8 + [hbm()] * 4,
        out_specs=[vmem()] * 2,
        scratch_shapes=[
            pltpu.VMEM((2, 2, size, dim), F32),
            pltpu.VMEM((2, 2, size, 128), F32),
            pltpu.VMEM((2, 2, size, 128), F32),
            pltpu.VMEM((2, size, 2 * dim), BF),
            *buffers,
            pltpu.VMEM((2, size, 128), F32),
            *flags,
        ],
        compiler_params=params(*prompt_mine, *prompt_mine, *prompt_mine, *prompt_mine),
        cost_estimate=cost(6e9, 16e6, 4e6),
        name="prompt_query_grad",
    )(
        meta,
        local,
        table,
        q_own,
        ids_rows,
        lse,
        delta,
        pack,
        pack_other,
        flag,
        weights,
        *prompt_mine,
        *prompt_theirs,
    )


def in_bank(meta, index, bank, slots):
    slot = slot_of((index // 2) ^ meta[0], meta[2], bit_orders(2 * slots))
    return (slot < slots) if bank == 0 else (slot >= slots)


def half_shard(meta, index, q_ref, ids_ref, low_ref, high_ref):
    slots, rows, double = (high_ref if low_ref is None else low_ref).shape
    half = q_ref.shape[1]
    size = rows - STATS
    shard, part = index // 2, index % 2
    slot = slot_of(shard ^ meta[0], meta[2], bit_orders(2 * slots))
    other = slot_of(shard ^ meta[0], 1 - meta[2], bit_orders(2 * slots))
    query = q_ref[jnp.where(part == meta[2], slot * 2, other * 2 + 1)]
    in_low = slot < slots
    place_low, place_high = jnp.minimum(slot, slots - 1), jnp.maximum(slot - slots, 0)
    span = pl.ds(pl.multiple_of(part * half, half), half)
    tail = pl.ds(size, STATS)

    def take(rows):
        if high_ref is None:
            return low_ref[place_low, rows, :]
        if low_ref is None:
            return high_ref[place_high, rows, :]
        return jnp.where(in_low, low_ref[place_low, rows, :], high_ref[place_high, rows, :])

    grad = take(span)
    line = ids_ref[slot]
    line = jnp.where(part == 0, line[:, :half], line[:, half : 2 * half])
    stats = take(tail).astype(F32)
    rows_per = size // double

    def stat(head, kind):
        total = 0.0
        for place in range(3):
            row = ((head * 2 + kind) * 3 + place) * rows_per
            term = stats[row : row + 1, :]
            for i in range(1, rows_per):
                term = jnp.where(part == i, stats[row + i : row + i + 1, :], term)
            total = total + term
        return total

    return query, grad, line, stat


def key_update(query, grad, kv_ref, mask, rows_mask, stat, factor, dk_ref, dv_ref):
    dim = query.shape[1] // 2
    cols = [slice(h * dim, (h + 1) * dim) for h in range(2)]
    raw = [mm_nt(kv_ref[:, cols[h]], query[:, cols[h]]) for h in range(2)]
    grads = [mm_nt(kv_ref[:, pl.ds((2 + h) * dim, dim)], grad[:, cols[h]]) for h in range(2)]
    probs, low = [], []
    for h in range(2):
        shift = stat(h, 0)
        scores = raw[h]
        if rows_mask is None:
            shift = jnp.where(mask, shift, -NEGATIVE)
        else:
            scores = jnp.where(rows_mask, scores, NEGATIVE)
        p = jnp.exp2(scores * factor - shift)
        probs.append(p.astype(BF))
        low.append((p * (grads[h] - stat(h, 1))).astype(BF))
    for h in range(2):
        dv_ref[:, cols[h]] += mm(probs[h], grad[:, cols[h]])
        dk_ref[:, cols[h]] += mm(low[h], query[:, cols[h]])


def prompt_terms(data_count, factor, bank, meta, starts, table, q_ref, ids_ref, pack_ref, kv_ref, dk_ref, dv_ref):
    half = q_ref.shape[1]
    number = meta[0] * kv_ref.shape[0] // PLEN
    low_ref, high_ref = (pack_ref, None) if bank == 0 else (None, pack_ref)

    def visit(data, carry):
        begin, end = starts[data], starts[data + 1]

        @pl.when((table[meta[1], data] == number) & (begin < end))
        def _():
            def step(index, inner):
                @pl.when(in_bank(meta, index, bank, pack_ref.shape[0]))
                def _():
                    query, grad, line, stat = half_shard(
                        meta, index, q_ref, ids_ref, low_ref, high_ref
                    )
                    mask = line == data.astype(F32)
                    key_update(query, grad, kv_ref, mask, None, stat, factor, dk_ref, dv_ref)

                return inner

            lax.fori_loop(begin // half, (end + half - 1) // half, step, 0)

        return carry

    lax.fori_loop(0, data_count, visit, 0)


def prompt_grad_first_kernel(
    data_count,
    factor,
    meta,
    starts,
    table,
    q_ref,
    ids_ref,
    pack_ref,
    kv_ref,
    _,
    dk_ref,
    dv_ref,
    flag,
):
    raise_flag(flag)
    dk_ref[...] = jnp.zeros(dk_ref.shape, F32)
    dv_ref[...] = jnp.zeros(dv_ref.shape, F32)
    prompt_terms(
        data_count, factor, 0, meta, starts, table, q_ref, ids_ref, pack_ref, kv_ref, dk_ref, dv_ref
    )


def prompt_grad_last_kernel(
    data_count,
    factor,
    meta,
    starts,
    table,
    q_ref,
    ids_ref,
    pack_ref,
    kv_ref,
    dk_in,
    dv_in,
    w_ref,
    keep_ref,
    send_ref,
    dk_ref,
    dv_ref,
):
    width = w_ref.shape[0]
    dim = kv_ref.shape[1] // 4
    dk_ref[...] = dk_in[...]
    dv_ref[...] = dv_in[...]
    prompt_terms(
        data_count, factor, 1, meta, starts, table, q_ref, ids_ref, pack_ref, kv_ref, dk_ref, dv_ref
    )
    grads = jnp.concatenate(
        [(dk_ref[...] * dim ** (-0.5)).astype(BF), dv_ref[...].astype(BF)], axis=1
    )
    split = width // 2
    parity = meta[2]
    send = w_ref[pl.ds(pl.multiple_of((1 - parity) * split, split), split), :]
    keep = w_ref[pl.ds(pl.multiple_of(parity * split, split), split), :]
    send_ref[...] = mm_nt(grads, send).astype(BF)
    keep_ref[...] = mm_nt(grads, keep)


def prompt_grad_first(meta, starts, table, q_all, ids_all, pack, kv, flag, factor, data_count):
    block, dim = kv.shape[0], kv.shape[1] // 4
    shape = jax.ShapeDtypeStruct((block, 2 * dim), F32)
    return pl.pallas_call(
        functools.partial(prompt_grad_first_kernel, data_count, factor),
        out_shape=(shape, shape, flag_shape()),
        in_specs=[smem()] * 3 + [vmem()] * 5,
        out_specs=[vmem()] * 3,
        compiler_params=params(q_all, pack),
        cost_estimate=cost(6e9, 16e6, 4e6),
        name="prompt_grad_first",
    )(meta, starts, table, q_all, ids_all, pack, kv, flag)


def prompt_grad_last(meta, starts, table, q_all, ids_all, pack, kv, terms, weights, factor, data_count):
    block, width = kv.shape[0], weights.shape[0]
    dim = kv.shape[1] // 4
    return pl.pallas_call(
        functools.partial(prompt_grad_last_kernel, data_count, factor),
        out_shape=(
            jax.ShapeDtypeStruct((block, width // 2), F32),
            jax.ShapeDtypeStruct((block, width // 2), BF),
        ),
        in_specs=[smem()] * 3 + [vmem()] * 7,
        out_specs=[vmem(), vmem()],
        scratch_shapes=[
            pltpu.VMEM((block, 2 * dim), F32),
            pltpu.VMEM((block, 2 * dim), F32),
        ],
        compiler_params=params(q_all, pack),
        cost_estimate=cost(6e9, 16e6, 4e6),
        name="prompt_grad_last",
    )(meta, starts, table, q_all, ids_all, pack, kv, *terms, weights)


def token_grad_kernel(
    data_count,
    factor,
    meta,
    starts,
    q_ref,
    ids_ref,
    low_ref,
    high_ref,
    kv_ref,
    own_ids,
    dq_ref,
    dq_other,
    wq_ref,
    wkv_ref,
    out_ref,
    flag,
    dk_ref,
    dv_ref,
    id_ref,
):
    raise_flag(flag)
    size = kv_ref.shape[0]
    half = q_ref.shape[1]
    dim = kv_ref.shape[1] // 4
    base = meta[0] * size
    first, last = key_range(starts, base, base + size, data_count)
    dk_ref[...] = jnp.zeros(dk_ref.shape, F32)
    dv_ref[...] = jnp.zeros(dv_ref.shape, F32)
    id_ref[...] = column_of(own_ids[meta[1]])

    def step(index, carry):
        query, grad, line, stat = half_shard(meta, index, q_ref, ids_ref, low_ref, high_ref)
        mask = wide(id_ref[...], half // 128) == line
        key_update(query, grad, kv_ref, None, mask, stat, factor, dk_ref, dv_ref)
        return carry

    lax.fori_loop(first // half, (last + half - 1) // half, step, 0)
    dq = (dq_ref[...] + dq_other[...].astype(F32)).astype(BF)
    grads = jnp.concatenate(
        [(dk_ref[...] * dim ** (-0.5)).astype(BF), dv_ref[...].astype(BF)], axis=1
    )
    out_ref[...] = (mm_nt(dq, wq_ref[...]) + mm_nt(grads, wkv_ref[...])).astype(BF)


def token_grad(
    meta, starts, q_all, ids_all, packs, kv_own, ids_rows, dq, weights, factor, data_count
):
    size, dim = kv_own.shape[0], kv_own.shape[1] // 4
    width = weights[0].shape[0]
    return pl.pallas_call(
        functools.partial(token_grad_kernel, data_count, factor),
        out_shape=(jax.ShapeDtypeStruct((size, width), BF), flag_shape()),
        in_specs=[smem()] * 2 + [vmem()] * 10,
        out_specs=[vmem()] * 2,
        scratch_shapes=[
            pltpu.VMEM((size, 2 * dim), F32),
            pltpu.VMEM((size, 2 * dim), F32),
            pltpu.VMEM((size, 128), F32),
        ],
        compiler_params=params(spare=VMEM_LIMIT),
        cost_estimate=cost(4e9, 16e6, 4e6),
        name="token_grad",
    )(meta, starts, q_all, ids_all, *packs, kv_own, ids_rows, *dq, *weights)


def sum_prompt_kernel(a_ref, b_ref, _, sum_ref, square_ref):
    low = (a_ref[...].astype(F32) + b_ref[...].astype(F32)).astype(BF)
    sum_ref[...] = low
    value = low.astype(F32)
    square_ref[...] = jnp.broadcast_to(jnp.sum(value * value, keepdims=True), square_ref.shape)


def sum_prompt(a, b, flag):
    return pl.pallas_call(
        sum_prompt_kernel,
        out_shape=(
            jax.ShapeDtypeStruct(a.shape, BF),
            jax.ShapeDtypeStruct((8, 128), F32),
        ),
        in_specs=[vmem()] * 3,
        out_specs=[vmem(), vmem()],
        compiler_params=params(),
        cost_estimate=cost(4 * a.size, 6 * a.size),
        name="sum_prompt",
    )(a, b, flag)


def optimizer_kernel(
    meta,
    biases,
    mine,
    theirs,
    squares,
    prompts,
    one_in,
    two_in,
    clip_out,
    one_out,
    two_out,
    new_out,
    norm_ref,
    held,
    sem,
):
    even = meta[2] == 0
    block = prompts.shape[0]
    tiles = sem.shape[1]
    tile = block // tiles
    norm_ref[...] = jnp.sqrt(squares[...])
    norm = norm_ref[0:1, :]
    factor = jnp.minimum(1.0, CLIP_NORM / (norm + 1e-06))
    copies = []
    for index in range(tiles):
        rows = pl.ds(index * tile, tile)
        a, b = mine[rows, :].astype(F32), theirs[rows, :].astype(F32)
        grads = jnp.concatenate([jnp.where(even, a, b), jnp.where(even, b, a)], axis=1)
        clipped = grads * wide(factor, grads.shape[1] // 128)
        new_one = BETA_ONE * one_in[rows, :] + (1.0 - BETA_ONE) * clipped
        new_two = BETA_TWO * two_in[rows, :] + (1.0 - BETA_TWO) * clipped * clipped
        first_hat = new_one / biases[0]
        second_hat = new_two / biases[1]
        held[0, rows, :] = clipped
        held[1, rows, :] = new_one
        held[2, rows, :] = new_two
        held[3, rows, :] = prompts[rows, :] * (
            1.0 - LEARNING_RATE * DECAY_RATE
        ) - LEARNING_RATE * first_hat / (jnp.sqrt(second_hat) + EPSILON)
        for place, out in enumerate((clip_out, one_out, two_out, new_out)):
            copies.append(
                pltpu.make_async_copy(held.at[place, rows], out.at[rows], sem.at[place, index])
            )
            copies[-1].start()
    for copy in copies:
        copy.wait()


def optimizer(meta, biases, mine, theirs, squares, prompts, moment_one, moment_two):
    block, width = prompts.shape
    tiles = 5 if block % 40 == 0 else 1
    shape = jax.ShapeDtypeStruct((block, width), F32)
    return pl.pallas_call(
        optimizer_kernel,
        out_shape=(shape,) * 4 + (jax.ShapeDtypeStruct(squares.shape, F32),),
        in_specs=[smem(), smem()] + [vmem()] * 6,
        out_specs=[hbm()] * 4 + [vmem()],
        scratch_shapes=[
            pltpu.VMEM((4, block, width), F32),
            pltpu.SemaphoreType.DMA((4, tiles)),
        ],
        compiler_params=params(prompts, prompts),
        cost_estimate=cost(20 * block * width, 32 * block * width),
        name="optimizer",
    )(meta, biases, mine, theirs, squares, prompts, moment_one, moment_two)


def per_device(
    tokens,
    cotangent,
    dataset_ids,
    prompt_map,
    attn_in,
    attn_out,
    up_weight,
    up_bias,
    down_weight,
    down_bias,
    norm_gains,
    norm_shifts,
    prompts,
    moment_one,
    moment_two,
    step_count,
):
    size, width = tokens.shape[1:]
    dim = attn_in.shape[2]
    hid = up_weight.shape[1]
    data_count = prompt_map.shape[1]
    row_count = lax.axis_size("rows")
    head_count = lax.axis_size("head")
    factor = dim ** (-0.5) * LOG2E
    row = lax.axis_index("rows")
    head = lax.axis_index("head")
    batch, parity = head // 2, head % 2
    half = size // 2
    meta = jnp.stack([row, batch, parity]).astype(jnp.int32)

    block = prompts.shape[0]

    part = half_rows(block)
    prompt_own = lax.dynamic_slice(
        prompts, (batch * (block - part), parity * (width // 2)), (part, width // 2)
    ).astype(BF)
    in_other = swap_head(attn_in, 2, head_count)
    ids = jnp.where(batch == 0, dataset_ids[0], dataset_ids[1])
    tok_half = lax.dynamic_slice(tokens, (batch, parity * half, 0), (1, half, width))[0]
    id_rows = jnp.broadcast_to(ids.astype(BF)[None, :], (PACK, size))
    shard = jnp.concatenate([tok_half, id_rows], axis=0)

    bias_high = lax.reduce_precision(up_bias, 8, 7)
    bias_rest = up_bias - bias_high
    bias_mid = lax.reduce_precision(bias_rest, 8, 7)
    bias_low = bias_rest - bias_mid
    bias_rows = jnp.concatenate([bias_high, bias_mid, bias_low, bias_low]).astype(BF)
    bias_rows = jnp.pad(bias_rows.reshape(-1, width), ((0, PACK - 4 * hid // width), (0, 0)))
    w_own = jnp.concatenate([down_weight, attn_out, up_weight.T, bias_rows], axis=0)
    in_other, w_own = lax.optimization_barrier((in_other, w_own))
    w_along = swap_head(w_own, 2, head_count)
    step_value = step_count.astype(F32)
    biases = jnp.stack(
        [1.0 - jnp.power(BETA_ONE, step_value), 1.0 - jnp.power(BETA_TWO, step_value)]
    )
    numbers = jnp.arange(data_count + 1, dtype=jnp.int32)
    local = jnp.sum((dataset_ids[:, None, :] < numbers[None, :, None]).astype(jnp.int32), axis=2)
    ids_rows = dataset_ids.astype(F32).reshape(2, 1, size)
    tied = {}

    orders, later = bit_orders(row_count), prompt_orders(row_count)
    stages = len(orders[0])
    held, prompt_held = shard[None], prompt_own[None]
    tok = lax.dynamic_index_in_dim(tokens, batch, 0, keepdims=False)
    cot = lax.dynamic_index_in_dim(cotangent, batch, 0, keepdims=False)

    def prompt_stage(place):
        other = gather_stage(prompt_held, place, later, row_count, head_count)
        return jnp.concatenate([prompt_held, other], axis=0)

    for place in range(stages):
        if place == stages - 1:
            held, in_other, meta, (biases, local, ids_rows, tok, cot) = lax.optimization_barrier(
                (held, in_other, meta, (biases, local, ids_rows, tok, cot))
            )
        if place != 1:
            held, prompt_held = lax.optimization_barrier((held, prompt_held))
        other = gather_stage(held, place, orders, row_count, head_count)
        if place != 1:
            prompt_held = prompt_stage(max(place - 1, 0))
        if place < stages - 1:
            held = jnp.concatenate([held, other], axis=0)
        if place == 0:
            held, prompt_held = lax.optimization_barrier((held, prompt_held))
    theirs_low = swap_head(held, 1, head_count)
    other, prompt_held, w_along = lax.optimization_barrier((other, prompt_held, w_along))
    mine = (held, other)
    prompt_high = gather_stage(prompt_held, stages - 1, later, row_count, head_count)
    theirs = (theirs_low, swap_head(other, 1, head_count))
    w_core = swap_head(w_own, 1, head_count)
    w_far = swap_head(w_along, 1, head_count)

    ids_all = jnp.concatenate([bank[:, half, :size] for bank in mine], axis=0).astype(F32)
    starts = jnp.sum(
        (ids_all.reshape(1, -1) < numbers.astype(F32)[:, None]).astype(jnp.int32), axis=1
    )
    ids_all = ids_all.reshape(row_count, 1, size)
    q_own, kv_own, w_q, w_kv, *state, flag = token_forward(
        meta, starts, tokens, ids_rows, mine, theirs, attn_in, in_other, factor, data_count
    )
    prompt_theirs_low = swap_head(prompt_held, 1, head_count)
    prompt_high, flag, prompt_theirs_low, w_core, w_far = lax.optimization_barrier(
        (prompt_high, flag, prompt_theirs_low, w_core, w_far)
    )
    prompt_mine = (prompt_held, prompt_high)
    prompt_theirs = (prompt_theirs_low, swap_head(prompt_high, 1, head_count))
    wide_half, lse_half, send_half = prompt_forward(
        meta,
        local,
        prompt_map,
        q_own,
        ids_rows,
        state,
        flag,
        prompt_mine,
        prompt_theirs,
        w_kv,
        factor,
        block,
    )
    prompt_low, send_half = lax.optimization_barrier((prompts.astype(BF), send_half))
    prompt_kv = jnp.dot(prompt_low, w_kv, preferred_element_type=F32).astype(BF)
    o_mine, wide_out, lse = join_halves(wide_half, lse_half, swap_head(send_half, 2, head_count))
    o_mine, prompt_kv = lax.optimization_barrier((o_mine, prompt_kv))
    o_theirs = swap_head(o_mine, 1, head_count)
    out, grad_sum, pack, delta = feed(
        meta,
        o_mine,
        o_theirs,
        wide_out,
        lse,
        tok,
        cot,
        (w_own, w_along, w_core, w_far),
        down_bias.reshape(1, width),
        norm_gains,
        norm_shifts,
    )
    pack_other = swap_head(pack, 2, head_count)

    def tie_query_grads(stages_left, held):
        if stages_left == 3:
            held, here = lax.optimization_barrier((held, w_q))
            tied["q"], tied["flag"] = project_query(mine, theirs, here)
        if stages_left == 2:
            held, other, flag = lax.optimization_barrier((held, pack_other, tied["flag"]))
            tied["dq"] = prompt_query_grad(
                meta,
                local,
                prompt_map,
                q_own,
                ids_rows,
                lse,
                delta,
                pack,
                other,
                flag,
                prompt_mine,
                prompt_theirs,
                w_kv,
                factor,
                block,
            )
        if stages_left == 1:
            acc, dq_send = tied["dq"]
            held, dq_send, ids_here = lax.optimization_barrier((held, dq_send, ids_rows))
            tied["dq_other"] = swap_head(dq_send, 2, head_count)
            tied["dq"], tied["flag"] = token_query_grad(
                meta,
                starts,
                q_own,
                ids_here,
                lse,
                delta,
                pack,
                acc,
                mine,
                theirs,
                w_kv,
                factor,
                data_count,
            )
            *tied["terms"], tied["flag"] = prompt_grad_first(
                meta,
                starts,
                prompt_map,
                tied["q"],
                ids_all,
                held,
                prompt_kv,
                tied["flag"],
                factor,
                data_count,
            )
        return held

    out_half = lax.dynamic_slice_in_dim(out, parity * half, half, 0)
    out_half = swap_head(out_half, 2, head_count)
    packs = gather_rows(pack, row_count, head_count, tie_query_grads)
    q_all = tied["q"]
    dq = tied["dq"]
    packs, dq_other, out_half = lax.optimization_barrier((packs, tied["dq_other"], out_half))
    keep, send = prompt_grad_last(
        meta,
        starts,
        prompt_map,
        q_all,
        ids_all,
        packs[1],
        prompt_kv,
        tied["terms"],
        w_kv,
        factor,
        data_count,
    )

    pair = keep + swap_head(send, 1, head_count).astype(F32)
    pair_low = lax.reduce_precision(pair, 8, 7).astype(BF)
    pair_low, ids_here = lax.optimization_barrier((pair_low, ids_rows))
    pair_other = swap_head(pair_low, 2, head_count)
    out_rest = swap_head(out_half, 1, head_count)
    token_part, flag = token_grad(
        meta,
        starts,
        q_all,
        ids_all,
        packs,
        kv_own,
        ids_here,
        (dq, dq_other),
        (w_q, w_kv),
        factor,
        data_count,
    )
    pair_other, flag = lax.optimization_barrier((pair_other, flag))
    full_low, squares = sum_prompt(pair_low, pair_other, flag)
    full_other = swap_head(full_low, 1, head_count)

    def both_batches(own, here, rest):
        other = jnp.concatenate(
            [jnp.where(parity == 0, here, rest), jnp.where(parity == 0, rest, here)], axis=0
        )
        first = jnp.where(batch == 0, own, other)
        return jnp.stack([first, jnp.where(batch == 0, other, own)]).astype(F32)

    core_sum = token_part.astype(F32) + swap_head(token_part, 1, head_count).astype(F32)
    total = lax.reduce_precision(grad_sum + core_sum, 8, 7).astype(BF)
    mine_half = lax.dynamic_slice_in_dim(total, parity * half, half, 0)
    other_half = swap_head(mine_half, 2, head_count)
    layer_out = both_batches(out, out_half, out_rest)

    def tie_sum(stages_done, value):
        if stages_done == 1:
            value, _ = lax.optimization_barrier((value, total))
        if stages_done == 2:
            value, tied["out"] = lax.optimization_barrier((value, layer_out))
        return value

    squares = xor_sum(squares, row_count, head_count, tie_sum)
    clipped, new_one, new_two, new_prompts, norm = optimizer(
        meta, biases, full_low, full_other, squares, prompts, moment_one, moment_two
    )
    other_half, norm = lax.optimization_barrier((other_half, norm))
    input_grad = both_batches(total, other_half, swap_head(other_half, 1, head_count))
    return (tied["out"], input_grad, clipped, norm[0, 0], new_one, new_two, new_prompts)


def solution(mesh):
    in_specs = (
        P(None, "rows", None),
        P(None, "rows", None),
        P(None, "rows"),
        P(),
        P(None, None, "head"),
        P("head", None),
        P(None, "head"),
        P("head"),
        P("head", None),
        P(),
        P(),
        P(),
        P("rows", None),
        P("rows", None),
        P("rows", None),
        P(),
    )
    out_specs = (
        P(None, "rows", None),
        P(None, "rows", None),
        P("rows", None),
        P(),
        P("rows", None),
        P("rows", None),
        P("rows", None),
    )
    return jax.shard_map(
        per_device, mesh=mesh, in_specs=in_specs, out_specs=out_specs, check_vma=False
    )
```

```python
import functools

import jax
import jax.numpy as jnp
from jax import lax
from jax.experimental import pallas as pl
from jax.experimental.pallas import tpu as pltpu
from jax.sharding import PartitionSpec as P

PLEN = 1000
NEGATIVE = -1e30
BETA_ONE = 0.9
BETA_TWO = 0.999
LEARNING_RATE = 0.5
DECAY_RATE = 0.01
EPSILON = 1e-08
CLIP_NORM = 1.0
LOG2E = 1.4426950408889634
PACK = 16
STATS = 32
VMEM_LIMIT = 60 * 1024 * 1024
BF = jnp.bfloat16
F32 = jnp.float32
BOTH = ("rows", "head")


def params(*operands, spare=20 << 20):
    held = sum(x.size * x.dtype.itemsize for x in operands)
    return pltpu.CompilerParams(vmem_limit_bytes=min(VMEM_LIMIT, held + spare))


def cost(flops, bytes_accessed, transcendentals=0):
    return pl.CostEstimate(
        flops=int(flops), bytes_accessed=int(bytes_accessed), transcendentals=int(transcendentals)
    )


def mm(a, b):
    return lax.dot_general(a, b, (((1,), (0,)), ((), ())), preferred_element_type=F32)


def mm_nt(a, b):
    return lax.dot_general(a, b, (((1,), (1,)), ((), ())), preferred_element_type=F32)


def split3(value):
    high = value.astype(BF)
    rest = value - high.astype(F32)
    mid = rest.astype(BF)
    low = (rest - mid.astype(F32)).astype(BF)
    return high, mid, low


def bit_orders(row_count):
    bits = row_count.bit_length() - 1
    return ([0] + list(range(bits - 1, 0, -1)), list(range(bits - 1, 0, -1)) + [0])


def prompt_orders(row_count):
    bits = row_count.bit_length() - 1
    if bits < 2:
        return bit_orders(row_count)
    high = list(range(bits - 1, 1, -1))
    return (high + [0, 1], [1] + high + [0])


def slot_of(offset, parity, orders):
    def mapped(order):
        total = 0
        for place, bit in enumerate(order):
            total = total + (((offset >> bit) & 1) << place)
        return total

    return jnp.where(parity == 0, mapped(orders[0]), mapped(orders[1]))


def gather_stage(held, place, orders, row_count, head_count):
    pairs = []
    for row in range(row_count):
        for head in range(head_count):
            bit = orders[head % 2][place]
            pairs.append((row * head_count + head, (row ^ (1 << bit)) * head_count + head))
    return lax.ppermute(held, BOTH, pairs)


def gather_rows(block, row_count, head_count, before_send):
    held = block[None]
    orders = bit_orders(row_count)
    stages = len(orders[0])
    for place in range(stages):
        held = before_send(stages - place, held)
        other = gather_stage(held, place, orders, row_count, head_count)
        if place < stages - 1:
            held = jnp.concatenate([held, other], axis=0)
    return held, other


def xor_sum(value, row_count, head_count, after):
    def moved(mask):
        count = row_count * head_count
        return lax.ppermute(value, BOTH, [(i, i ^ mask) for i in range(count)])

    masks = [1]
    bit = head_count
    while bit < row_count * head_count:
        masks.append(bit)
        bit = bit * 2
    done = 0
    while masks:
        if len(masks) == 1:
            value = value + moved(masks[0])
        else:
            first, second, both = (moved(m) for m in (masks[0], masks[1], masks[0] ^ masks[1]))
            value = (value + first) + (second + both)
        masks = masks[2:]
        done = done + 1
        value = after(done, value)
    return value


def swap_head(value, mask, head_count):
    return lax.ppermute(value, "head", [(i, i ^ mask) for i in range(head_count)])


def smem():
    return pl.BlockSpec(memory_space=pltpu.SMEM)


def vmem():
    return pl.BlockSpec(memory_space=pltpu.VMEM)


def hbm():
    return pl.BlockSpec(memory_space=pltpu.HBM)


def flag_shape():
    return jax.ShapeDtypeStruct((8, 128), F32)


def raise_flag(ref):
    ref[...] = jnp.zeros(ref.shape, F32)


def join_weights(meta, own, other, target, kinds):
    dim = own.shape[2]
    for index, kind in enumerate(kinds):
        for place in range(2):
            column = (index * 2 + place) * dim
            target[:, column : column + dim] = jnp.where(meta[1] == place, own[kind], other[kind])


def wide(value, count):
    return jnp.concatenate([value] * count, axis=1)


def line_of(columns):
    return jnp.transpose(columns)[0:1, :]


def column_of(line):
    return jnp.transpose(jnp.broadcast_to(line, (128, line.shape[1])))


def project_query_kernel(a, b, c, d, weights, q_out, flag):
    raise_flag(flag)
    half = a.shape[1] - PACK
    for high, pair in enumerate(((a, b), (c, d))):
        for place, ref in enumerate(pair):
            q_out[high, 0, place] = mm(ref[0, :half], weights[...]).astype(BF)


def project_query(mine, theirs, weights):
    slots, rows, width = mine[0].shape
    half = rows - PACK
    double = weights.shape[1]
    block = pl.BlockSpec((1, rows, width), lambda g: (g, 0, 0))
    whole = pl.BlockSpec(weights.shape, lambda g: (0, 0))
    out, flag = pl.pallas_call(
        project_query_kernel,
        out_shape=(jax.ShapeDtypeStruct((2, slots, 2, half, double), BF), flag_shape()),
        grid=(slots,),
        in_specs=[block] * 4 + [whole],
        out_specs=[
            pl.BlockSpec((2, 1, 2, half, double), lambda g: (0, g, 0, 0, 0)),
            pl.BlockSpec((8, 128), lambda g: (0, 0)),
        ],
        compiler_params=params(),
        cost_estimate=cost(8 * slots * half * width * double, 8 * slots * half * width),
        name="project_query",
    )(mine[0], theirs[0], mine[1], theirs[1], weights)
    return out.reshape(4 * slots, half, double), flag


def key_range(starts, low, high, data_count):
    first = jnp.int32(1 << 30)
    last = jnp.int32(0)
    for data in range(data_count):
        begin, end = starts[data], starts[data + 1]
        hit = (begin < high) & (end > low) & (begin < end)
        first = jnp.where(hit, jnp.minimum(first, begin), first)
        last = jnp.where(hit, jnp.maximum(last, end), last)
    return first, last


def shard_copies(meta, shard, gathered, x_ref, sem):
    slots = gathered[0].shape[0]
    copies = []
    for place in range(2):
        slot = slot_of(shard ^ meta[0], meta[2] ^ place, bit_orders(2 * slots))
        for bank in range(2):
            here = (slot < slots) if bank == 0 else (slot >= slots)
            source = gathered[place * 2 + bank]
            copy = pltpu.make_async_copy(
                source.at[jnp.where(here, slot - bank * slots, 0)],
                x_ref.at[shard, place],
                sem.at[shard, place],
            )
            copies.append((here, copy))
    return copies


def fetch_shards(meta, first, last, gathered, x_ref, sem):
    def start(shard, carry):
        for here, copy in shard_copies(meta, shard, gathered, x_ref, sem):

            @pl.when(here)
            def _():
                copy.start()

        return carry

    lax.fori_loop(first, last, start, 0)


def load_shard(meta, shard, gathered, x_ref, sem):
    half = x_ref.shape[2] - PACK
    parity = meta[2]
    for place in range(2):
        pltpu.make_async_copy(gathered[0].at[0], x_ref.at[shard, place], sem.at[shard, place]).wait()
    line = x_ref[shard, 0, half : half + 1, :].astype(F32)
    first, second = line[:, :half], line[:, half : 2 * half]
    line = jnp.concatenate(
        [jnp.where(parity == 0, first, second), jnp.where(parity == 0, second, first)], axis=1
    )
    return jnp.concatenate([x_ref[shard, 0, :half, :], x_ref[shard, 1, :half, :]], axis=0), line


def online(scores, factor, mask, m_ref, place):
    old_max = m_ref[place]
    size = old_max.shape[0]
    top = jnp.broadcast_to(jnp.max(scores, axis=1, keepdims=True) * factor, (size, 128))
    new_max = jnp.maximum(old_max, top)
    shift = new_max
    if mask is not None:
        new_max = jnp.where(mask, new_max, old_max)
        shift = jnp.where(mask, new_max, -NEGATIVE)
    m_ref[place] = new_max
    probs = jnp.exp2(scores * factor - wide(shift, scores.shape[1] // 128))
    return probs.astype(BF), jnp.exp2(old_max - new_max)


def accumulate(acc_ref, place, alpha, probs, value):
    with_ones = jnp.concatenate([value, jnp.ones((value.shape[0], 128), BF)], axis=1)
    acc_ref[place] = acc_ref[place] * wide(alpha, with_ones.shape[1] // 128) + mm(probs, with_ones)


def token_forward_kernel(
    data_count,
    factor,
    meta,
    starts,
    ids_ref,
    in_own,
    in_other,
    tok_hbm,
    mine_low,
    mine_high,
    theirs_low,
    theirs_high,
    q_ref,
    kv_own,
    wq_ref,
    wkv_ref,
    m_out,
    l_out,
    acc_out,
    flag,
    m_ref,
    acc_ref,
    x_ref,
    id_ref,
    tok_ref,
    sem,
    tok_sem,
):
    raise_flag(flag)
    size, dim = tok_ref.shape[1], in_own.shape[2]
    tok_copy = pltpu.make_async_copy(tok_hbm, tok_ref, tok_sem)
    tok_copy.start()
    base = meta[0] * size
    first, last = key_range(starts, base, base + size, data_count)
    first, last = first // size, (last + size - 1) // size
    gathered = (mine_low, mine_high, theirs_low, theirs_high)
    fetch_shards(meta, first, last, gathered, x_ref, sem)
    join_weights(meta, in_own, in_other, wq_ref, (0,))
    join_weights(meta, in_own, in_other, wkv_ref, (1, 2))
    tok_copy.wait()
    for slot in range(2):
        q_ref[slot] = mm(tok_ref[meta[1] ^ slot], wq_ref[...]).astype(BF)
    kv_own[...] = mm(tok_ref[meta[1]], wkv_ref[...]).astype(BF)
    m_ref[...] = jnp.full(m_ref.shape, NEGATIVE, F32)
    acc_ref[...] = jnp.zeros(acc_ref.shape, F32)
    id_ref[...] = column_of(ids_ref[meta[1]])
    rows = pl.ds(0, size)

    def step(shard, carry):
        raw_rows, line = load_shard(meta, shard, gathered, x_ref, sem)
        kv = mm(raw_rows, wkv_ref[...]).astype(BF)
        mask = wide(id_ref[...], size // 128) == line
        raw = [
            mm_nt(q_ref[0, :, h * dim : (h + 1) * dim], kv[:, h * dim : (h + 1) * dim])
            for h in range(2)
        ]
        parts = [
            online(jnp.where(mask, raw[h], NEGATIVE), factor, None, m_ref, (h, rows))
            for h in range(2)
        ]
        for h in range(2):
            value = kv[:, (2 + h) * dim : (3 + h) * dim]
            accumulate(acc_ref, (h, rows), parts[h][1], parts[h][0], value)
        return carry

    lax.fori_loop(first, last, step, 0)
    for h in range(2):
        m_out[h : h + 1, :] = line_of(m_ref[h])
        l_out[h : h + 1, :] = line_of(acc_ref[h, :, dim:])
        acc_out[h] = acc_ref[h, :, :dim]


def shard_scratch(banks):
    slots, rows, width = banks[0].shape
    return pltpu.VMEM((2 * slots, 2, rows, width), BF)


def token_forward(meta, starts, tokens, ids_rows, mine, theirs, in_own, in_other, factor, data_count):
    size, width = tokens.shape[1:]
    dim = in_own.shape[2]
    return pl.pallas_call(
        functools.partial(token_forward_kernel, data_count, factor),
        out_shape=(
            jax.ShapeDtypeStruct((2, size, 2 * dim), BF),
            jax.ShapeDtypeStruct((size, 4 * dim), BF),
            jax.ShapeDtypeStruct((width, 2 * dim), BF),
            jax.ShapeDtypeStruct((width, 4 * dim), BF),
            jax.ShapeDtypeStruct((2, size), F32),
            jax.ShapeDtypeStruct((2, size), F32),
            jax.ShapeDtypeStruct((2, size, dim), F32),
            flag_shape(),
        ),
        in_specs=[smem(), smem()] + [vmem()] * 3 + [hbm()] * 5,
        out_specs=[vmem()] * 8,
        scratch_shapes=[
            pltpu.VMEM((2, size, 128), F32),
            pltpu.VMEM((2, size, dim + 128), F32),
            shard_scratch(mine),
            pltpu.VMEM((size, 128), F32),
            pltpu.VMEM(tokens.shape, BF),
            pltpu.SemaphoreType.DMA((2 * mine[0].shape[0], 2)),
            pltpu.SemaphoreType.DMA,
        ],
        compiler_params=params(spare=VMEM_LIMIT),
        cost_estimate=cost(8e9, 8e6, 2e6),
        name="token_forward",
    )(meta, starts, ids_rows, in_own, in_other, tokens, *mine, *theirs)


def half_rows(block):
    return -(-block // 32) * 16


def fetch_prompts(meta, local, table, sources, raws, state, sem):
    pieces = raws.shape[2]
    slots = sources[0].shape[0]
    for number in range(state.shape[0]):
        state[number] = 0
    for batch in range(2):
        for data in range(table.shape[1]):
            number = table[batch, data]
            used = local[batch, data + 1] > local[batch, data]
            state[number] = jnp.where(used, 1, state[number])

    def start(number, carry):
        @pl.when(state[number] == 1)
        def _():
            for piece in range(pieces):
                for place in range(2):
                    shard = number * pieces + piece
                    slot = slot_of(shard ^ meta[0], meta[2] ^ place, prompt_orders(2 * slots))
                    for bank in range(2):

                        @pl.when((slot < slots) if bank == 0 else (slot >= slots))
                        def _():
                            pltpu.make_async_copy(
                                sources[place * 2 + bank].at[slot - bank * slots],
                                raws.at[place, number, piece],
                                sem.at[place, number, piece],
                            ).start()

        return carry

    lax.fori_loop(0, state.shape[0], start, 0)


def project_prompt(meta, number, sources, raws, w_ref, kv_ref, state, sem):
    pieces, block = raws.shape[2:4]

    @pl.when(state[number] == 1)
    def _():
        even = meta[2] == 0
        for piece in range(pieces):
            for place in range(2):
                pltpu.make_async_copy(
                    sources[0].at[0], raws.at[place, number, piece], sem.at[place, number, piece]
                ).wait()
            a, b = raws[0, number, piece], raws[1, number, piece]
            rows = jnp.concatenate([jnp.where(even, a, b), jnp.where(even, b, a)], axis=1)
            kv_ref[number, pl.ds(piece * block, block), :] = mm(rows, w_ref[...]).astype(BF)
        full = pieces * block
        if full < kv_ref.shape[1]:
            kv_ref[number, full:, :] = jnp.zeros((kv_ref.shape[1] - full, kv_ref.shape[2]), BF)
        state[number] = 2


def prompt_mask(meta, scores, block):
    part = half_rows(block)
    pieces = PLEN // block
    doubled = 2 * part - block
    head = min(128, part) if pieces == 1 else scores.shape[1]
    lanes = lax.broadcasted_iota(jnp.int32, (scores.shape[0], head), 1)
    out = (lanes % part < doubled * meta[1]) | (lanes >= pieces * part)
    first = jnp.where(out, NEGATIVE, scores[:, :head])
    if head == scores.shape[1]:
        return first
    return jnp.concatenate([first, scores[:, head:]], axis=1)


def visit_prompts(meta, local, table, size, prepare, update):
    data_count = table.shape[1]

    def visit(index, carry):
        slot, data = index // data_count, index % data_count
        batch = meta[1] ^ slot
        begin, end = local[batch, data], local[batch, data + 1]

        @pl.when(begin < end)
        def _():
            number = table[batch, data]
            prepare(number)
            low = begin // 128
            count = (end + 127) // 128 - low
            for case in range(1, size // 128 + 1):

                @pl.when(count == case)
                def _():
                    rows = pl.ds(pl.multiple_of(low * 128, 128), case * 128)
                    update(slot, rows, data, number)

        return carry

    lax.fori_loop(0, 2 * data_count, visit, 0)


def store_line(ref, row, line):
    width = ref.shape[1]
    for term in split3(line):
        for low in range(0, line.shape[1], width):
            ref[row : row + 1, :] = term[:, low : low + width]
            row = row + 1
    return row


def load_line(ref, row, length):
    width = ref.shape[1]
    rows_per = length // width
    total = 0.0
    for place in range(3):
        first = row + place * rows_per
        pieces = [ref[first + i : first + i + 1, :].astype(F32) for i in range(rows_per)]
        total = total + jnp.concatenate(pieces, axis=1)
    return total


def prompt_forward_kernel(
    block,
    factor,
    meta,
    local,
    table,
    q_ref,
    ids_ref,
    m_in,
    l_in,
    acc_in,
    _,
    w_ref,
    mine_low,
    mine_high,
    theirs_low,
    theirs_high,
    wide_ref,
    lse_ref,
    send_ref,
    m_ref,
    acc_ref,
    raws,
    kv_ref,
    id_ref,
    state,
    sem,
):
    size, dim = q_ref.shape[1], q_ref.shape[2] // 2
    sources = (mine_low, mine_high, theirs_low, theirs_high)
    fetch_prompts(meta, local, table, sources, raws, state, sem)
    for h in range(2):
        m_ref[0, h] = column_of(m_in[h : h + 1, :])
        acc_ref[0, h, :, dim:] = column_of(l_in[h : h + 1, :])
        acc_ref[0, h, :, :dim] = acc_in[h]
    m_ref[1] = jnp.full(m_ref.shape[1:], NEGATIVE, F32)
    acc_ref[1] = jnp.zeros(acc_ref.shape[1:], F32)
    for slot in range(2):
        id_ref[slot] = column_of(ids_ref[meta[1] ^ slot])

    def prepare(number):
        project_prompt(meta, number, sources, raws, w_ref, kv_ref, state, sem)

    def update(slot, rows, data, number):
        mask = id_ref[slot, rows, :] == data.astype(F32)
        raw = [
            mm_nt(q_ref[slot, rows, pl.ds(h * dim, dim)], kv_ref[number, :, pl.ds(h * dim, dim)])
            for h in range(2)
        ]
        parts = [
            online(prompt_mask(meta, raw[h], block), factor, mask, m_ref, (slot, h, rows))
            for h in range(2)
        ]
        for h in range(2):
            value = kv_ref[number, :, pl.ds((2 + h) * dim, dim)]
            accumulate(acc_ref, (slot, h, rows), parts[h][1], parts[h][0], value)

    visit_prompts(meta, local, table, size, prepare, update)
    row = size
    send_ref[pl.ds(size, PACK), :] = jnp.zeros((PACK, 2 * dim), BF)
    for h in range(2):
        cols = pl.ds(h * dim, dim)
        total = acc_ref[0, h, :, dim:]
        wide_ref[:, cols] = acc_ref[0, h, :, :dim] / total
        lse_ref[h : h + 1, :] = line_of(m_ref[0, h] + jnp.log2(total))
        total = acc_ref[1, h, :, dim:]
        send_ref[pl.ds(0, size), cols] = (acc_ref[1, h, :, :dim] / total).astype(BF)
        line = line_of(m_ref[1, h] + jnp.log2(total))
        row = store_line(send_ref, row, line)


def prompt_scratch(prompt_banks, dim, block):
    slots, part, columns = prompt_banks[0].shape
    pieces = PLEN // block
    count = 2 * slots // pieces
    return [
        pltpu.VMEM((2, count, pieces, part, columns), BF),
        pltpu.VMEM((count, -(-pieces * part // 128) * 128, 4 * dim), BF),
    ], [pltpu.SMEM((count,), jnp.int32), pltpu.SemaphoreType.DMA((2, count, pieces))]


def prompt_forward(
    meta, local, table, q_own, ids_rows, state, flag, prompt_mine, prompt_theirs, weights, factor, block
):
    size, dim = q_own.shape[1], q_own.shape[2] // 2
    buffers, flags = prompt_scratch(prompt_mine, dim, block)
    return pl.pallas_call(
        functools.partial(prompt_forward_kernel, block, factor),
        out_shape=(
            jax.ShapeDtypeStruct((size, 2 * dim), F32),
            jax.ShapeDtypeStruct((2, size), F32),
            jax.ShapeDtypeStruct((size + PACK, 2 * dim), BF),
        ),
        in_specs=[smem()] * 3 + [vmem()] * 7 + [hbm()] * 4,
        out_specs=[vmem()] * 3,
        scratch_shapes=[
            pltpu.VMEM((2, 2, size, 128), F32),
            pltpu.VMEM((2, 2, size, dim + 128), F32),
            *buffers,
            pltpu.VMEM((2, size, 128), F32),
            *flags,
        ],
        compiler_params=params(*prompt_mine, *prompt_mine, *prompt_mine),
        cost_estimate=cost(4e9, 8e6, 2e6),
        name="prompt_forward",
    )(meta, local, table, q_own, ids_rows, *state, flag, weights, *prompt_mine, *prompt_theirs)


def join_kernel(wide_in, lse_in, other_ref, o_ref, wide_ref, lse_ref):
    size, dim = wide_in.shape[0], wide_in.shape[1] // 2
    rows_per = size // (2 * dim)
    for h in range(2):
        cols = pl.ds(h * dim, dim)
        first = column_of(lse_in[h : h + 1, :])
        second = column_of(load_line(other_ref, size + h * 3 * rows_per, size))
        top = jnp.maximum(first, second)
        first, second = jnp.exp2(first - top), jnp.exp2(second - top)
        total = first + second
        other = other_ref[pl.ds(0, size), cols].astype(F32)
        attended = (first * wide_in[:, cols] + second * other) / total
        wide_ref[:, cols] = attended
        o_ref[:, cols] = attended.astype(BF)
        lse_ref[h : h + 1, :] = line_of(top + jnp.log2(total))


def join_halves(wide_half, lse_half, other):
    return pl.pallas_call(
        join_kernel,
        out_shape=(
            jax.ShapeDtypeStruct(wide_half.shape, BF),
            jax.ShapeDtypeStruct(wide_half.shape, F32),
            jax.ShapeDtypeStruct(lse_half.shape, F32),
        ),
        in_specs=[vmem()] * 3,
        out_specs=[vmem()] * 3,
        compiler_params=params(),
        cost_estimate=cost(4e6, 3e6, 1e6),
        name="join_halves",
    )(wide_half, lse_half, other)


def norm_parts(value):
    center = value - jnp.mean(value, axis=-1, keepdims=True)
    scale = lax.rsqrt(jnp.mean(center * center, axis=-1, keepdims=True) + 1e-05)
    return center * scale, scale


def norm_back(grad, unit, scale, gain):
    part = grad * gain
    return scale * (
        part
        - jnp.mean(part, axis=-1, keepdims=True)
        - unit * jnp.mean(part * unit, axis=-1, keepdims=True)
    )


def feed_kernel(
    meta,
    mine,
    theirs,
    wide_ref,
    lse_ref,
    tok_ref,
    cot_ref,
    down_bias,
    gains,
    shifts,
    w_own,
    w_along,
    w_core,
    w_far,
    out_ref,
    da_ref,
    pack_ref,
    delta_ref,
    w_ref,
    sem,
):
    size, width = tok_ref.shape
    dim = mine.shape[1] // 2
    heads = w_ref.shape[0]
    hid = (w_ref.shape[1] - PACK - dim) // 2
    batch, parity = meta[1], meta[2]
    even = parity == 0
    cuts = (pl.ds(hid, dim), pl.ds(hid + dim, hid + PACK), pl.ds(0, hid))

    def arrived(part):
        for q in range(heads):
            pltpu.make_async_copy(
                w_own.at[cuts[part]], w_ref.at[q, cuts[part]], sem.at[q, part]
            ).wait()

    for q in range(heads):
        for place, ref in enumerate((w_own, w_along, w_core, w_far)):

            @pl.when((2 * batch + parity) == (q ^ (0, 2, 1, 3)[place]))
            def _():
                for part, rows in enumerate(cuts):
                    pltpu.make_async_copy(
                        ref.at[rows], w_ref.at[q, rows], sem.at[q, part]
                    ).start()

    place_out = slice(hid, hid + dim)
    place_up = slice(hid + dim, 2 * hid + dim)
    place_bias = 2 * hid + dim
    sub = size
    pack_ref[pl.ds(size, STATS), :] = jnp.zeros((STATS, 2 * dim), BF)
    g0, g1 = gains[0:1, :], gains[1:2, :]
    for part in range(size // sub):
        rows = pl.ds(part * sub, sub)
        a, b = mine[rows, :], theirs[rows, :]
        if part == 0:
            arrived(0)
        first = jnp.where(even, a, b)
        second = jnp.where(even, b, a)
        attn = mm(first, jnp.concatenate([w_ref[0, place_out, :], w_ref[2, place_out, :]], axis=0))
        attn += mm(second, jnp.concatenate([w_ref[1, place_out, :], w_ref[3, place_out, :]], axis=0))
        unit_one, scale_one = norm_parts(tok_ref[rows, :].astype(F32) + attn)
        normed = unit_one * g0 + shifts[0:1, :]
        normed_low = normed.astype(BF)
        branch = down_bias[...]
        slopes = []
        if part == 0:
            arrived(1)
            arrived(2)
        for q in range(heads):
            bias = (
                w_ref[q, place_bias : place_bias + 1, :hid].astype(F32)
                + w_ref[q, place_bias : place_bias + 1, hid : 2 * hid].astype(F32)
                + w_ref[q, place_bias + 1 : place_bias + 2, :hid].astype(F32)
            )
            pre = mm_nt(normed_low, w_ref[q, place_up, :]) + bias
            cdf = 0.5 * (1.0 + lax.erf(pre * 0.7071067811865476))
            slopes.append(cdf + pre * (jnp.exp(-0.5 * pre * pre) * 0.3989422804014327))
            branch = branch + mm((pre * cdf).astype(BF), w_ref[q, :hid, :])
        unit_two, scale_two = norm_parts(normed + branch)
        out_ref[rows, :] = (unit_two * g1 + shifts[1:2, :]).astype(BF)
        grad_mixed = norm_back(cot_ref[rows, :].astype(F32), unit_two, scale_two, g1)
        mixed_low = grad_mixed.astype(BF)
        grad_normed = grad_mixed
        for q in range(heads):
            grad_pre = mm_nt(mixed_low, w_ref[q, :hid, :]) * slopes[q]
            grad_normed = grad_normed + mm(grad_pre.astype(BF), w_ref[q, place_up, :])
        grad_sum = norm_back(grad_normed, unit_one, scale_one, g0)
        da_ref[rows, :] = grad_sum
        sum_low = grad_sum.astype(BF)
        own = [w_ref[2 * head + parity, place_out, :] for head in range(2)]
        grads_out = mm_nt(sum_low, jnp.concatenate(own, axis=0)).astype(BF)
        for head in range(2):
            cols = pl.ds(head * dim, dim)
            grad_out = grads_out[:, head * dim : (head + 1) * dim]
            pack_ref[rows, cols] = grad_out
            delta = jnp.sum(grad_out.astype(F32) * wide_ref[rows, cols], axis=1, keepdims=True)
            delta_ref[head : head + 1, rows] = line_of(jnp.broadcast_to(delta, (sub, 128)))
    row = size
    for head in range(2):
        for ref in (lse_ref, delta_ref):
            row = store_line(pack_ref, row, ref[head : head + 1, :])


def feed(meta, mine, theirs, wide_out, lse, tokens, cotangent, w, down_bias, gains, shifts):
    size, width = tokens.shape
    dim = mine.shape[1] // 2
    return pl.pallas_call(
        feed_kernel,
        out_shape=(
            jax.ShapeDtypeStruct((size, width), BF),
            jax.ShapeDtypeStruct((size, width), F32),
            jax.ShapeDtypeStruct((size + STATS, 2 * dim), BF),
            jax.ShapeDtypeStruct((2, size), F32),
        ),
        in_specs=[smem()] + [vmem()] * 9 + [hbm()] * 4,
        out_specs=[vmem()] * 4,
        scratch_shapes=[pltpu.VMEM((4,) + w[0].shape, BF), pltpu.SemaphoreType.DMA((4, 3))],
        compiler_params=params(),
        cost_estimate=cost(3e9, 8e6, 1e6),
        name="feed",
    )(meta, mine, theirs, wide_out, lse, tokens, cotangent, down_bias, gains, shifts, *w)


def low_grads(scores, factor, shift, grads, delta):
    count = scores.shape[1] // 128
    probs = jnp.exp2(scores * factor - wide(shift, count))
    return (probs * (grads - wide(delta, count))).astype(BF)


def token_query_grad_kernel(
    data_count,
    factor,
    meta,
    starts,
    q_ref,
    ids_ref,
    lse_ref,
    delta_ref,
    do_ref,
    acc_in,
    w_ref,
    mine_low,
    mine_high,
    theirs_low,
    theirs_high,
    dq_ref,
    flag,
    acc_ref,
    x_ref,
    id_ref,
    lse_cols,
    delta_cols,
    sem,
):
    raise_flag(flag)
    size, dim = q_ref.shape[1], q_ref.shape[2] // 2
    base = meta[0] * size
    first, last = key_range(starts, base, base + size, data_count)
    first, last = first // size, (last + size - 1) // size
    gathered = (mine_low, mine_high, theirs_low, theirs_high)
    fetch_shards(meta, first, last, gathered, x_ref, sem)
    for h in range(2):
        lse_cols[h] = column_of(lse_ref[h : h + 1, :])
        delta_cols[h] = column_of(delta_ref[h : h + 1, :])
    acc_ref[...] = acc_in[...]
    id_ref[...] = column_of(ids_ref[meta[1]])

    def step(shard, carry):
        raw_rows, line = load_shard(meta, shard, gathered, x_ref, sem)
        kv = mm(raw_rows, w_ref[...]).astype(BF)
        mask = wide(id_ref[...], size // 128) == line
        raw, grads, low = [], [], []
        for h in range(2):
            raw.append(mm_nt(q_ref[0, :, h * dim : (h + 1) * dim], kv[:, h * dim : (h + 1) * dim]))
            grads.append(
                mm_nt(
                    do_ref[pl.ds(0, size), h * dim : (h + 1) * dim],
                    kv[:, (2 + h) * dim : (3 + h) * dim],
                )
            )
        for h in range(2):
            scores = jnp.where(mask, raw[h], NEGATIVE)
            low.append(low_grads(scores, factor, lse_cols[h], grads[h], delta_cols[h]))
        for h in range(2):
            acc_ref[h] += mm(low[h], kv[:, h * dim : (h + 1) * dim])
        return carry

    lax.fori_loop(first, last, step, 0)
    for h in range(2):
        dq_ref[:, pl.ds(h * dim, dim)] = acc_ref[h] * dim ** (-0.5)


def token_query_grad(
    meta, starts, q_own, ids_rows, lse, delta, pack, acc, mine, theirs, weights, factor, data_count
):
    size, dim = q_own.shape[1], q_own.shape[2] // 2
    return pl.pallas_call(
        functools.partial(token_query_grad_kernel, data_count, factor),
        out_shape=(jax.ShapeDtypeStruct((size, 2 * dim), F32), flag_shape()),
        in_specs=[smem()] * 2 + [vmem()] * 7 + [hbm()] * 4,
        out_specs=[vmem()] * 2,
        scratch_shapes=[
            pltpu.VMEM((2, size, dim), F32),
            shard_scratch(mine),
            pltpu.VMEM((size, 128), F32),
            pltpu.VMEM((2, size, 128), F32),
            pltpu.VMEM((2, size, 128), F32),
            pltpu.SemaphoreType.DMA((2 * mine[0].shape[0], 2)),
        ],
        compiler_params=params(*mine, *theirs),
        cost_estimate=cost(6e9, 16e6, 4e6),
        name="token_query_grad",
    )(
        meta,
        starts,
        q_own,
        ids_rows,
        lse,
        delta,
        pack,
        acc,
        weights,
        *mine,
        *theirs,
    )


def prompt_query_grad_kernel(
    block,
    factor,
    meta,
    local,
    table,
    q_ref,
    ids_ref,
    lse_in,
    delta_in,
    pack_own,
    pack_other,
    _,
    w_ref,
    mine_low,
    mine_high,
    theirs_low,
    theirs_high,
    dq_ref,
    send_ref,
    acc_ref,
    lse_ref,
    delta_ref,
    do_ref,
    raws,
    kv_ref,
    id_ref,
    state,
    sem,
):
    size, dim = q_ref.shape[1], q_ref.shape[2] // 2
    rows_per = size // (2 * dim)
    sources = (mine_low, mine_high, theirs_low, theirs_high)
    fetch_prompts(meta, local, table, sources, raws, state, sem)
    acc_ref[...] = jnp.zeros(acc_ref.shape, F32)
    for h in range(2):
        lse_ref[0, h] = column_of(lse_in[h : h + 1, :])
        delta_ref[0, h] = column_of(delta_in[h : h + 1, :])
    do_ref[0] = pack_own[pl.ds(0, size), :]
    do_ref[1] = pack_other[pl.ds(0, size), :]
    for h in range(2):
        for kind, ref in enumerate((lse_ref, delta_ref)):
            row = size + (h * 2 + kind) * 3 * rows_per
            ref[1, h] = column_of(load_line(pack_other, row, size))
    for slot in range(2):
        id_ref[slot] = column_of(ids_ref[meta[1] ^ slot])

    def prepare(number):
        project_prompt(meta, number, sources, raws, w_ref, kv_ref, state, sem)

    def update(slot, rows, data, number):
        mask = id_ref[slot, rows, :] == data.astype(F32)
        raw, grads, low = [], [], []
        for h in range(2):
            cols = pl.ds(h * dim, dim)
            raw.append(mm_nt(q_ref[slot, rows, cols], kv_ref[number, :, cols]))
            value = kv_ref[number, :, pl.ds((2 + h) * dim, dim)]
            grads.append(mm_nt(do_ref[slot, rows, cols], value))
        for h in range(2):
            shift = jnp.where(mask, lse_ref[slot, h, rows, :], -NEGATIVE)
            scores = prompt_mask(meta, raw[h], block)
            low.append(low_grads(scores, factor, shift, grads[h], delta_ref[slot, h, rows, :]))
        for h in range(2):
            acc_ref[slot, h, rows, :] += mm(low[h], kv_ref[number, :, pl.ds(h * dim, dim)])

    visit_prompts(meta, local, table, size, prepare, update)
    for h in range(2):
        cols = pl.ds(h * dim, dim)
        dq_ref[h] = acc_ref[0, h]
        send_ref[:, cols] = (acc_ref[1, h] * dim ** (-0.5)).astype(BF)


def prompt_query_grad(
    meta,
    local,
    table,
    q_own,
    ids_rows,
    lse,
    delta,
    pack,
    pack_other,
    flag,
    prompt_mine,
    prompt_theirs,
    weights,
    factor,
    block,
):
    size, dim = q_own.shape[1], q_own.shape[2] // 2
    buffers, flags = prompt_scratch(prompt_mine, dim, block)
    return pl.pallas_call(
        functools.partial(prompt_query_grad_kernel, block, factor),
        out_shape=(
            jax.ShapeDtypeStruct((2, size, dim), F32),
            jax.ShapeDtypeStruct((size, 2 * dim), BF),
        ),
        in_specs=[smem()] * 3 + [vmem()] * 8 + [hbm()] * 4,
        out_specs=[vmem()] * 2,
        scratch_shapes=[
            pltpu.VMEM((2, 2, size, dim), F32),
            pltpu.VMEM((2, 2, size, 128), F32),
            pltpu.VMEM((2, 2, size, 128), F32),
            pltpu.VMEM((2, size, 2 * dim), BF),
            *buffers,
            pltpu.VMEM((2, size, 128), F32),
            *flags,
        ],
        compiler_params=params(*prompt_mine, *prompt_mine, *prompt_mine, *prompt_mine),
        cost_estimate=cost(6e9, 16e6, 4e6),
        name="prompt_query_grad",
    )(
        meta,
        local,
        table,
        q_own,
        ids_rows,
        lse,
        delta,
        pack,
        pack_other,
        flag,
        weights,
        *prompt_mine,
        *prompt_theirs,
    )


def in_bank(meta, index, bank, slots):
    slot = slot_of((index // 2) ^ meta[0], meta[2], bit_orders(2 * slots))
    return (slot < slots) if bank == 0 else (slot >= slots)


def half_shard(meta, index, q_ref, ids_ref, low_ref, high_ref):
    slots, rows, double = (high_ref if low_ref is None else low_ref).shape
    half = q_ref.shape[1]
    size = rows - STATS
    shard, part = index // 2, index % 2
    slot = slot_of(shard ^ meta[0], meta[2], bit_orders(2 * slots))
    other = slot_of(shard ^ meta[0], 1 - meta[2], bit_orders(2 * slots))
    query = q_ref[jnp.where(part == meta[2], slot * 2, other * 2 + 1)]
    in_low = slot < slots
    place_low, place_high = jnp.minimum(slot, slots - 1), jnp.maximum(slot - slots, 0)
    span = pl.ds(pl.multiple_of(part * half, half), half)
    tail = pl.ds(size, STATS)

    def take(rows):
        if high_ref is None:
            return low_ref[place_low, rows, :]
        if low_ref is None:
            return high_ref[place_high, rows, :]
        return jnp.where(in_low, low_ref[place_low, rows, :], high_ref[place_high, rows, :])

    grad = take(span)
    line = ids_ref[slot]
    line = jnp.where(part == 0, line[:, :half], line[:, half : 2 * half])
    stats = take(tail).astype(F32)
    rows_per = size // double

    def stat(head, kind):
        total = 0.0
        for place in range(3):
            row = ((head * 2 + kind) * 3 + place) * rows_per
            term = stats[row : row + 1, :]
            for i in range(1, rows_per):
                term = jnp.where(part == i, stats[row + i : row + i + 1, :], term)
            total = total + term
        return total

    return query, grad, line, stat


def key_update(query, grad, kv_ref, mask, rows_mask, stat, factor, dk_ref, dv_ref):
    dim = query.shape[1] // 2
    cols = [slice(h * dim, (h + 1) * dim) for h in range(2)]
    raw = [mm_nt(kv_ref[:, cols[h]], query[:, cols[h]]) for h in range(2)]
    grads = [mm_nt(kv_ref[:, pl.ds((2 + h) * dim, dim)], grad[:, cols[h]]) for h in range(2)]
    probs, low = [], []
    for h in range(2):
        shift = stat(h, 0)
        scores = raw[h]
        if rows_mask is None:
            shift = jnp.where(mask, shift, -NEGATIVE)
        else:
            scores = jnp.where(rows_mask, scores, NEGATIVE)
        p = jnp.exp2(scores * factor - shift)
        probs.append(p.astype(BF))
        low.append((p * (grads[h] - stat(h, 1))).astype(BF))
    for h in range(2):
        dv_ref[:, cols[h]] += mm(probs[h], grad[:, cols[h]])
        dk_ref[:, cols[h]] += mm(low[h], query[:, cols[h]])


def prompt_terms(data_count, factor, bank, meta, starts, table, q_ref, ids_ref, pack_ref, kv_ref, dk_ref, dv_ref):
    half = q_ref.shape[1]
    number = meta[0] * kv_ref.shape[0] // PLEN
    low_ref, high_ref = (pack_ref, None) if bank == 0 else (None, pack_ref)

    def visit(data, carry):
        begin, end = starts[data], starts[data + 1]

        @pl.when((table[meta[1], data] == number) & (begin < end))
        def _():
            def step(index, inner):
                @pl.when(in_bank(meta, index, bank, pack_ref.shape[0]))
                def _():
                    query, grad, line, stat = half_shard(
                        meta, index, q_ref, ids_ref, low_ref, high_ref
                    )
                    mask = line == data.astype(F32)
                    key_update(query, grad, kv_ref, mask, None, stat, factor, dk_ref, dv_ref)

                return inner

            lax.fori_loop(begin // half, (end + half - 1) // half, step, 0)

        return carry

    lax.fori_loop(0, data_count, visit, 0)


def prompt_grad_first_kernel(
    data_count,
    factor,
    meta,
    starts,
    table,
    q_ref,
    ids_ref,
    pack_ref,
    kv_ref,
    _,
    dk_ref,
    dv_ref,
    flag,
):
    raise_flag(flag)
    dk_ref[...] = jnp.zeros(dk_ref.shape, F32)
    dv_ref[...] = jnp.zeros(dv_ref.shape, F32)
    prompt_terms(
        data_count, factor, 0, meta, starts, table, q_ref, ids_ref, pack_ref, kv_ref, dk_ref, dv_ref
    )


def prompt_grad_last_kernel(
    data_count,
    factor,
    meta,
    starts,
    table,
    q_ref,
    ids_ref,
    pack_ref,
    kv_ref,
    dk_in,
    dv_in,
    w_ref,
    keep_ref,
    send_ref,
    dk_ref,
    dv_ref,
):
    width = w_ref.shape[0]
    dim = kv_ref.shape[1] // 4
    dk_ref[...] = dk_in[...]
    dv_ref[...] = dv_in[...]
    prompt_terms(
        data_count, factor, 1, meta, starts, table, q_ref, ids_ref, pack_ref, kv_ref, dk_ref, dv_ref
    )
    grads = jnp.concatenate(
        [(dk_ref[...] * dim ** (-0.5)).astype(BF), dv_ref[...].astype(BF)], axis=1
    )
    split = width // 2
    parity = meta[2]
    send = w_ref[pl.ds(pl.multiple_of((1 - parity) * split, split), split), :]
    keep = w_ref[pl.ds(pl.multiple_of(parity * split, split), split), :]
    send_ref[...] = mm_nt(grads, send).astype(BF)
    keep_ref[...] = mm_nt(grads, keep)


def prompt_grad_first(meta, starts, table, q_all, ids_all, pack, kv, flag, factor, data_count):
    block, dim = kv.shape[0], kv.shape[1] // 4
    shape = jax.ShapeDtypeStruct((block, 2 * dim), F32)
    return pl.pallas_call(
        functools.partial(prompt_grad_first_kernel, data_count, factor),
        out_shape=(shape, shape, flag_shape()),
        in_specs=[smem()] * 3 + [vmem()] * 5,
        out_specs=[vmem()] * 3,
        compiler_params=params(q_all, pack),
        cost_estimate=cost(6e9, 16e6, 4e6),
        name="prompt_grad_first",
    )(meta, starts, table, q_all, ids_all, pack, kv, flag)


def prompt_grad_last(meta, starts, table, q_all, ids_all, pack, kv, terms, weights, factor, data_count):
    block, width = kv.shape[0], weights.shape[0]
    dim = kv.shape[1] // 4
    return pl.pallas_call(
        functools.partial(prompt_grad_last_kernel, data_count, factor),
        out_shape=(
            jax.ShapeDtypeStruct((block, width // 2), F32),
            jax.ShapeDtypeStruct((block, width // 2), BF),
        ),
        in_specs=[smem()] * 3 + [vmem()] * 7,
        out_specs=[vmem(), vmem()],
        scratch_shapes=[
            pltpu.VMEM((block, 2 * dim), F32),
            pltpu.VMEM((block, 2 * dim), F32),
        ],
        compiler_params=params(q_all, pack),
        cost_estimate=cost(6e9, 16e6, 4e6),
        name="prompt_grad_last",
    )(meta, starts, table, q_all, ids_all, pack, kv, *terms, weights)


def token_grad_kernel(
    data_count,
    factor,
    meta,
    starts,
    q_ref,
    ids_ref,
    low_ref,
    high_ref,
    kv_ref,
    own_ids,
    dq_ref,
    dq_other,
    wq_ref,
    wkv_ref,
    out_ref,
    flag,
    dk_ref,
    dv_ref,
    id_ref,
):
    raise_flag(flag)
    size = kv_ref.shape[0]
    half = q_ref.shape[1]
    dim = kv_ref.shape[1] // 4
    base = meta[0] * size
    first, last = key_range(starts, base, base + size, data_count)
    dk_ref[...] = jnp.zeros(dk_ref.shape, F32)
    dv_ref[...] = jnp.zeros(dv_ref.shape, F32)
    id_ref[...] = column_of(own_ids[meta[1]])

    def step(index, carry):
        query, grad, line, stat = half_shard(meta, index, q_ref, ids_ref, low_ref, high_ref)
        mask = wide(id_ref[...], half // 128) == line
        key_update(query, grad, kv_ref, None, mask, stat, factor, dk_ref, dv_ref)
        return carry

    lax.fori_loop(first // half, (last + half - 1) // half, step, 0)
    dq = (dq_ref[...] + dq_other[...].astype(F32)).astype(BF)
    grads = jnp.concatenate(
        [(dk_ref[...] * dim ** (-0.5)).astype(BF), dv_ref[...].astype(BF)], axis=1
    )
    out_ref[...] = (mm_nt(dq, wq_ref[...]) + mm_nt(grads, wkv_ref[...])).astype(BF)


def token_grad(
    meta, starts, q_all, ids_all, packs, kv_own, ids_rows, dq, weights, factor, data_count
):
    size, dim = kv_own.shape[0], kv_own.shape[1] // 4
    width = weights[0].shape[0]
    return pl.pallas_call(
        functools.partial(token_grad_kernel, data_count, factor),
        out_shape=(jax.ShapeDtypeStruct((size, width), BF), flag_shape()),
        in_specs=[smem()] * 2 + [vmem()] * 10,
        out_specs=[vmem()] * 2,
        scratch_shapes=[
            pltpu.VMEM((size, 2 * dim), F32),
            pltpu.VMEM((size, 2 * dim), F32),
            pltpu.VMEM((size, 128), F32),
        ],
        compiler_params=params(spare=VMEM_LIMIT),
        cost_estimate=cost(4e9, 16e6, 4e6),
        name="token_grad",
    )(meta, starts, q_all, ids_all, *packs, kv_own, ids_rows, *dq, *weights)


def sum_prompt_kernel(a_ref, b_ref, _, sum_ref, square_ref):
    low = (a_ref[...].astype(F32) + b_ref[...].astype(F32)).astype(BF)
    sum_ref[...] = low
    value = low.astype(F32)
    square_ref[...] = jnp.broadcast_to(jnp.sum(value * value, keepdims=True), square_ref.shape)


def sum_prompt(a, b, flag):
    return pl.pallas_call(
        sum_prompt_kernel,
        out_shape=(
            jax.ShapeDtypeStruct(a.shape, BF),
            jax.ShapeDtypeStruct((8, 128), F32),
        ),
        in_specs=[vmem()] * 3,
        out_specs=[vmem(), vmem()],
        compiler_params=params(),
        cost_estimate=cost(4 * a.size, 6 * a.size),
        name="sum_prompt",
    )(a, b, flag)


def optimizer_kernel(
    meta,
    biases,
    mine,
    theirs,
    squares,
    prompts,
    one_in,
    two_in,
    clip_out,
    one_out,
    two_out,
    new_out,
    norm_ref,
    held,
    sem,
):
    even = meta[2] == 0
    block = prompts.shape[0]
    tiles = sem.shape[1]
    tile = block // tiles
    norm_ref[...] = jnp.sqrt(squares[...])
    norm = norm_ref[0:1, :]
    factor = jnp.minimum(1.0, CLIP_NORM / (norm + 1e-06))
    copies = []
    for index in range(tiles):
        rows = pl.ds(index * tile, tile)
        a, b = mine[rows, :].astype(F32), theirs[rows, :].astype(F32)
        grads = jnp.concatenate([jnp.where(even, a, b), jnp.where(even, b, a)], axis=1)
        clipped = grads * wide(factor, grads.shape[1] // 128)
        new_one = BETA_ONE * one_in[rows, :] + (1.0 - BETA_ONE) * clipped
        new_two = BETA_TWO * two_in[rows, :] + (1.0 - BETA_TWO) * clipped * clipped
        first_hat = new_one / biases[0]
        second_hat = new_two / biases[1]
        held[0, rows, :] = clipped
        held[1, rows, :] = new_one
        held[2, rows, :] = new_two
        held[3, rows, :] = prompts[rows, :] * (
            1.0 - LEARNING_RATE * DECAY_RATE
        ) - LEARNING_RATE * first_hat / (jnp.sqrt(second_hat) + EPSILON)
        for place, out in enumerate((clip_out, one_out, two_out, new_out)):
            copies.append(
                pltpu.make_async_copy(held.at[place, rows], out.at[rows], sem.at[place, index])
            )
            copies[-1].start()
    for copy in copies:
        copy.wait()


def optimizer(meta, biases, mine, theirs, squares, prompts, moment_one, moment_two):
    block, width = prompts.shape
    tiles = 5 if block % 40 == 0 else 1
    shape = jax.ShapeDtypeStruct((block, width), F32)
    return pl.pallas_call(
        optimizer_kernel,
        out_shape=(shape,) * 4 + (jax.ShapeDtypeStruct(squares.shape, F32),),
        in_specs=[smem(), smem()] + [vmem()] * 6,
        out_specs=[hbm()] * 4 + [vmem()],
        scratch_shapes=[
            pltpu.VMEM((4, block, width), F32),
            pltpu.SemaphoreType.DMA((4, tiles)),
        ],
        compiler_params=params(prompts, prompts),
        cost_estimate=cost(20 * block * width, 32 * block * width),
        name="optimizer",
    )(meta, biases, mine, theirs, squares, prompts, moment_one, moment_two)


def per_device(
    tokens,
    cotangent,
    dataset_ids,
    prompt_map,
    attn_in,
    attn_out,
    up_weight,
    up_bias,
    down_weight,
    down_bias,
    norm_gains,
    norm_shifts,
    prompts,
    moment_one,
    moment_two,
    step_count,
):
    size, width = tokens.shape[1:]
    dim = attn_in.shape[2]
    hid = up_weight.shape[1]
    data_count = prompt_map.shape[1]
    row_count = lax.axis_size("rows")
    head_count = lax.axis_size("head")
    factor = dim ** (-0.5) * LOG2E
    row = lax.axis_index("rows")
    head = lax.axis_index("head")
    batch, parity = head // 2, head % 2
    half = size // 2
    meta = jnp.stack([row, batch, parity]).astype(jnp.int32)

    block = prompts.shape[0]

    part = half_rows(block)
    prompt_own = lax.dynamic_slice(
        prompts, (batch * (block - part), parity * (width // 2)), (part, width // 2)
    ).astype(BF)
    in_other = swap_head(attn_in, 2, head_count)
    ids = jnp.where(batch == 0, dataset_ids[0], dataset_ids[1])
    tok_half = lax.dynamic_slice(tokens, (batch, parity * half, 0), (1, half, width))[0]
    id_rows = jnp.broadcast_to(ids.astype(BF)[None, :], (PACK, size))
    shard = jnp.concatenate([tok_half, id_rows], axis=0)

    bias_high = lax.reduce_precision(up_bias, 8, 7)
    bias_rest = up_bias - bias_high
    bias_mid = lax.reduce_precision(bias_rest, 8, 7)
    bias_low = bias_rest - bias_mid
    bias_rows = jnp.concatenate([bias_high, bias_mid, bias_low, bias_low]).astype(BF)
    bias_rows = jnp.pad(bias_rows.reshape(-1, width), ((0, PACK - 4 * hid // width), (0, 0)))
    w_own = jnp.concatenate([down_weight, attn_out, up_weight.T, bias_rows], axis=0)
    in_other, w_own = lax.optimization_barrier((in_other, w_own))
    w_along = swap_head(w_own, 2, head_count)
    step_value = step_count.astype(F32)
    biases = jnp.stack(
        [1.0 - jnp.power(BETA_ONE, step_value), 1.0 - jnp.power(BETA_TWO, step_value)]
    )
    numbers = jnp.arange(data_count + 1, dtype=jnp.int32)
    local = jnp.sum((dataset_ids[:, None, :] < numbers[None, :, None]).astype(jnp.int32), axis=2)
    ids_rows = dataset_ids.astype(F32).reshape(2, 1, size)
    tied = {}

    orders, later = bit_orders(row_count), prompt_orders(row_count)
    stages = len(orders[0])
    held, prompt_held = shard[None], prompt_own[None]
    tok = lax.dynamic_index_in_dim(tokens, batch, 0, keepdims=False)
    cot = lax.dynamic_index_in_dim(cotangent, batch, 0, keepdims=False)

    def prompt_stage(place):
        other = gather_stage(prompt_held, place, later, row_count, head_count)
        return jnp.concatenate([prompt_held, other], axis=0)

    for place in range(stages):
        if place == stages - 1:
            held, in_other, meta, (biases, local, ids_rows, tok, cot) = lax.optimization_barrier(
                (held, in_other, meta, (biases, local, ids_rows, tok, cot))
            )
        if place != 1:
            held, prompt_held = lax.optimization_barrier((held, prompt_held))
        other = gather_stage(held, place, orders, row_count, head_count)
        if place != 1:
            prompt_held = prompt_stage(max(place - 1, 0))
        if place < stages - 1:
            held = jnp.concatenate([held, other], axis=0)
        if place == 0:
            held, prompt_held = lax.optimization_barrier((held, prompt_held))
    theirs_low = swap_head(held, 1, head_count)
    other, prompt_held, w_along = lax.optimization_barrier((other, prompt_held, w_along))
    mine = (held, other)
    prompt_high = gather_stage(prompt_held, stages - 1, later, row_count, head_count)
    theirs = (theirs_low, swap_head(other, 1, head_count))
    w_core = swap_head(w_own, 1, head_count)
    w_far = swap_head(w_along, 1, head_count)

    ids_all = jnp.concatenate([bank[:, half, :size] for bank in mine], axis=0).astype(F32)
    starts = jnp.sum(
        (ids_all.reshape(1, -1) < numbers.astype(F32)[:, None]).astype(jnp.int32), axis=1
    )
    ids_all = ids_all.reshape(row_count, 1, size)
    q_own, kv_own, w_q, w_kv, *state, flag = token_forward(
        meta, starts, tokens, ids_rows, mine, theirs, attn_in, in_other, factor, data_count
    )
    prompt_theirs_low = swap_head(prompt_held, 1, head_count)
    prompt_high, flag, prompt_theirs_low, w_core, w_far = lax.optimization_barrier(
        (prompt_high, flag, prompt_theirs_low, w_core, w_far)
    )
    prompt_mine = (prompt_held, prompt_high)
    prompt_theirs = (prompt_theirs_low, swap_head(prompt_high, 1, head_count))
    wide_half, lse_half, send_half = prompt_forward(
        meta,
        local,
        prompt_map,
        q_own,
        ids_rows,
        state,
        flag,
        prompt_mine,
        prompt_theirs,
        w_kv,
        factor,
        block,
    )
    prompt_low, send_half = lax.optimization_barrier((prompts.astype(BF), send_half))
    prompt_kv = jnp.dot(prompt_low, w_kv, preferred_element_type=F32).astype(BF)
    o_mine, wide_out, lse = join_halves(wide_half, lse_half, swap_head(send_half, 2, head_count))
    o_mine, prompt_kv = lax.optimization_barrier((o_mine, prompt_kv))
    o_theirs = swap_head(o_mine, 1, head_count)
    out, grad_sum, pack, delta = feed(
        meta,
        o_mine,
        o_theirs,
        wide_out,
        lse,
        tok,
        cot,
        (w_own, w_along, w_core, w_far),
        down_bias.reshape(1, width),
        norm_gains,
        norm_shifts,
    )
    pack_other = swap_head(pack, 2, head_count)

    def tie_query_grads(stages_left, held):
        if stages_left == 3:
            held, here = lax.optimization_barrier((held, w_q))
            tied["q"], tied["flag"] = project_query(mine, theirs, here)
        if stages_left == 2:
            held, other, flag = lax.optimization_barrier((held, pack_other, tied["flag"]))
            tied["dq"] = prompt_query_grad(
                meta,
                local,
                prompt_map,
                q_own,
                ids_rows,
                lse,
                delta,
                pack,
                other,
                flag,
                prompt_mine,
                prompt_theirs,
                w_kv,
                factor,
                block,
            )
        if stages_left == 1:
            acc, dq_send = tied["dq"]
            held, dq_send, ids_here = lax.optimization_barrier((held, dq_send, ids_rows))
            tied["dq_other"] = swap_head(dq_send, 2, head_count)
            tied["dq"], tied["flag"] = token_query_grad(
                meta,
                starts,
                q_own,
                ids_here,
                lse,
                delta,
                pack,
                acc,
                mine,
                theirs,
                w_kv,
                factor,
                data_count,
            )
            *tied["terms"], tied["flag"] = prompt_grad_first(
                meta,
                starts,
                prompt_map,
                tied["q"],
                ids_all,
                held,
                prompt_kv,
                tied["flag"],
                factor,
                data_count,
            )
        return held

    out_half = lax.dynamic_slice_in_dim(out, parity * half, half, 0)
    out_half = swap_head(out_half, 2, head_count)
    packs = gather_rows(pack, row_count, head_count, tie_query_grads)
    q_all = tied["q"]
    dq = tied["dq"]
    packs, dq_other, out_half = lax.optimization_barrier((packs, tied["dq_other"], out_half))
    keep, send = prompt_grad_last(
        meta,
        starts,
        prompt_map,
        q_all,
        ids_all,
        packs[1],
        prompt_kv,
        tied["terms"],
        w_kv,
        factor,
        data_count,
    )

    pair = keep + swap_head(send, 1, head_count).astype(F32)
    pair_low = lax.reduce_precision(pair, 8, 7).astype(BF)
    pair_low, ids_here = lax.optimization_barrier((pair_low, ids_rows))
    pair_other = swap_head(pair_low, 2, head_count)
    out_rest = swap_head(out_half, 1, head_count)
    token_part, flag = token_grad(
        meta,
        starts,
        q_all,
        ids_all,
        packs,
        kv_own,
        ids_here,
        (dq, dq_other),
        (w_q, w_kv),
        factor,
        data_count,
    )
    pair_other, flag = lax.optimization_barrier((pair_other, flag))
    full_low, squares = sum_prompt(pair_low, pair_other, flag)
    full_other = swap_head(full_low, 1, head_count)

    def both_batches(own, here, rest):
        other = jnp.concatenate(
            [jnp.where(parity == 0, here, rest), jnp.where(parity == 0, rest, here)], axis=0
        )
        first = jnp.where(batch == 0, own, other)
        return jnp.stack([first, jnp.where(batch == 0, other, own)]).astype(F32)

    core_sum = token_part.astype(F32) + swap_head(token_part, 1, head_count).astype(F32)
    total = lax.reduce_precision(grad_sum + core_sum, 8, 7).astype(BF)
    mine_half = lax.dynamic_slice_in_dim(total, parity * half, half, 0)
    other_half = swap_head(mine_half, 2, head_count)
    layer_out = both_batches(out, out_half, out_rest)

    def tie_sum(stages_done, value):
        if stages_done == 1:
            value, _ = lax.optimization_barrier((value, total))
        if stages_done == 2:
            value, tied["out"] = lax.optimization_barrier((value, layer_out))
        return value

    squares = xor_sum(squares, row_count, head_count, tie_sum)
    clipped, new_one, new_two, new_prompts, norm = optimizer(
        meta, biases, full_low, full_other, squares, prompts, moment_one, moment_two
    )
    other_half, norm = lax.optimization_barrier((other_half, norm))
    input_grad = both_batches(total, other_half, swap_head(other_half, 1, head_count))
    return (tied["out"], input_grad, clipped, norm[0, 0], new_one, new_two, new_prompts)


def solution(mesh):
    in_specs = (
        P(None, "rows", None),
        P(None, "rows", None),
        P(None, "rows"),
        P(),
        P(None, None, "head"),
        P("head", None),
        P(None, "head"),
        P("head"),
        P("head", None),
        P(),
        P(),
        P(),
        P("rows", None),
        P("rows", None),
        P("rows", None),
        P(),
    )
    out_specs = (
        P(None, "rows", None),
        P(None, "rows", None),
        P("rows", None),
        P(),
        P("rows", None),
        P("rows", None),
        P("rows", None),
    )
    return jax.shard_map(
        per_device, mesh=mesh, in_specs=in_specs, out_specs=out_specs, check_vma=False
    )
```
